32 devices in a mesh: seq: 8 (over z, y), tp: 4 (over x, core).
Axes of the slice: x: 2, y: 2, z: 4, core: 2. Of those that a mesh axis runs over, the one named last changes fastest.
Arguments:
- tokens: bfloat16 [2, 3072, 2048], P(None, ('seq', 'tp')), may hold values from -6 to 6
- seq_cuts: int32 [2], replicated, may hold values from 1024 to 3072, as said below
- w_query: bfloat16 [2048, 2048], P(('seq', 'tp')), may hold values from -2 to 2
- w_key: bfloat16 [2048, 2048], P(('seq', 'tp')), may hold values from -0.125 to 0.125
- w_value: bfloat16 [2048, 2048], P(('seq', 'tp')), may hold values from -0.125 to 0.125
- w_gate_out: bfloat16 [2048, 2048], P(('seq', 'tp')), may hold values from -0.125 to 0.125
- w_output: bfloat16 [2048, 2048], P(('seq', 'tp')), may hold values from -0.125 to 0.125
- w_low: bfloat16 [2048, 16], P(('seq', 'tp')), may hold values from -0.125 to 0.125
- w_rank: bfloat16 [256, 16], P(('seq', 'tp')), may hold values from -1.5 to 1.5
- gate_bias: bfloat16 [256], P(('seq', 'tp')), may hold values from 1 to 12
- attn_gain: bfloat16 [2048], P(('seq', 'tp')), may hold values from 0.099609375 to 1.8984375
- out_gain: bfloat16 [512], P(('seq', 'tp')), may hold values from 0.099609375 to 1.8984375
- ffn_gain: bfloat16 [2048], P(('seq', 'tp')), may hold values from 0.099609375 to 1.8984375
- w_gate: bfloat16 [2048, 5632], P('seq', 'tp'), may hold values from -0.125 to 0.125
- w_up: bfloat16 [2048, 5632], P('seq', 'tp'), may hold values from -0.125 to 0.125
- w_down: bfloat16 [2048, 5632], P('seq', 'tp'), may hold values from -0.078125 to 0.078125
- cotangent: bfloat16 [2, 3072, 2048], P(None, ('seq', 'tp')), may hold values from -6 to 6
Outputs:
- out: bfloat16 [2, 3072, 2048], P(None, ('seq', 'tp'))
- grad_tokens: float32 [2, 3072, 2048], P(None, ('seq', 'tp'))
- grad_w_query: float32 [2048, 2048], P(('seq', 'tp'))
- grad_w_key: float32 [2048, 2048], P(('seq', 'tp'))
- grad_w_value: float32 [2048, 2048], P(('seq', 'tp'))
- grad_w_gate_out: float32 [2048, 2048], P(('seq', 'tp'))
- grad_w_output: float32 [2048, 2048], P(('seq', 'tp'))
- grad_w_low: float32 [2048, 16], P(('seq', 'tp'))
- grad_w_rank: float32 [256, 16], P(('seq', 'tp'))
- grad_gate_bias: float32 [256], P(('seq', 'tp'))
- grad_attn_gain: float32 [2048], P(('seq', 'tp'))
- grad_out_gain: float32 [512], P(('seq', 'tp'))
- grad_ffn_gain: float32 [2048], P(('seq', 'tp'))
- grad_w_gate: float32 [2048, 5632], P('seq', 'tp')
- grad_w_up: float32 [2048, 5632], P('seq', 'tp')
- grad_w_down: float32 [2048, 5632], P('seq', 'tp')
The draws below stay inside these ranges and needn't reach their ends.
Inputs may be any that keep to these rules, and one draw needn't show every extreme that they name: In stream s the first sequence holds positions 0 to seq_cuts[s] - 1 and the second the rest. One stream, drawn from the seed, is a single sequence (seq_cuts = 3072); in the others seq_cuts lies between 1024 and 2048.
All inputs are finite; a program needn't handle non-finite values.
Results may differ from the reference program's by a relative error of at most 0.03.
Values may be sent and summed in bfloat16 or wider, within the bound.
A program may use at most 448 MiB of HBM per device.

```python
import jax
import jax.numpy as jnp
from jax import lax

D = 2048
H = 4
M = 64
R = 16
FF = 5632
HD = 512
STREAMS = 2
BLOCK = 32
MINLEN = 1024
LENGTH = 3072


def draw_seq_cuts(key, part):
    key = jax.random.fold_in(key, 11)
    pick_key, cut_key = jax.random.split(key)
    chosen = jax.random.randint(pick_key, (), 0, STREAMS)
    inner = jax.random.randint(cut_key, (STREAMS,), MINLEN, LENGTH - MINLEN + 1)
    return jnp.where(jnp.arange(STREAMS) == chosen, LENGTH, inner).astype(jnp.int32)


def level_of(stream_key, shape, cuts, low, largest):
    level = 1.0
    for dim, parts in cuts:
        steps = jax.random.uniform(jax.random.fold_in(jax.random.fold_in(stream_key, 6), dim), (parts,), jnp.float32, low / len(cuts), largest / len(cuts))
        level = level * jnp.repeat(jnp.exp(steps), shape[dim] // parts).reshape((-1,) + (1,) * (len(shape) - 1 - dim))
    return level


def gaussian(rng, dims, spread, most, cuts=(), kind=jnp.bfloat16):
    values = jax.random.normal(rng, dims, jnp.float32) * spread
    if len(cuts) > 0:
        values = level_of(rng, dims, cuts, -0.22, 0.18) * values
    return jnp.clip(values, min=-most, max=most).astype(kind)


def setup_inputs(seed: int = 0) -> dict:
    keys = jax.random.split(jax.random.key(seed), 18)
    tokens = gaussian(keys[0], (STREAMS, LENGTH, D), 1.0, 6.0, ((1, 32),))
    seq_cuts = draw_seq_cuts(jax.random.fold_in(keys[17], 71), 0)
    w_query = gaussian(keys[2], (D, D), (D // 256) ** -0.5, 2.0, ((0, 32),))
    w_key = gaussian(keys[3], (D, D), D ** -0.5, 0.125, ((0, 32),))
    w_value = gaussian(keys[4], (D, D), D ** -0.5, 0.125, ((0, 32),))
    w_gate_out = gaussian(keys[5], (D, D), D ** -0.5, 0.125, ((0, 32),))
    w_output = gaussian(keys[6], (D, D), D ** -0.5, 0.125, ((0, 32),))
    w_low = gaussian(keys[7], (D, R), D ** -0.5, 0.125, ((0, 32),))
    w_rank = gaussian(keys[8], (H * M, R), R ** -0.5, 1.5, ((0, 32),))
    gate_bias = jnp.clip(1.0 + 11.0 * jax.random.uniform(keys[9], (H * M,), jnp.float32) ** level_of(keys[9], (H * M,), ((0, 32),), -0.2, 0.2), 1.0, 12.0).astype(jnp.bfloat16)
    attn_gain = jnp.clip(1.0 + 0.18 * jax.random.normal(keys[10], (D,), jnp.float32), 0.099609375, 1.8984375).astype(jnp.bfloat16)
    out_gain = jnp.clip(1.0 + 0.18 * jax.random.normal(keys[11], (HD,), jnp.float32), 0.099609375, 1.8984375).astype(jnp.bfloat16)
    ffn_gain = jnp.clip(1.0 + 0.18 * jax.random.normal(keys[12], (D,), jnp.float32), 0.099609375, 1.8984375).astype(jnp.bfloat16)
    w_gate = gaussian(keys[13], (D, FF), D ** -0.5, 0.125, ((0, 8), (1, 4)))
    w_up = gaussian(keys[14], (D, FF), D ** -0.5, 0.125, ((0, 8), (1, 4)))
    w_down = gaussian(keys[15], (D, FF), FF ** -0.5, 0.078125, ((0, 8), (1, 4)))
    cotangent = gaussian(keys[16], (STREAMS, LENGTH, D), 1.0, 6.0, ((1, 32),))
    return {"tokens": tokens, "seq_cuts": seq_cuts, "w_query": w_query, "w_key": w_key, "w_value": w_value, "w_gate_out": w_gate_out, "w_output": w_output, "w_low": w_low, "w_rank": w_rank, "gate_bias": gate_bias, "attn_gain": attn_gain, "out_gain": out_gain, "ffn_gain": ffn_gain, "w_gate": w_gate, "w_up": w_up, "w_down": w_down, "cotangent": cotangent}


GATE_SCALE = 8.0
EPSILON = 1e-05
HIGHEST = lax.Precision.HIGHEST

@jax.custom_vjp
def low(v):
    return lax.optimization_barrier(v.astype(jnp.bfloat16)).astype(jnp.float32)

@jax.custom_vjp
def low_back(v):
    return v

def low_keep(v):
    return (low(v), None)

def low_pass(kept, grad):
    return (grad,)

def back_keep(v):
    return (v, None)

def back_low(kept, grad):
    return (low(grad),)
low.defvjp(low_keep, low_pass)
low_back.defvjp(back_keep, back_low)

def high_dot(left, right):
    return jnp.dot(left, right, precision=HIGHEST)

def root_norm(values, gain_vec):
    return values * lax.rsqrt(lax.optimization_barrier(jnp.mean(values * values, axis=-1, keepdims=True)) + EPSILON) * gain_vec

def to_heads(flat, head_count):
    streams, positions, columns = flat.shape
    return flat.reshape(streams, positions, head_count, columns // head_count).transpose(0, 2, 1, 3)

def from_heads(grouped):
    streams, head_count, positions, piece_len = grouped.shape
    return grouped.transpose(0, 2, 1, 3).reshape(streams, positions, head_count * piece_len)

def to_blocks(values, dim_at, block_len):
    shaped = values.reshape(values.shape[:dim_at] + (values.shape[dim_at] // block_len, block_len) + values.shape[dim_at + 1:])
    return jnp.moveaxis(shaped, dim_at, 0)

def from_blocks(values, dim_at):
    moved = jnp.moveaxis(values, 0, dim_at)
    return moved.reshape(moved.shape[:dim_at] + (moved.shape[dim_at] * moved.shape[dim_at + 1],) + moved.shape[dim_at + 2:])

def block_terms(log_keep, starts):
    history = jnp.cumsum(log_keep, axis=2)
    started = jnp.cumsum(starts, axis=1)
    offsets = jnp.arange(log_keep.shape[2])
    causal = offsets[:, None] >= offsets[None, :]
    same_doc = ((started[:, :, None] == started[:, None, :]) & causal[None])[:, None, :, :, None]
    spans = history[:, :, :, None, :] - history[:, :, None, :, :]
    decay = jnp.where(same_doc, jnp.exp(jnp.where(same_doc, spans, 0.0)), 0.0)
    coefficient = decay * (-jnp.expm1(log_keep))[:, :, None, :, :]
    initial = jnp.where((started == 0)[:, None, :, None], jnp.exp(history), 0.0)
    return (coefficient, initial)

def carried(slots_in, coefficient, initial, key_rows, value_rows):
    paired = jnp.concatenate([key_rows, value_rows], axis=-1)
    return jnp.einsum('shjm,shjd->shmd', coefficient[:, :, -1], paired, precision=HIGHEST) + initial[:, :, -1, :, None] * slots_in

def read_step(slots_in, pieces):
    query, key_rows, value_rows, log_keep, starts = pieces
    coefficient, initial = block_terms(log_keep, starts)
    head_dim = key_rows.shape[-1]
    affinity = jnp.einsum('shtd,shjd->shtj', query, key_rows, precision=HIGHEST)
    scores = jnp.einsum('shtjm,shtj->shtm', coefficient, affinity, precision=HIGHEST)
    scores = scores + initial * jnp.einsum('shtd,shmd->shtm', query, slots_in[..., :head_dim], precision=HIGHEST)
    weights_read = jax.nn.softmax(scores, axis=-1)
    mixing = jnp.einsum('shtm,shtjm->shtj', weights_read, coefficient, precision=HIGHEST)
    reading = jnp.einsum('shtj,shjd->shtd', mixing, value_rows, precision=HIGHEST)
    reading = reading + jnp.einsum('shtm,shmd->shtd', weights_read * initial, slots_in[..., head_dim:], precision=HIGHEST)
    return (carried(slots_in, coefficient, initial, key_rows, value_rows), reading)

def readout(query, key_rows, value_rows, log_keep, slots_in, starts):
    head_dim = query.shape[-1] // H
    pieces = (to_blocks(to_heads(query, H) * head_dim ** (-0.5), 2, BLOCK), to_blocks(to_heads(key_rows, H), 2, BLOCK), to_blocks(to_heads(value_rows, H), 2, BLOCK), to_blocks(to_heads(log_keep, H), 2, BLOCK), to_blocks(starts, 1, BLOCK))
    last_state, readings = lax.scan(jax.checkpoint(read_step), slots_in, pieces)
    return from_heads(from_blocks(readings, 2))

def gated_read(reading, gate_out, out_gain):
    streams, positions, columns = reading.shape
    grouped = reading.reshape(streams, positions, H, columns // H)
    normed = root_norm(grouped, out_gain)
    return normed.reshape(streams, positions, columns) * jax.nn.silu(gate_out)

def forget_logs(low_rank, w_rank, gate_bias):
    logits = jnp.dot(low_rank, w_rank.T, precision=HIGHEST) + gate_bias
    return jax.nn.log_sigmoid(logits) / GATE_SCALE

def reference(tokens, seq_cuts, w_query, w_key, w_value, w_gate_out, w_output, w_low, w_rank, gate_bias, attn_gain, out_gain, ffn_gain, w_gate, w_up, w_down, cotangent):
    offsets = jnp.arange(LENGTH)
    starts = ((offsets[None, :] == 0) | (offsets[None, :] == seq_cuts[:, None])).astype(jnp.float32)

    def forward(tokens_f, query_w, key_w, value_w, gate_out_w, output_w, low_w, rank_w, bias_vec, attn_vec, out_vec, ffn_vec, gate_w, up_w, down_w):
        normed = low(root_norm(tokens_f, attn_vec))
        query = low_back(high_dot(normed, query_w))
        key_rows = low_back(high_dot(normed, key_w))
        value_rows = low_back(high_dot(normed, value_w))
        gate_out = low_back(high_dot(normed, gate_out_w))
        query_feat = jax.nn.silu(query)
        key_feat = jax.nn.silu(key_rows)
        value_feat = jax.nn.silu(value_rows)
        log_keep = forget_logs(high_dot(normed, low_w), rank_w, bias_vec)
        slots_zero = jnp.zeros((tokens_f.shape[0], H, log_keep.shape[-1] // H, 2 * (query.shape[-1] // H)), jnp.float32)
        reading = readout(query_feat, key_feat, value_feat, log_keep, slots_zero, starts)
        branch = low(gated_read(reading, gate_out, out_vec))
        mixed_out = low_back(high_dot(branch, output_w))
        hidden = tokens_f + mixed_out
        ffn_in = low(root_norm(hidden, ffn_vec))
        gate_pre = low_back(high_dot(ffn_in, gate_w))
        up_pre = low_back(high_dot(ffn_in, up_w))
        product_in = low(jax.nn.silu(gate_pre) * up_pre)
        return hidden + high_dot(product_in, down_w.T)
    floats = tuple((param.astype(jnp.float32) for param in (tokens, w_query, w_key, w_value, w_gate_out, w_output, w_low, w_rank, gate_bias, attn_gain, out_gain, ffn_gain, w_gate, w_up, w_down)))
    result, pullback = jax.vjp(forward, *floats)
    grads = pullback(cotangent.astype(jnp.float32))
    return (result.astype(jnp.bfloat16), grads[0], grads[1], grads[2], grads[3], grads[4], grads[5], grads[6], grads[7], grads[8], grads[9], grads[10], grads[11], grads[12], grads[13], grads[14])
```

```python
import functools

import jax
import jax.numpy as jnp
from jax import lax
from jax.experimental import pallas as pl
from jax.experimental.pallas import tpu as pltpu
from jax.sharding import PartitionSpec as P

H = 4
GATE_SCALE = 8.0
EPSILON = 1e-05
BF = jnp.bfloat16
F32 = jnp.float32
CHUNK = 128
SUB = 16
HALVES = (16, 32, 64)


def mm(left, right, dims):
    return lax.dot_general(
        left.astype(BF), right.astype(BF), (dims, ((), ())), preferred_element_type=F32
    )


def mm_fine(left, right, dims):
    left_hi, right_hi = left.astype(BF), right.astype(BF)
    left_lo = (left - left_hi.astype(F32)).astype(BF)
    right_lo = (right - right_hi.astype(F32)).astype(BF)

    def part(a, b):
        return lax.dot_general(a, b, (dims, ((), ())), preferred_element_type=F32)

    return part(left_hi, right_hi) + (part(left_hi, right_lo) + part(left_lo, right_hi))


NN = ((1,), (0,))
NT = ((1,), (1,))
TN = ((0,), (0,))


def turn(values, amount):
    return pltpu.roll(values, amount % values.shape[1], 1)


def column(shape):
    return lax.broadcasted_iota(jnp.int32, shape, 1)


def row(shape):
    return lax.broadcasted_iota(jnp.int32, shape, 0)


def ahead_product(keep, size):
    place = column(keep.shape) & (size - 1)
    total, step = keep, 1
    while step < size:
        total = total * jnp.where(place >= step, turn(total, step), 1.0)
        step *= 2
    return total


def behind_product(keep, size):
    place = column(keep.shape) & (size - 1)
    total = jnp.where(place == size - 1, 1.0, turn(keep, -1))
    step = 1
    while step < size:
        total = total * jnp.where(place < size - step, turn(total, -step), 1.0)
        step *= 2
    return total


def chunks_of(values):
    return [values[:, at : at + CHUNK] for at in range(0, values.shape[1], CHUNK)]


def rows_of(values):
    return [values[at : at + CHUNK] for at in range(0, values.shape[0], CHUNK)]


class Decays:
    def __init__(self, keep):
        self.keep = chunks_of(keep)
        self.count = len(self.keep)
        self.ahead = [ahead_product(k, CHUNK) for k in self.keep]
        self.behind = [behind_product(k, CHUNK) for k in self.keep]
        self.total = [a[:, CHUNK - 1 :] for a in self.ahead]

    def levels(self):
        self.ahead_in = [{h: ahead_product(k, h) for h in HALVES} for k in self.keep]
        self.behind_in = [{h: behind_product(k, h) for h in HALVES} for k in self.keep]
        inside = (column(self.keep[0].shape) & (SUB - 1)) != 0
        self.short = [jnp.where(inside, k, 0.0) for k in self.keep]

    def from_start(self, c):
        out = self.ahead[c]
        for earlier in range(c):
            out = out * self.total[earlier]
        return out

    def to_end(self, c):
        out = self.behind[c]
        for later in range(c + 1, self.count):
            out = out * self.total[later]
        return out

    def to_chunk(self, c):
        parts = []
        for earlier in range(c):
            out = self.behind[earlier]
            for between in range(earlier + 1, c):
                out = out * self.total[between]
            parts.append(out)
        return parts

    def survive(self):
        out = self.total[0]
        for t in self.total[1:]:
            out = out * t
        return out


def level_mask(half):
    shape = (CHUNK, CHUNK)
    source, target = row(shape) // half, column(shape) // half
    return ((source & 1) == 0) & (target == source + 1)


def diagonals(square):
    shape = (SUB, CHUNK)
    group = column(shape) // SUB
    out = jnp.zeros(shape, F32)
    for b in range(CHUNK // SUB):
        out = out + jnp.where(group == b, square[b * SUB : (b + 1) * SUB], 0.0)
    return out


def at_lag(compact, lag):
    shape = (SUB, CHUNK)
    hit = row(shape) == (column(shape) & (SUB - 1)) - lag
    return jnp.sum(jnp.where(hit, compact, 0.0), axis=0, keepdims=True)


def undiagonal(lagged):
    shape = (SUB, CHUNK)
    place = (column(shape) & (SUB - 1)) - row(shape)
    compact = jnp.zeros(shape, F32)
    for lag, values in enumerate(lagged):
        compact = jnp.where(place == lag, values, compact)
    group = column(shape) // SUB
    return jnp.concatenate(
        [jnp.where(group == b, compact, 0.0) for b in range(CHUNK // SUB)], axis=0
    )


def read_slots(decays, written, c, affinity, entering, dot):
    near = affinity[c * CHUNK :]
    out = decays.from_start(c) * entering
    if c > 0:
        far = jnp.concatenate(
            [b * w for b, w in zip(decays.to_chunk(c), written[:c])], axis=1
        )
        out = out + decays.ahead[c] * dot(far, affinity[: c * CHUNK], NN)
    for h in HALVES:
        part = dot(decays.behind_in[c][h] * written[c], jnp.where(level_mask(h), near, 0.0), NN)
        out = out + decays.ahead_in[c][h] * part
    compact = diagonals(near)
    weight = written[c]
    for lag in range(SUB):
        out = out + weight * at_lag(compact, lag)
        if lag + 1 < SUB:
            weight = decays.short[c] * turn(weight, 1)
    return out


def mix_sources(decays, written, c, shares):
    lagged = [[] for _ in shares]
    weight = written[c]
    for lag in range(SUB):
        for place, share in enumerate(shares):
            lagged[place].append(jnp.sum(weight * share, axis=0, keepdims=True))
        if lag + 1 < SUB:
            weight = decays.short[c] * turn(weight, 1)
    outs = []
    for place, share in enumerate(shares):
        near = undiagonal(lagged[place])
        for h in HALVES:
            part = mm(decays.behind_in[c][h] * written[c], decays.ahead_in[c][h] * share, TN)
            near = near + jnp.where(level_mask(h), part, 0.0)
        if c > 0:
            far = jnp.concatenate(
                [b * w for b, w in zip(decays.to_chunk(c), written[:c])], axis=1
            )
            near = jnp.concatenate([mm(far, decays.ahead[c] * share, TN), near], axis=0)
        outs.append(near)
    return outs


def gather_back(decays, c, shares, affinities):
    outs = []
    if c > 0:
        pulled = sum(
            mm_fine(decays.ahead[c] * s, a[: c * CHUNK], NT) for s, a in zip(shares, affinities)
        )
        outs = [b * p for b, p in zip(decays.to_chunk(c), chunks_of(pulled))]
    nears = [a[c * CHUNK :] for a in affinities]
    own = 0.0
    for h in HALVES:
        mask = level_mask(h)
        pulled = sum(
            mm_fine(decays.ahead_in[c][h] * s, jnp.where(mask, a, 0.0), NT)
            for s, a in zip(shares, nears)
        )
        own = own + decays.behind_in[c][h] * pulled
    compacts = [diagonals(a) for a in nears]
    held = 0.0
    for lag in range(SUB - 1, -1, -1):
        if lag < SUB - 1:
            held = turn(decays.short[c] * held, -1)
        for s, a in zip(shares, compacts):
            held = held + s * at_lag(a, lag)
    outs.append(own + held)
    return outs


def silu(x):
    return x * jax.nn.sigmoid(x)


def silu_slope(x):
    sig = jax.nn.sigmoid(x)
    return sig * (1.0 + x * (1.0 - sig))


def piece_state(key_raw, value_raw, keep, written):
    decays = Decays(keep)
    left = jnp.concatenate(
        [decays.to_end(c) * w for c, w in enumerate(chunks_of(written))], axis=1
    )
    state = jnp.concatenate([mm(left, silu(key_raw), NN), mm(left, silu(value_raw), NN)], axis=1)
    return state, decays.survive()


def piece_read(query_raw, key_raw, value_raw, keep, written, slots_in):
    width = query_raw.shape[1]
    query, keys, values = silu(query_raw) * width**-0.5, silu(key_raw), silu(value_raw)
    slot_keys, slot_values = slots_in[:, :width], slots_in[:, width:]
    decays = Decays(keep)
    decays.levels()
    writes = chunks_of(written)
    entering = mm_fine(slot_keys, query, NT)
    readings, scores_all, shares = [], [], []
    for c in range(decays.count):
        last = (c + 1) * CHUNK
        affinity = mm_fine(keys[:last], query[c * CHUNK : last], NT)
        scores = read_slots(
            decays, writes, c, affinity, chunks_of(entering)[c], mm_fine
        )
        spread = jnp.exp(scores - jnp.max(scores, axis=0, keepdims=True))
        share = spread / jnp.sum(spread, axis=0, keepdims=True)
        (mixing,) = mix_sources(decays, writes, c, [share])
        reading = mm(mixing, values[:last], TN)
        reading = reading + mm(decays.from_start(c) * share, slot_values, TN)
        readings.append(reading)
        scores_all.append(scores)
        shares.append(share)
    return (
        jnp.concatenate(readings, axis=0),
        jnp.concatenate(scores_all, axis=1),
        jnp.concatenate(shares, axis=1),
    )


def add_chunks(total, extra):
    return [t + e for t, e in zip(total, extra)] + total[len(extra) :]


def piece_back(query_raw, key_raw, value_raw, keep, written, slots_in, scores, share, grad_read):
    width = query_raw.shape[1]
    query, keys, values = silu(query_raw) * width**-0.5, silu(key_raw), silu(value_raw)
    slot_keys, slot_values = slots_in[:, :width], slots_in[:, width:]
    decays = Decays(keep)
    decays.levels()
    writes = chunks_of(written)
    count = decays.count
    entering = chunks_of(mm_fine(slot_values, grad_read, NT))
    grad_q = []
    grad_k = [jnp.zeros((CHUNK, width), F32)] * count
    grad_v = [jnp.zeros((CHUNK, width), F32)] * count
    back = [jnp.zeros(writes[0].shape, F32)] * count
    direct_k, direct_v, own = 0.0, 0.0, []
    for c in range(count):
        last = (c + 1) * CHUNK
        here = slice(c * CHUNK, last)
        p = chunks_of(share)[c]
        affinity = mm_fine(keys[:last], query[here], NT)
        pull = mm_fine(values[:last], grad_read[here], NT)
        grad_p = read_slots(decays, writes, c, pull, entering[c], mm_fine)
        weighed = p * grad_p
        grad_s = weighed - p * jnp.sum(weighed, axis=0, keepdims=True)
        own.append(weighed + grad_s * chunks_of(scores)[c])
        mix_k, mix_v = mix_sources(decays, writes, c, [grad_s, p])
        from_start = decays.from_start(c)
        far_s, far_p = from_start * grad_s, from_start * p
        grad_q.append(mm(mix_k, keys[:last], TN) + mm(far_s, slot_keys, TN))
        grad_k = add_chunks(grad_k, rows_of(mm(mix_k, query[here], NN)))
        grad_v = add_chunks(grad_v, rows_of(mm(mix_v, grad_read[here], NN)))
        direct_k = direct_k + mm(far_s, query[here], NN)
        direct_v = direct_v + mm(far_p, grad_read[here], NN)
        back = add_chunks(back, gather_back(decays, c, [grad_s, p], [affinity, pull]))
    grad_query = jnp.concatenate(grad_q, axis=0) * width**-0.5 * silu_slope(query_raw)
    return (
        grad_query,
        jnp.concatenate(grad_k, axis=0),
        jnp.concatenate(grad_v, axis=0),
        jnp.concatenate([direct_k, direct_v], axis=1),
        jnp.concatenate(back, axis=1),
        jnp.concatenate(own, axis=1),
    )


def piece_after(
    key_raw, value_raw, keep, true_keep, written, grad_k, grad_v, back, own, after, slots_end
):
    width = key_raw.shape[1]
    keys, values = silu(key_raw), silu(value_raw)
    decays = Decays(keep)
    writes = chunks_of(written)
    to_end = jnp.concatenate([decays.to_end(c) for c in range(decays.count)], axis=1)
    left = to_end * written
    grad_k = grad_k + mm(left, after[:, :width], TN)
    grad_v = grad_v + mm(left, after[:, width:], TN)
    pulled = mm_fine(after[:, :width], keys, NT)
    pulled = pulled + mm_fine(after[:, width:], values, NT)
    back = back + to_end * pulled
    flow = own - written * back
    held = jnp.sum(after * slots_end, axis=1, keepdims=True)
    parts = chunks_of(flow)
    outs = []
    for part in reversed(parts):
        place, total, step = column(part.shape), part, 1
        while step < CHUNK:
            total = total + jnp.where(place < CHUNK - step, turn(total, -step), 0.0)
            step *= 2
        outs.append(total + held)
        held = held + total[:, :1]
    grad_log = jnp.concatenate(outs[::-1], axis=1) - true_keep * back
    return grad_k * silu_slope(key_raw), grad_v * silu_slope(value_raw), grad_log


def tie(value, *after):
    if not after:
        return value

    def body(*refs):
        pass

    anywhere = pl.BlockSpec(memory_space=pl.ANY)
    return pl.pallas_call(
        body,
        in_specs=[anywhere] * (1 + len(after)),
        out_specs=anywhere,
        out_shape=jax.ShapeDtypeStruct(value.shape, value.dtype),
        input_output_aliases={0: 0},
        cost_estimate=pl.CostEstimate(flops=0, bytes_accessed=0, transcendentals=0),
    )(value, *after)


def per_stream(work, arrays, outs, flops):
    def body(*refs):
        results = work(*[ref[...] for ref in refs[: len(arrays)]])
        for ref, result in zip(refs[len(arrays) :], results):
            ref[...] = result.astype(ref.dtype)

    def whole(shape):
        return pl.BlockSpec((None,) + tuple(shape[1:]), lambda s: (s, 0, 0))

    streams = arrays[0].shape[0]
    outs = [jax.ShapeDtypeStruct((streams,) + shape, kind) for shape, kind in outs]
    return pl.pallas_call(
        body,
        grid=(streams,),
        in_specs=[whole(a.shape) for a in arrays],
        out_specs=[whole(o.shape) for o in outs],
        out_shape=outs,
        compiler_params=pltpu.CompilerParams(vmem_limit_bytes=40 * 1024 * 1024),
        cost_estimate=pl.CostEstimate(flops=flops, bytes_accessed=1 << 16, transcendentals=0),
    )(*arrays)


def inverse_rms(values):
    return lax.rsqrt(jnp.mean(values * values, axis=-1, keepdims=True) + EPSILON)


def norm_back(values, scale, gain, grad):
    pulled = gain * grad
    along = jnp.mean(values * pulled, axis=-1, keepdims=True)
    return scale * pulled - values * (scale * scale * scale) * along


def product(left, right, dims):
    return lax.dot_general(left, right, (dims, ((), ())), preferred_element_type=F32)


def chain(earlier, later):
    return (earlier[0] * later[0], later[0][..., None] * earlier[1] + later[1])


CORE, X, Y, NEAR, FAR = 1, 2, 4, 8, 16


class Place:
    def __init__(self):
        self.seq, self.tp = lax.axis_index("seq"), lax.axis_index("tp")
        self.core, self.x = self.tp % 2, self.tp // 2
        self.y, self.z = self.seq % 2, self.seq // 2
        self.near, self.far = self.z % 2, self.z // 2
        self.flat = self.seq * 4 + self.tp

    def partner(self, mask):
        seq, tp = self.seq, self.tp
        if mask & CORE:
            tp = tp + 1 - 2 * self.core
        if mask & X:
            tp = tp + 2 - 4 * self.x
        if mask & Y:
            seq = seq + 1 - 2 * self.y
        if mask & NEAR:
            seq = seq + 2 - 4 * self.near
        if mask & FAR:
            seq = seq + 4 - 8 * self.far
        return seq, tp

    def z_turn(self, index):
        low, high = index % 2, index // 2
        low = low + self.near - 2 * low * self.near
        high = high + self.far - 2 * high * self.far
        return 2 * high + low


class Wire:
    def __init__(self, place, sends, receives, locals_):
        self.place, self.sends, self.receives, self.locals = place, sends, receives, locals_
        self.remote, self.near_by, self.seen = [], [], set()

    def greet(self, masks):
        barrier = pltpu.get_barrier_semaphore()
        for mask in masks:
            pl.semaphore_signal(
                barrier,
                inc=1,
                device_id=self.place.partner(mask),
                device_id_type=pl.DeviceIdType.MESH,
            )
        pl.semaphore_wait(barrier, len(masks))

    def send(self, source, target, mask):
        at = len(self.remote)
        copy = pltpu.make_async_remote_copy(
            src_ref=source,
            dst_ref=target,
            send_sem=self.sends.at[at],
            recv_sem=self.receives.at[at],
            device_id=self.place.partner(mask),
            device_id_type=pl.DeviceIdType.MESH,
        )
        copy.start()
        self.remote.append(copy)
        return ("remote", at)

    def keep(self, source, target):
        at = len(self.near_by)
        copy = pltpu.make_async_copy(source, target, self.locals.at[at])
        copy.start()
        self.near_by.append(copy)
        return ("local", at)

    def arrived(self, *handles):
        for handle in handles:
            if handle in self.seen:
                continue
            self.seen.add(handle)
            if handle[0] == "remote":
                self.remote[handle[1]].wait_recv()
            else:
                self.near_by[handle[1]].wait()

    def run(self, *tasks):
        live = [(task, next(task)) for task in tasks]
        while live:
            later = []
            for task, handles in live:
                self.arrived(*handles)
                try:
                    later.append((task, next(task)))
                except StopIteration:
                    pass
            live = later

    def finish(self):
        for at, copy in enumerate(self.remote):
            self.arrived(("remote", at))
            copy.wait_send()
        for at in range(len(self.near_by)):
            self.arrived(("local", at))


def comm_call(work, number, masks, arrays, in_vmem, outs, out_vmem, scratch, copies, stay, mb=48):
    def space(fast):
        return pl.BlockSpec(memory_space=pltpu.VMEM if fast else pl.ANY)

    def body(*refs):
        n, m = len(arrays), len(outs)
        place = Place()
        wire = Wire(place, *refs[-3:])
        wire.greet(masks)
        work(place, wire, refs[:n], refs[n : n + m], refs[n + m : -3])
        wire.finish()

    return pl.pallas_call(
        body,
        in_specs=[space(v) for v in in_vmem],
        out_specs=[space(v) for v in out_vmem],
        out_shape=[jax.ShapeDtypeStruct(shape, kind) for shape, kind in outs],
        scratch_shapes=list(scratch)
        + [
            pltpu.SemaphoreType.DMA((copies,)),
            pltpu.SemaphoreType.DMA((copies,)),
            pltpu.SemaphoreType.DMA((max(stay, 1),)),
        ],
        compiler_params=pltpu.CompilerParams(
            collective_id=number, has_side_effects=True, vmem_limit_bytes=mb * 1024 * 1024
        ),
        cost_estimate=pl.CostEstimate(flops=0, bytes_accessed=1 << 16, transcendentals=0),
    )(*arrays)


def head_gather(place, wire, weight, out):
    rows, width = weight.shape[0], out.shape[1]
    block = 4 * rows
    base = place.y * 4 * block

    def columns(tp):
        return weight.at[:, pl.ds(pl.multiple_of(tp * width, 128), width)]

    def part(m):
        return out.at[pl.ds(pl.multiple_of(base + m * block, 16), block)]

    own = out.at[pl.ds(pl.multiple_of(base + place.tp * rows, 16), rows)]
    handles = [wire.keep(columns(place.tp), own)]
    for mask in (X, X | CORE, CORE):
        handles.append(wire.send(columns(place.partner(mask)[1]), own, mask))
    yield handles
    far = wire.send(part(0), part(2), FAR)
    near = wire.send(part(0), part(1), NEAR)
    over = [wire.send(part(0), part(0), Y)]
    yield [far]
    last = wire.send(part(2), part(3), NEAR)
    over.append(wire.send(part(2), part(2), Y))
    yield [near]
    over.append(wire.send(part(1), part(1), Y))
    yield [last]
    over.append(wire.send(part(3), part(3), Y))
    yield over


def output_gather(place, wire, block, out):
    def part(m):
        return out.at[m, place.y]

    yield [wire.keep(block, part(0))]
    far = wire.send(part(0), part(2), FAR)
    near = wire.send(part(0), part(1), NEAR)
    over = [wire.send(part(0), part(0), Y)]
    yield [far]
    last = wire.send(part(2), part(3), NEAR)
    over.append(wire.send(part(2), part(2), Y))
    yield [near]
    over.append(wire.send(part(1), part(1), Y))
    yield [last]
    over.append(wire.send(part(3), part(3), Y))
    yield over


def ffn_trade(place, wire, halves, out):
    own = out.at[0, place.y]
    yield [
        wire.send(halves.at[1 - place.y], own, Y),
        wire.keep(halves.at[place.y], own),
    ]


def later(task, rounds):
    for unused in range(rounds):
        yield []
    yield from task


def ffn_gather(place, wire, halves, out, rounds):
    yield from ffn_trade(place, wire, halves, out)
    yield from later(ffn_spread(place, wire, None, out), rounds)


def ffn_spread(place, wire, block, out):
    start = out.at[0] if block is None else block
    stay = [] if block is None else [wire.keep(block, out.at[0])]
    far = wire.send(start, out.at[2], FAR)
    near = wire.send(start, out.at[1], NEAR)
    yield [far]
    last = wire.send(out.at[2], out.at[3], NEAR)
    yield [near, last] + stay


def rows_gather(place, wire, own, out):
    mine = out.at[:, place.tp]
    stay = wire.keep(own, mine)
    across = wire.send(own, mine, X)
    beside = wire.send(own, mine, CORE)
    yield [across]
    theirs = out.at[:, place.partner(X)[1]]
    yield [stay, beside, wire.send(theirs, theirs, CORE)]


def small_gather(place, wire, own, out):
    handles = [
        wire.keep(own, out.at[pl.ds(place.flat, 1)]),
        wire.send(own, out.at[pl.ds(place.flat, 1)], CORE),
    ]
    size = 2
    for mask in (X, Y, NEAR, FAR):
        yield handles
        part = out.at[pl.ds(place.flat // size * size, size)]
        handles = [wire.send(part, part, mask)]
        size *= 2
    yield handles


def plane_gather(place, wire, first, second, out):
    line_a = [out.at[0, 0, m] for m in range(4)]
    line_b = [out.at[0, 1, m] for m in range(4)]
    beside = []

    def pass_on(half, m):
        beside.append(wire.send(out.at[0, half, m], out.at[1, half, m], CORE))

    stay = [wire.keep(first, line_a[0]), wire.keep(second, line_b[0])]
    a_x = wire.send(first, line_a[1], X)
    b_y = wire.send(second, line_b[1], Y)
    a_y = wire.send(first, line_a[2], Y)
    b_x = wire.send(second, line_b[2], X)
    beside.append(wire.send(first, out.at[1, 0, 0], CORE))
    beside.append(wire.send(second, out.at[1, 1, 0], CORE))
    yield [a_x]
    a_xy = wire.send(line_a[1], line_a[3], Y)
    pass_on(0, 1)
    yield [b_y]
    b_xy = wire.send(line_b[1], line_b[3], X)
    pass_on(1, 1)
    yield [a_y, b_x]
    pass_on(0, 2)
    pass_on(1, 2)
    yield [a_xy, b_xy]
    pass_on(0, 3)
    pass_on(1, 3)
    yield stay + beside


def heads_trade(place, wire, branch, out):
    width = out.shape[1] // 4

    def columns(ref, index):
        return ref.at[:, pl.ds(pl.multiple_of(index * width, 128), width)]

    mine = columns(out, place.z_turn(place.tp))
    handles = [wire.keep(columns(branch, place.tp), mine)]
    for mask in (X, X | CORE, CORE):
        handles.append(wire.send(columns(branch, place.partner(mask)[1]), mine, mask))
    yield handles


def heads_return(place, wire, grads, out):
    width = out.shape[1] // 4

    def columns(ref, index):
        return ref.at[:, pl.ds(pl.multiple_of(index * width, 128), width)]

    mine = columns(out, place.tp)
    handles = [wire.keep(columns(grads, place.z_turn(place.tp)), mine)]
    for mask in (X, X | CORE, CORE):
        there = place.z_turn(place.partner(mask)[1])
        handles.append(wire.send(columns(grads, there), mine, mask))
    yield handles


def pieces_scan(place, wire, reverse, survive, state, out, bufs):
    send_s, send_b, got_s, got_b = bufs
    wide = state.shape[-1] // survive.shape[-1]
    total_s, total_b = survive[...], state[...]
    before_s = before_b = None

    def join(first_s, first_b, second_s, second_b):
        spread = jnp.concatenate([second_s] * wide, axis=-1)
        return first_s * second_s, spread * first_b + second_b

    for step, (mask, bit) in enumerate(((Y, place.y), (NEAR, place.near), (FAR, place.far))):
        send_s[step] = total_s
        send_b[step] = total_b.astype(BF)
        yield [
            wire.send(send_b.at[step], got_b.at[step], mask),
            wire.send(send_s.at[step], got_s.at[step], mask),
        ]
        other_s, other_b = got_s[step], got_b[step].astype(F32)
        later = bit == (0 if reverse else 1)
        if before_s is None:
            before_s = jnp.where(later, other_s, 1.0)
            before_b = jnp.where(later, other_b, 0.0)
        else:
            joined_s, joined_b = join(other_s, other_b, before_s, before_b)
            before_s = jnp.where(later, joined_s, before_s)
            before_b = jnp.where(later, joined_b, before_b)
        if mask != FAR:
            first_s, first_b = jnp.where(later, other_s, total_s), jnp.where(later, other_b, total_b)
            second_s = jnp.where(later, total_s, other_s)
            second_b = jnp.where(later, total_b, other_b)
            total_s, total_b = join(first_s, first_b, second_s, second_b)
    out[...] = before_b


def scan_buffers(state_shape, survive_shape):
    return [
        pltpu.VMEM((3,) + survive_shape, F32),
        pltpu.VMEM((3,) + state_shape, BF),
        pltpu.VMEM((3,) + survive_shape, F32),
        pltpu.VMEM((3,) + state_shape, BF),
    ]


def row_loop(count, step, work):
    def body(i, carry):
        work(pl.ds(pl.multiple_of(i * step, step), step))
        return carry

    lax.fori_loop(0, count // step, body, 0)


def hidden_rows(place, wire, mixed, tokens, gain, hidden, ready, sums, got_core, got_x):
    streams, count, width = tokens.shape
    other_x = 1 - place.x
    beside = [wire.send(mixed.at[s, :, 1 - place.core], got_core.at[s], CORE) for s in range(streams)]
    across = []
    for s in range(streams):
        yield [beside[s]]

        def to_send(rows, s=s):
            part = mixed[s, other_x, place.core, rows].astype(F32)
            sums[s, rows] = (part + got_core[s, other_x, rows].astype(F32)).astype(BF)

        row_loop(count, 16, to_send)
        across.append(wire.send(sums.at[s], got_x.at[s], X))
    for s in range(streams):
        yield [across[s]]

        def to_norm(rows, s=s):
            part = mixed[s, place.x, place.core, rows].astype(F32)
            part = part + got_core[s, place.x, rows].astype(F32) + got_x[s, rows].astype(F32)
            values = tokens[s, rows].astype(F32) + part
            hidden[s, rows] = values
            normed = (values * inverse_rms(values) * gain[...]).astype(BF)
            size = width // 4
            for m in range(4):
                there = pl.ds(pl.multiple_of(place.z_turn(m) * size, 128), size)
                ready[s, rows, there] = normed[:, m * size : (m + 1) * size]

        row_loop(count, 16, to_norm)


class Bits:
    CORE, X, Y, NEAR, FAR = 1, 2, 4, 8, 16

    def __init__(self):
        seq, tp = lax.axis_index("seq"), lax.axis_index("tp")
        self.core, self.x = tp & 1, tp >> 1
        self.y, self.z = seq & 1, seq >> 1

    def steps(self):
        return (
            (self.CORE, self.core),
            (self.X, self.x),
            (self.Y, self.y),
            (self.NEAR, self.z & 1),
            (self.FAR, self.z >> 1),
        )


def swap(values, mask):
    pairs = [(i, i ^ mask) for i in range(32)]
    return lax.ppermute(values, ("seq", "tp"), pairs)


def half(values, axis, which):
    size = values.shape[axis] // 2
    return lax.dynamic_slice_in_dim(values, which * size, size, axis)


def trade(values, mask, bit, axis, kind=None):
    other = half(values, axis, 1 - bit)
    if kind is not None:
        other = other.astype(kind)
    return half(values, axis, bit), swap(other, mask)


def in_order(mine, theirs, bit):
    first = bit == 0
    return jnp.where(first, mine, theirs), jnp.where(first, theirs, mine)


def z_blocks(block):
    far = swap(block, Bits.FAR)
    return [block, swap(block, Bits.NEAR), far, swap(far, Bits.NEAR)]


def z_fold(blocks, kind=BF):
    first = blocks[0] + swap(blocks[1].astype(kind), Bits.NEAR).astype(F32)
    second = blocks[2] + swap(blocks[3].astype(kind), Bits.NEAR).astype(F32)
    return first + swap(second.astype(kind), Bits.FAR).astype(F32)


def z_relative(values, z, axis):
    size = values.shape[axis] // 4
    return jnp.concatenate(
        [lax.dynamic_slice_in_dim(values, (m ^ z) * size, size, axis) for m in range(4)], axis
    )


def spread_tp(values, at):
    streams, count, width = values.shape
    pair = jnp.stack(in_order(values, swap(values, Bits.X), at.x), axis=1)
    both = jnp.stack(in_order(pair, swap(pair, Bits.CORE), at.core), axis=2)
    return both.reshape(streams, 4 * count, width)


def fold_tp(part, at):
    streams, count, width = part.shape
    parts = part.reshape(streams, 2, 2, count // 4, width)
    mine, got = trade(parts, Bits.CORE, at.core, 2, BF)
    mine, got = trade(mine + got.astype(F32), Bits.X, at.x, 1, BF)
    return (mine + got.astype(F32)).reshape(streams, count // 4, width)


def spread_plane(rows):
    count = rows.shape[0] // 2
    first, second = rows[:count], rows[count:]
    first = jnp.concatenate([first, swap(first, Bits.X)], axis=0)
    second = jnp.concatenate([second, swap(second, Bits.Y)], axis=0)
    four = [first, swap(first, Bits.Y), second, swap(second, Bits.X)]
    four = jnp.concatenate(four, axis=0)
    return jnp.concatenate([four, swap(four, Bits.CORE)], axis=0)


def fold_half(part, mask):
    size = part.shape[0] // 2
    return part[:size] + swap(part[size:].astype(BF), mask).astype(F32)


def fold_plane(work):
    sent = swap(work(1).astype(BF), Bits.CORE)
    part = work(0) + sent.astype(F32)
    size = part.shape[0] // 2
    first = fold_half(fold_half(part[:size], Bits.Y), Bits.X)
    second = fold_half(fold_half(part[size:], Bits.X), Bits.Y)
    return jnp.concatenate([first, second], axis=0)


def gather_head(weight, at):
    rows, width = weight.shape
    mine, got = trade(weight, Bits.X, at.x, 1)
    both = jnp.stack(in_order(mine, got, at.x), axis=0)
    mine, got = trade(both, Bits.CORE, at.core, 2)
    both = jnp.stack(in_order(mine, got, at.core), axis=1).reshape(4 * rows, width // 4)
    line = jnp.concatenate(z_blocks(both), axis=0)
    return jnp.concatenate(in_order(line, swap(line, Bits.Y), at.y), axis=0)


def fold_head(grad, at):
    mine, got = trade(grad, Bits.Y, at.y, 0, BF)
    line = mine + got.astype(F32)
    rows = line.shape[0] // 4
    own = z_fold([line[m * rows : (m + 1) * rows] for m in range(4)])
    width = own.shape[1]
    own = own.reshape(2, 2, rows // 4, width)
    mine, got = trade(own, Bits.CORE, at.core, 1, BF)
    own = jnp.concatenate(in_order(mine, got.astype(F32), at.core), axis=-1)
    mine, got = trade(own, Bits.X, at.x, 0, BF)
    own = jnp.concatenate(in_order(mine, got.astype(F32), at.x), axis=-1)
    return own.reshape(rows // 4, 4 * width)


def turn_bits(values, back):
    pairs = []
    for i in range(32):
        z, y, x, core = i >> 3, (i >> 2) & 1, (i >> 1) & 1, i & 1
        there = z * 8 + core * 4 + y * 2 + x
        pairs.append((there, i) if back else (i, there))
    return lax.ppermute(values, ("seq", "tp"), pairs)


def gather_output(weight, at):
    block = turn_bits(weight, False)
    line = jnp.stack(z_blocks(block), axis=0)
    both = jnp.stack(in_order(line, swap(line, Bits.Y), at.y), axis=1)
    return both.reshape(8 * weight.shape[0], weight.shape[1])


def fold_output(grad, at):
    rows, width = grad.shape
    parts = grad.reshape(4, 2, rows // 8, width)
    mine, got = trade(parts, Bits.Y, at.y, 1, BF)
    line = (mine + got.astype(F32)).reshape(4, rows // 8, width)
    own = z_fold([line[m] for m in range(4)])
    return turn_bits(own.astype(BF), True).astype(F32)


def heads_to_rows(values, at):
    mine, got = trade(values, Bits.X, at.x, 1)
    both = jnp.stack(in_order(mine, got, at.x), axis=0)
    mine, got = trade(both, Bits.CORE, at.core, 2)
    both = jnp.stack(in_order(mine, got, at.core), axis=1)
    parts = both.reshape((4,) + both.shape[2:])
    return jnp.concatenate(
        [lax.dynamic_index_in_dim(parts, m ^ at.z, 0, False) for m in range(4)], axis=1
    )


def rows_to_heads(values, at):
    width = values.shape[1] // 4
    parts = jnp.stack(
        [
            lax.dynamic_slice_in_dim(values, (m ^ at.z) * width, width, 1)
            for m in range(4)
        ],
        axis=0,
    ).reshape(2, 2, values.shape[0], width)
    mine, got = trade(parts, Bits.X, at.x, 0)
    first, second = in_order(mine[0], got[0], at.x)
    both = jnp.stack([first, second], axis=0)
    mine, got = trade(both, Bits.CORE, at.core, 1)
    first, second = in_order(mine[:, 0], got[:, 0], at.core)
    both = jnp.stack([first, second], axis=1)
    return jnp.concatenate([both[0, 0], both[0, 1], both[1, 0], both[1, 1]], axis=1)


class FfnGather:
    def __init__(self, weight, at):
        mine, got = trade(weight, Bits.Y, at.y, 1)
        self.block = jnp.concatenate(in_order(mine, got, at.y), axis=0)

    def far(self, *after):
        self.block = tie(self.block, *after)
        self.far_block = swap(self.block, Bits.FAR)
        return (self.far_block,)

    def near(self, *after):
        self.block = tie(self.block, *after)
        self.near_block = swap(self.block, Bits.NEAR)
        self.last_block = swap(self.far_block, Bits.NEAR)
        return (self.near_block, self.last_block)

    def whole(self):
        parts = [self.block, self.near_block, self.far_block, self.last_block]
        return jnp.concatenate(parts, axis=0)


class FfnFold:
    def __init__(self, grad, at):
        self.at = at
        rows = grad.shape[0] // 4
        self.parts = [grad[m * rows : (m + 1) * rows] for m in range(4)]

    def near(self, *after):
        sent = [tie(self.parts[1].astype(BF), *after), self.parts[3].astype(BF)]
        self.got = [swap(s, Bits.NEAR) for s in sent]
        return tuple(self.got)

    def far(self, *after):
        second = self.parts[2] + self.got[1].astype(F32)
        self.last = swap(tie(second.astype(BF), *after), Bits.FAR)
        return (self.last,)

    def whole(self):
        own = self.parts[0] + self.got[0].astype(F32) + self.last.astype(F32)
        mine, got = trade(own, Bits.Y, self.at.y, 0, BF)
        return jnp.concatenate(in_order(mine, got.astype(F32), self.at.y), axis=1)


class PlainWhole:
    def __init__(self, value):
        self.value = value

    def far(self, *after):
        return ()

    near = far

    def whole(self):
        return self.value


def spread_all(values, at):
    for mask, bit in at.steps():
        values = jnp.concatenate(in_order(values, swap(values, mask), bit), axis=0)
    return values


def fold_all(values, at):
    for mask, bit in reversed(at.steps()):
        mine, got = trade(values, mask, bit, 0)
        values = mine + got
    return values


def scan_pieces(part, at, reverse):
    total, before = part, None
    steps = ((Bits.Y, at.y), (Bits.NEAR, at.z & 1), (Bits.FAR, at.z >> 1))
    for mask, bit in steps:
        other = (swap(total[0], mask), swap(total[1].astype(BF), mask).astype(F32))
        later = bit == (0 if reverse else 1)
        if before is None:
            before = (
                jnp.where(later, other[0], 1.0),
                jnp.where(later, other[1], 0.0),
            )
        else:
            joined = chain(other, before)
            before = tuple(jnp.where(later, a, b) for a, b in zip(joined, before))
        if mask != Bits.FAR:
            first = tuple(jnp.where(later, o, t) for o, t in zip(other, total))
            second = tuple(jnp.where(later, t, o) for o, t in zip(other, total))
            total = chain(first, second)
    return before


class Plain:
    def __init__(self):
        self.seq, self.tp = lax.axis_index("seq"), lax.axis_index("tp")
        self.seq_count, self.tp_count = lax.axis_size("seq"), lax.axis_size("tp")
        self.sharing = self.tp_count // H
        self.head, self.member = self.tp // self.sharing, self.tp % self.sharing


def plain_scan(part, at, reverse):
    gathered = (
        lax.all_gather(part[0], "seq"),
        lax.all_gather(part[1].astype(BF), "seq"),
    )
    state = (jnp.ones_like(part[0]), jnp.zeros_like(part[1]))

    def step(count, state):
        source = at.seq_count - 1 - count if reverse else count
        piece = tuple(lax.dynamic_index_in_dim(a, source, 0, False) for a in gathered)
        return chain(state, (piece[0], piece[1].astype(F32)))

    steps = at.seq_count - 1 - at.seq if reverse else at.seq
    return lax.fori_loop(0, steps, step, state)


class PlainMoves:
    def small(self, packed):
        return lax.all_gather(packed, ("seq", "tp"))

    def small_sum(self, packed):
        return lax.psum_scatter(packed, ("seq", "tp"), scatter_dimension=0, tiled=True)[0]

    def begin(self, packed, tokens, weights, w_output, ffn):
        self.weights, self.w_output, self.ffn = weights, w_output, ffn
        return self.small(packed), self.piece(tokens), [self.head_weight(w) for w in weights[:2]]

    def scan_in(self, survive, state):
        weights = [self.head_weight(w) for w in self.weights[2:]]
        return self.scan((survive, state), False)[1], weights, self.output_weight(self.w_output)

    def hidden(self, mixed, tokens, gain, cotangent):
        streams, count, width = tokens.shape
        hidden = tokens.astype(F32) + self.sum_piece(mixed)
        hidden = hidden.reshape(streams * count, width)
        ready = (hidden * inverse_rms(hidden) * gain).astype(BF)
        cot = self.ffn_rows(cotangent.reshape(streams * count, width))
        return hidden, self.ffn_rows(ready), cot

    def ffn_weights(self):
        return [lax.all_gather(w, "seq", axis=0, tiled=True) for w in self.ffn]

    def __init__(self):
        self.at = Plain()
        self.head, self.member = self.at.head, self.at.member

    def own_streams(self, values):
        count = values.shape[0] // self.at.sharing
        return lax.dynamic_slice_in_dim(values, self.member * count, count, 0)

    def piece(self, own):
        return self.own_streams(lax.all_gather(own, "tp", axis=1, tiled=True))

    def sum_piece(self, part):
        streams = part.shape[0] * self.at.sharing
        entire = jnp.zeros((streams,) + part.shape[1:], BF)
        entire = lax.dynamic_update_slice_in_dim(
            entire, part.astype(BF), self.member * part.shape[0], 0
        )
        own = lax.psum_scatter(entire, "tp", scatter_dimension=1, tiled=True)
        return own.astype(F32)

    def mixer_order(self, values):
        return values

    mixer_unorder = ffn_order = ffn_unorder = mixer_order

    def head_weight(self, weight):
        entire = lax.all_gather(weight, ("seq", "tp"), axis=0, tiled=True)
        width = entire.shape[1] // H
        return lax.dynamic_slice_in_dim(entire, self.head * width, width, 1)

    def head_grad(self, grad):
        entire = jnp.zeros((grad.shape[0], grad.shape[1] * H), BF)
        entire = lax.dynamic_update_slice_in_dim(
            entire, grad.astype(BF), self.head * grad.shape[1], 1
        )
        own = lax.psum_scatter(entire, ("seq", "tp"), scatter_dimension=0, tiled=True)
        return own.astype(F32)

    def output_weight(self, weight):
        entire = lax.all_gather(weight, ("seq", "tp"), axis=0, tiled=True)
        rows = entire.shape[0] // H
        return lax.dynamic_slice_in_dim(entire, self.head * rows, rows, 0)

    def output_grad(self, grad):
        entire = jnp.zeros((grad.shape[0] * H, grad.shape[1]), BF)
        entire = lax.dynamic_update_slice_in_dim(
            entire, grad.astype(BF), self.head * grad.shape[0], 0
        )
        own = lax.psum_scatter(entire, ("seq", "tp"), scatter_dimension=0, tiled=True)
        return own.astype(F32)

    def to_output(self, branch):
        return branch

    def from_output(self, grad):
        return grad

    def scan(self, part, reverse):
        return plain_scan(part, self.at, reverse)

    def ffn_rows(self, own):
        entire = lax.all_gather(own, "tp", axis=0)
        return entire.reshape((-1,) + own.shape[1:])

    def ffn_sum(self, work):
        part = jnp.concatenate([work(0), work(1)], axis=0)
        parts = part.reshape((self.at.tp_count, -1) + part.shape[1:])
        own = lax.psum_scatter(parts.astype(BF), "tp", scatter_dimension=0, tiled=True)
        return own.reshape((-1,) + part.shape[1:]).astype(F32)

    def ffn_weight(self, weight):
        return PlainWhole(lax.all_gather(weight, "seq", axis=0, tiled=True))

    def ffn_grad(self, grad):
        own = lax.psum_scatter(grad.astype(BF), "seq", scatter_dimension=0, tiled=True)
        return PlainWhole(own.astype(F32))

    def tie(self, value, *after):
        return value


class BitMoves:
    def __init__(self):
        self.at = Bits()
        self.head, self.member = lax.axis_index("tp"), 0

    def begin(self, packed, tokens, weights, w_output, ffn):
        block = turn_bits(w_output, False)
        streams, count, width = tokens.shape
        length = -(-packed.size // 2048) * 16
        own = jnp.pad(packed, (0, length * 128 - packed.size)).reshape(1, length, 128)
        self.rest, self.block = weights[2:], block
        self.halves = [jnp.swapaxes(w.reshape(w.shape[0], 2, -1), 0, 1) for w in ffn]
        ffn_shape = (4,) + self.halves[0].shape
        head = (weights[0].shape[0] * 32, width // 4)

        def work(place, wire, given, outs, scratch):
            wire.run(
                small_gather(place, wire, given[0], outs[0]),
                head_gather(place, wire, given[2], outs[2]),
                head_gather(place, wire, given[3], outs[3]),
                rows_gather(place, wire, given[1], outs[1]),
                ffn_gather(place, wire, given[4], outs[4], 2),
            )

        small, rows, key_w, value_w, self.down = comm_call(
            work,
            1,
            (CORE, X, X | CORE, Y, NEAR, FAR),
            [own, self.mixer_order(tokens), weights[0], weights[1], self.halves[0]],
            [False] * 5,
            [
                ((32, length, 128), BF),
                ((streams, 4, count, width), BF),
                (head, BF),
                (head, BF),
                (ffn_shape, BF),
            ],
            [False] * 5,
            [],
            40,
            8,
        )
        small = small.reshape(32, length * 128)[:, : packed.size]
        return small, rows.reshape(streams, 4 * count, width), [key_w, value_w]

    def scan_in(self, survive, state):
        streams, slots, width = state.shape
        head = (self.rest[0].shape[0] * 32, self.rest[0].shape[1] // 4)
        rows = self.block.shape
        spread = jnp.broadcast_to(survive[..., None], (streams, slots, 128))

        def work(place, wire, given, outs, scratch):
            wire.run(
                pieces_scan(place, wire, False, given[0], given[1], outs[0], scratch),
                head_gather(place, wire, given[2], outs[1]),
                head_gather(place, wire, given[3], outs[2]),
                output_gather(place, wire, given[4], outs[3]),
                ffn_gather(place, wire, given[5], outs[4], 2),
                ffn_trade(place, wire, given[6], outs[5]),
            )

        ffn_shape = (4,) + self.halves[0].shape
        slots_in, query_w, gate_w, output_w, self.gate, self.up = comm_call(
            work,
            2,
            (CORE, X, X | CORE, Y, NEAR, FAR),
            [spread, state] + list(self.rest) + [self.block] + self.halves[1:],
            [True, True] + [False] * 5,
            [
                (state.shape, F32),
                (head, BF),
                (head, BF),
                ((4, 2) + rows, BF),
                (ffn_shape, BF),
                (ffn_shape, BF),
            ],
            [True] + [False] * 5,
            scan_buffers(state.shape, spread.shape),
            60,
            8,
        )
        return slots_in, [query_w, gate_w], output_w.reshape(8 * rows[0], rows[1])

    def hidden(self, mixed, tokens, gain, cotangent):
        streams, count, width = tokens.shape
        cot = self.ffn_order(cotangent)
        plane = (2, 2, 4, count, width)

        def work(place, wire, given, outs, scratch):
            ready, sums, got_core, got_x = scratch
            rows = hidden_rows(
                place, wire, given[0], given[1], given[2], outs[0], ready, sums, got_core, got_x
            )

            def then():
                yield from rows
                yield from plane_gather(place, wire, ready.at[0], ready.at[1], outs[1])

            wire.run(
                then(),
                ffn_spread(place, wire, given[4].at[0], outs[3]),
                plane_gather(place, wire, given[3].at[0], given[3].at[1], outs[2]),
            )

        hidden, ready, cot, self.up = comm_call(
            work,
            3,
            (CORE, X, Y, NEAR, FAR),
            [mixed.reshape(streams, 2, 2, count, width), tokens, gain[None], cot, self.up],
            [True, True, True, False, False],
            [
                ((streams, count, width), F32),
                (plane, BF),
                (plane, BF),
                (self.up.shape, BF),
            ],
            [True, False, False, False],
            [
                pltpu.VMEM((streams, count, width), BF),
                pltpu.VMEM((streams, count, width), BF),
                pltpu.VMEM((streams, 2, count, width), BF),
                pltpu.VMEM((streams, count, width), BF),
            ],
            60,
            8,
        )
        flat = 16 * count
        return (
            hidden.reshape(streams * count, width),
            ready.reshape(flat, width),
            cot.reshape(flat, width),
        )

    def ffn_weights(self):
        return [w.reshape(-1, w.shape[-1]) for w in (self.down, self.gate, self.up)]

    def small_sum(self, packed):
        return fold_all(packed, self.at)[0]

    def own_streams(self, values):
        return values

    def piece(self, own):
        return spread_tp(own, self.at)

    def sum_piece(self, part):
        return fold_tp(part, self.at)

    def mixer_order(self, values):
        lead, width = values.shape[:-1], values.shape[-1]
        parts = jnp.swapaxes(values.reshape(lead + (4, 2, width // 8)), -3, -2)
        return z_relative(parts, self.at.z, len(lead) + 1).reshape(lead + (width,))

    def mixer_unorder(self, values):
        lead, width = values.shape[:-1], values.shape[-1]
        parts = z_relative(values.reshape(lead + (2, 4, width // 8)), self.at.z, len(lead) + 1)
        return jnp.swapaxes(parts, -3, -2).reshape(lead + (width,))

    def ffn_order(self, values):
        return z_relative(values, self.at.z, values.ndim - 1)

    ffn_unorder = ffn_order

    def head_weight(self, weight):
        return gather_head(weight, self.at)

    def head_grad(self, grad):
        return fold_head(grad, self.at)

    def output_weight(self, weight):
        return gather_output(weight, self.at)

    def output_grad(self, grad):
        return fold_output(grad, self.at)

    def to_output(self, branch):
        def work(place, wire, given, outs, scratch):
            wire.run(heads_trade(place, wire, given[0], outs[0]))

        (out,) = comm_call(
            work,
            4,
            (CORE, X, X | CORE),
            [branch],
            [False],
            [(branch.shape, BF)],
            [False],
            [],
            4,
            1,
        )
        return out

    def from_output(self, grad):
        return rows_to_heads(grad, self.at)

    def scan(self, part, reverse):
        return scan_pieces(part, self.at, reverse)

    def ffn_rows(self, own):
        return spread_plane(own)

    def ffn_sum(self, work):
        return fold_plane(work)

    def ffn_weight(self, weight):
        return FfnGather(weight, self.at)

    def ffn_grad(self, grad):
        return FfnFold(grad, self.at)

    def tie(self, value, *after):
        return tie(value, *after)


def on_device(
    tokens,
    seq_cuts,
    w_query,
    w_key,
    w_value,
    w_gate_out,
    w_output,
    w_low,
    w_rank,
    gate_bias,
    attn_gain,
    out_gain,
    ffn_gain,
    w_gate,
    w_up,
    w_down,
    cotangent,
):
    seq_count, tp_count = lax.axis_size("seq"), lax.axis_size("tp")
    devices = seq_count * tp_count
    seq_rank = lax.axis_index("seq")
    move = BitMoves() if (seq_count, tp_count) == (8, 4) else PlainMoves()
    streams, local_len, width = tokens.shape
    rank = w_low.shape[1]

    small = (w_low, w_rank, gate_bias, attn_gain, out_gain, ffn_gain)
    packed = jnp.concatenate([a.reshape(-1) for a in small])
    gathered, rows_in, (key_w, value_w) = move.begin(
        packed, tokens, (w_key, w_value, w_query, w_gate_out), w_output, (w_down, w_gate, w_up)
    )
    unpacked, taken = [], 0
    for a in small:
        part = gathered[:, taken : taken + a.size]
        unpacked.append(part.reshape((devices * a.shape[0],) + a.shape[1:]))
        taken += a.size
    full_low, full_rank, full_bias, full_attn, full_out, full_ffn = unpacked
    slots = full_bias.shape[0] // H
    head_rank = lax.dynamic_slice_in_dim(full_rank, move.head * slots, slots, 0).astype(F32)
    head_bias = lax.dynamic_slice_in_dim(full_bias, move.head * slots, slots, 0).astype(F32)
    attn_vec, ffn_vec = full_attn.astype(F32), full_ffn.astype(F32)
    out_vec = full_out.astype(F32)
    order_low = jnp.swapaxes(move.mixer_order(jnp.swapaxes(full_low, 0, 1)), 0, 1)

    held, piece_len = rows_in.shape[:2]
    flat = held * piece_len
    positions = seq_rank * piece_len + jnp.arange(piece_len)
    cuts = move.own_streams(seq_cuts)
    starts = (positions[None, :] == 0) | (positions[None, :] == cuts[:, None])
    inputs = rows_in.reshape(flat, width).astype(F32)
    attn_scale = inverse_rms(inputs)
    normed = (inputs * attn_scale * move.mixer_order(attn_vec)).astype(BF)
    low_rank = product(normed, order_low, NN)
    logits = lax.dot_general(
        head_rank,
        low_rank.reshape(held, piece_len, rank),
        (((1,), (2,)), ((), ())),
        precision=lax.Precision.HIGHEST,
    )
    logits = jnp.swapaxes(logits, 0, 1) + head_bias[None, :, None]
    log_keep = jax.nn.log_sigmoid(logits) / GATE_SCALE
    true_keep, written = jnp.exp(log_keep), -jnp.expm1(log_keep)
    keep = jnp.where(starts[:, None, :], 0.0, true_keep)

    def project(weight):
        out = product(normed, weight, NN)
        return out.reshape(held, piece_len, weight.shape[1])

    key_rows, value_rows = project(key_w), project(value_w)
    hd = key_rows.shape[-1]
    gflop = 1000 * 1000 * 1000
    state, survive = per_stream(
        piece_state,
        [key_rows, value_rows, keep, written],
        [((slots, 2 * hd), F32), ((slots, 1), F32)],
        gflop,
    )
    survive = survive[..., 0]
    slots_in, (query_w, gate_w), output_w = move.scan_in(survive, state)
    query, gate_out = project(query_w), project(gate_w)
    slots_end = survive[..., None] * slots_in + state
    reading, scores, share = per_stream(
        piece_read,
        [query, key_rows, value_rows, keep, written, slots_in],
        [
            ((piece_len, hd), F32),
            ((slots, piece_len), F32),
            ((slots, piece_len), F32),
        ],
        gflop,
    )
    read_scale = inverse_rms(reading)
    gate_act = silu(gate_out)
    read_normed = reading * read_scale * out_vec
    branch = (read_normed * gate_act).astype(BF).reshape(flat, hd)
    branch_out = move.to_output(branch)
    mixed = product(branch_out, output_w, NN).reshape(held, piece_len, width)
    own_tokens = tokens.astype(F32)
    own_rows = streams * local_len
    hidden, ffn_in, cot_all = move.hidden(mixed.astype(BF), tokens, ffn_vec, cotangent)
    ffn_down, ffn_gate, ffn_up = move.ffn_weights()

    ffn_scale = inverse_rms(hidden)
    grad_product = product(cot_all, ffn_down, NN)
    gate_pre = product(ffn_in, ffn_gate, NN)
    up_pre = product(ffn_in, ffn_up, NN)
    gate_sig = jax.nn.sigmoid(gate_pre)
    product_in = (gate_pre * gate_sig * up_pre).astype(BF)
    slope = gate_sig * (1.0 + gate_pre * (1.0 - gate_sig))
    grad_gate_pre = (grad_product * up_pre * slope).astype(BF)
    grad_up_pre = (grad_product * gate_pre * gate_sig).astype(BF)
    half_rows = grad_gate_pre.shape[0] // 2

    def grad_ffn_half(which):
        here = slice(which * half_rows, (which + 1) * half_rows)
        part = product(grad_gate_pre[here], ffn_gate, NT)
        return part + product(grad_up_pre[here], ffn_up, NT)

    grad_ffn_in = move.ffn_unorder(move.ffn_sum(grad_ffn_half))
    gate_fold = move.ffn_grad(product(ffn_in, grad_gate_pre, TN))
    up_fold = move.ffn_grad(product(ffn_in, grad_up_pre, TN))
    down_fold = move.ffn_grad(product(cot_all, product_in, TN))
    moved = gate_fold.near()
    grad_ffn_in = move.tie(grad_ffn_in, *moved)
    moved = gate_fold.far(grad_ffn_in) + up_fold.near(grad_ffn_in)

    def ffn_out_half(which):
        here = slice(which * half_rows, (which + 1) * half_rows)
        return product(product_late[here], ffn_down, NT)

    product_late = move.tie(product_in, grad_ffn_in)
    ffn_out = move.ffn_unorder(move.ffn_sum(ffn_out_half))
    result = (hidden + ffn_out).astype(BF).reshape(tokens.shape)
    grad_ffn_gain = jnp.sum(grad_ffn_in * hidden * ffn_scale, axis=0)
    grad_hidden = cotangent.reshape(own_rows, width).astype(F32)
    grad_hidden = grad_hidden + norm_back(hidden, ffn_scale, ffn_vec, grad_ffn_in)

    grad_mixed = move.piece(grad_hidden.astype(BF).reshape(tokens.shape)).reshape(flat, width)
    grad_branch_out = product(grad_mixed, output_w, NT).astype(BF)
    grad_branch = move.from_output(grad_branch_out).astype(F32).reshape(held, piece_len, hd)
    grad_w_output = move.output_grad(product(branch_out, grad_mixed, TN))
    grad_gate_rounded = (grad_branch * read_normed * silu_slope(gate_out)).astype(BF)
    grad_read_normed = grad_branch * gate_act
    grad_out_gain = jnp.sum(grad_read_normed * reading * read_scale, axis=(0, 1))
    grad_reading = norm_back(reading, read_scale, out_vec, grad_read_normed)
    grad_reading = move.tie(grad_reading, *moved)
    moved = up_fold.far(grad_reading) + down_fold.near(grad_reading)
    grad_query, grad_k, grad_v, direct, back, own = per_stream(
        piece_back,
        [query, key_rows, value_rows, keep, written, slots_in, scores, share, grad_reading],
        [
            ((piece_len, hd), BF),
            ((piece_len, hd), F32),
            ((piece_len, hd), F32),
            ((slots, 2 * hd), F32),
            ((slots, piece_len), F32),
            ((slots, piece_len), F32),
        ],
        gflop,
    )
    unused, after = move.scan((survive, direct), True)
    after = move.tie(after, *moved)
    down_fold.far(after)
    grad_key, grad_value, grad_log = per_stream(
        piece_after,
        [
            key_rows,
            value_rows,
            keep,
            true_keep,
            written,
            grad_k,
            grad_v,
            back,
            own,
            after,
            slots_end,
        ],
        [((piece_len, hd), BF), ((piece_len, hd), BF), ((slots, piece_len), F32)],
        gflop,
    )
    grad_f = grad_log * jax.nn.sigmoid(-logits) / GATE_SCALE
    grad_bias = jnp.sum(grad_f, axis=(0, 2))
    low_pieces = low_rank.reshape(held, piece_len, rank)
    highest = lax.Precision.HIGHEST
    grad_rank = jnp.einsum("smt,str->mr", grad_f, low_pieces, precision=highest)
    grad_low_rank = jnp.einsum("smt,mr->str", grad_f, head_rank, precision=highest)
    grad_low_rank = grad_low_rank.reshape(flat, rank)
    grads = [g.reshape(flat, hd) for g in (grad_query, grad_key, grad_value, grad_gate_rounded)]
    grad_normed = sum(
        product(g, w, NT) for g, w in zip(grads, (query_w, key_w, value_w, gate_w))
    )
    grad_normed = grad_normed + product(grad_low_rank, order_low.astype(F32), NT)
    grad_normed = move.sum_piece(grad_normed.reshape(held, piece_len, width))
    grad_normed = move.mixer_unorder(grad_normed)
    own_scale = inverse_rms(own_tokens)
    grad_tokens = grad_hidden.reshape(tokens.shape)
    grad_tokens = grad_tokens + norm_back(own_tokens, own_scale, attn_vec, grad_normed)
    grad_attn_gain = jnp.sum(grad_normed * own_tokens * own_scale, axis=(0, 1))
    grad_w_query, grad_w_key, grad_w_value, grad_w_gate_out = (
        move.head_grad(product(normed, g, TN)) for g in grads
    )
    grad_low = product(grad_low_rank, normed.astype(F32), TN)
    grad_low = jnp.swapaxes(move.mixer_unorder(grad_low), 0, 1)

    def placed(part):
        entire = jnp.zeros((part.shape[0] * H,) + part.shape[1:], F32)
        return lax.dynamic_update_slice_in_dim(entire, part, move.head * part.shape[0], 0)

    sums = (
        grad_low,
        placed(grad_rank),
        placed(grad_bias),
        grad_attn_gain,
        grad_out_gain,
        grad_ffn_gain,
    )
    packed = jnp.concatenate([a.reshape(devices, -1) for a in sums], axis=1)
    own_sums = move.small_sum(packed)
    small_grads, taken = [], 0
    for a in small:
        small_grads.append(own_sums[taken : taken + a.size].reshape(a.shape))
        taken += a.size
    return (
        (result, grad_tokens)
        + (grad_w_query, grad_w_key, grad_w_value, grad_w_gate_out, grad_w_output)
        + tuple(small_grads)
        + (gate_fold.whole(), up_fold.whole(), down_fold.whole())
    )


def solution(mesh):
    both, row_split, line = ("seq", "tp"), P(("seq", "tp"), None), P(("seq", "tp"))
    tokens_at, ffn_at = P(None, both, None), P("seq", "tp")
    params = (row_split,) * 7 + (line,) * 4 + (ffn_at,) * 3
    return jax.shard_map(
        on_device,
        mesh=mesh,
        in_specs=(tokens_at, P()) + params + (tokens_at,),
        out_specs=(tokens_at, tokens_at) + params,
        check_vma=False,
    )
```

```python
import dataclasses
import math

import jax
import jax.numpy as jnp
from jax import lax
from jax.experimental import pallas as pl
from jax.experimental.pallas import tpu as pltpu
from jax.sharding import PartitionSpec as P

H = 4
GATE_SCALE = 8.0
EPSILON = 1e-05
BF = jnp.bfloat16
F32 = jnp.float32
CHUNK = 128
SUB = 16
HALVES = (16, 32, 64)


def mm(left, right, dims):
    return lax.dot_general(
        left.astype(BF), right.astype(BF), (dims, ((), ())), preferred_element_type=F32
    )


def mm_fine(left, right, dims):
    left_hi, right_hi = left.astype(BF), right.astype(BF)
    left_lo = (left - left_hi.astype(F32)).astype(BF)
    right_lo = (right - right_hi.astype(F32)).astype(BF)

    def part(a, b):
        return lax.dot_general(a, b, (dims, ((), ())), preferred_element_type=F32)

    return part(left_hi, right_hi) + (part(left_hi, right_lo) + part(left_lo, right_hi))


NN = ((1,), (0,))
NT = ((1,), (1,))
TN = ((0,), (0,))


def turn(values, amount):
    return pltpu.roll(values, amount % values.shape[1], 1)


def column(shape):
    return lax.broadcasted_iota(jnp.int32, shape, 1)


def row(shape):
    return lax.broadcasted_iota(jnp.int32, shape, 0)


def ahead_product(keep, size):
    place = column(keep.shape) & (size - 1)
    total, step = keep, 1
    while step < size:
        total = total * jnp.where(place >= step, turn(total, step), 1.0)
        step *= 2
    return total


def behind_product(keep, size):
    place = column(keep.shape) & (size - 1)
    total = jnp.where(place == size - 1, 1.0, turn(keep, -1))
    step = 1
    while step < size:
        total = total * jnp.where(place < size - step, turn(total, -step), 1.0)
        step *= 2
    return total


def chunks_of(values):
    return [values[:, at : at + CHUNK] for at in range(0, values.shape[1], CHUNK)]


def rows_of(values):
    return [values[at : at + CHUNK] for at in range(0, values.shape[0], CHUNK)]


class Decays:
    def __init__(self, keep):
        self.keep = chunks_of(keep)
        self.count = len(self.keep)
        self.ahead = [ahead_product(k, CHUNK) for k in self.keep]
        self.behind = [behind_product(k, CHUNK) for k in self.keep]
        self.total = [a[:, CHUNK - 1 :] for a in self.ahead]

    def levels(self):
        self.ahead_in = [{h: ahead_product(k, h) for h in HALVES} for k in self.keep]
        self.behind_in = [{h: behind_product(k, h) for h in HALVES} for k in self.keep]
        inside = (column(self.keep[0].shape) & (SUB - 1)) != 0
        self.short = [jnp.where(inside, k, 0.0) for k in self.keep]

    def from_start(self, c):
        out = self.ahead[c]
        for earlier in range(c):
            out = out * self.total[earlier]
        return out

    def to_end(self, c):
        out = self.behind[c]
        for later in range(c + 1, self.count):
            out = out * self.total[later]
        return out

    def to_chunk(self, c):
        parts = []
        for earlier in range(c):
            out = self.behind[earlier]
            for between in range(earlier + 1, c):
                out = out * self.total[between]
            parts.append(out)
        return parts

    def survive(self):
        out = self.total[0]
        for t in self.total[1:]:
            out = out * t
        return out


def level_mask(half):
    shape = (CHUNK, CHUNK)
    source, target = row(shape) // half, column(shape) // half
    return ((source & 1) == 0) & (target == source + 1)


def diagonals(square):
    shape = (SUB, CHUNK)
    group = column(shape) // SUB
    out = jnp.zeros(shape, F32)
    for b in range(CHUNK // SUB):
        out = out + jnp.where(group == b, square[b * SUB : (b + 1) * SUB], 0.0)
    return out


def at_lag(compact, lag):
    shape = (SUB, CHUNK)
    hit = row(shape) == (column(shape) & (SUB - 1)) - lag
    return jnp.sum(jnp.where(hit, compact, 0.0), axis=0, keepdims=True)


def undiagonal(lagged):
    shape = (SUB, CHUNK)
    place = (column(shape) & (SUB - 1)) - row(shape)
    compact = jnp.zeros(shape, F32)
    for lag, values in enumerate(lagged):
        compact = jnp.where(place == lag, values, compact)
    group = column(shape) // SUB
    return jnp.concatenate(
        [jnp.where(group == b, compact, 0.0) for b in range(CHUNK // SUB)], axis=0
    )


def read_slots(decays, written, c, affinity, entering, dot):
    near = affinity[c * CHUNK :]
    out = decays.from_start(c) * entering
    if c > 0:
        far = jnp.concatenate(
            [b * w for b, w in zip(decays.to_chunk(c), written[:c])], axis=1
        )
        out = out + decays.ahead[c] * dot(far, affinity[: c * CHUNK], NN)
    for h in HALVES:
        part = dot(decays.behind_in[c][h] * written[c], jnp.where(level_mask(h), near, 0.0), NN)
        out = out + decays.ahead_in[c][h] * part
    compact = diagonals(near)
    weight = written[c]
    for lag in range(SUB):
        out = out + weight * at_lag(compact, lag)
        if lag + 1 < SUB:
            weight = decays.short[c] * turn(weight, 1)
    return out


def mix_sources(decays, written, c, shares):
    lagged = [[] for _ in shares]
    weight = written[c]
    for lag in range(SUB):
        for place, share in enumerate(shares):
            lagged[place].append(jnp.sum(weight * share, axis=0, keepdims=True))
        if lag + 1 < SUB:
            weight = decays.short[c] * turn(weight, 1)
    outs = []
    for place, share in enumerate(shares):
        near = undiagonal(lagged[place])
        for h in HALVES:
            part = mm(decays.behind_in[c][h] * written[c], decays.ahead_in[c][h] * share, TN)
            near = near + jnp.where(level_mask(h), part, 0.0)
        if c > 0:
            far = jnp.concatenate(
                [b * w for b, w in zip(decays.to_chunk(c), written[:c])], axis=1
            )
            near = jnp.concatenate([mm(far, decays.ahead[c] * share, TN), near], axis=0)
        outs.append(near)
    return outs


def gather_back(decays, c, shares, affinities):
    outs = []
    if c > 0:
        pulled = sum(
            mm_fine(decays.ahead[c] * s, a[: c * CHUNK], NT) for s, a in zip(shares, affinities)
        )
        outs = [b * p for b, p in zip(decays.to_chunk(c), chunks_of(pulled))]
    nears = [a[c * CHUNK :] for a in affinities]
    own = 0.0
    for h in HALVES:
        mask = level_mask(h)
        pulled = sum(
            mm_fine(decays.ahead_in[c][h] * s, jnp.where(mask, a, 0.0), NT)
            for s, a in zip(shares, nears)
        )
        own = own + decays.behind_in[c][h] * pulled
    compacts = [diagonals(a) for a in nears]
    held = 0.0
    for lag in range(SUB - 1, -1, -1):
        if lag < SUB - 1:
            held = turn(decays.short[c] * held, -1)
        for s, a in zip(shares, compacts):
            held = held + s * at_lag(a, lag)
    outs.append(own + held)
    return outs


def silu(x):
    return x * jax.nn.sigmoid(x)


def silu_slope(x):
    sig = jax.nn.sigmoid(x)
    return sig * (1.0 + x * (1.0 - sig))


def gates(logits):
    small = jnp.exp(-jnp.abs(logits))
    ratio = small / (2.0 + small)
    square = ratio * ratio
    series = jnp.full_like(square, 1.0 / 17.0)
    for odd in (15, 13, 11, 9, 7, 5, 3, 1):
        series = series * square + 1.0 / odd
    log_keep = (jnp.minimum(logits, 0.0) - 2.0 * ratio * series) / GATE_SCALE
    keep = jnp.exp(log_keep)
    near = jnp.ones_like(log_keep)
    for order in (9, 8, 7, 6, 5, 4, 3, 2):
        near = 1.0 + log_keep / order * near
    return keep, jnp.where(log_keep > -0.5, -log_keep * near, 1.0 - keep)


def piece_state(key_raw, value_raw, keep, written):
    decays = Decays(keep)
    left = jnp.concatenate(
        [decays.to_end(c) * w for c, w in enumerate(chunks_of(written))], axis=1
    )
    keys, values = mm_fine(left, silu(key_raw), NN), mm_fine(left, silu(value_raw), NN)
    state = jnp.concatenate([keys, values], axis=1)
    return state, decays.survive()


def piece_read(query_raw, key_raw, value_raw, keep, written, slots_in):
    width = query_raw.shape[1]
    query, keys, values = silu(query_raw) * width**-0.5, silu(key_raw), silu(value_raw)
    slot_keys, slot_values = slots_in[:, :width], slots_in[:, width:]
    decays = Decays(keep)
    decays.levels()
    writes = chunks_of(written)
    entering = mm_fine(slot_keys, query, NT)
    readings, scores_all, shares = [], [], []
    for c in range(decays.count):
        last = (c + 1) * CHUNK
        affinity = mm_fine(keys[:last], query[c * CHUNK : last], NT)
        scores = read_slots(
            decays, writes, c, affinity, chunks_of(entering)[c], mm_fine
        )
        spread = jnp.exp(scores - jnp.max(scores, axis=0, keepdims=True))
        share = spread / jnp.sum(spread, axis=0, keepdims=True)
        (mixing,) = mix_sources(decays, writes, c, [share])
        reading = mm(mixing, values[:last], TN)
        reading = reading + mm(decays.from_start(c) * share, slot_values, TN)
        readings.append(reading)
        scores_all.append(scores)
        shares.append(share)
    return (
        jnp.concatenate(readings, axis=0),
        jnp.concatenate(scores_all, axis=1),
        jnp.concatenate(shares, axis=1),
    )


def add_chunks(total, extra):
    return [t + e for t, e in zip(total, extra)] + total[len(extra) :]


def piece_back(query_raw, key_raw, value_raw, keep, written, slots_in, scores, share, grad_read):
    width = query_raw.shape[1]
    query, keys, values = silu(query_raw) * width**-0.5, silu(key_raw), silu(value_raw)
    slot_keys, slot_values = slots_in[:, :width], slots_in[:, width:]
    decays = Decays(keep)
    decays.levels()
    writes = chunks_of(written)
    count = decays.count
    entering = chunks_of(mm_fine(slot_values, grad_read, NT))
    grad_q = []
    grad_k = [jnp.zeros((CHUNK, width), F32)] * count
    grad_v = [jnp.zeros((CHUNK, width), F32)] * count
    back = [jnp.zeros(writes[0].shape, F32)] * count
    direct_k, direct_v, own = 0.0, 0.0, []
    for c in range(count):
        last = (c + 1) * CHUNK
        here = slice(c * CHUNK, last)
        p = chunks_of(share)[c]
        affinity = mm_fine(keys[:last], query[here], NT)
        pull = mm_fine(values[:last], grad_read[here], NT)
        grad_p = read_slots(decays, writes, c, pull, entering[c], mm_fine)
        weighed = p * grad_p
        grad_s = weighed - p * jnp.sum(weighed, axis=0, keepdims=True)
        own.append(weighed + grad_s * chunks_of(scores)[c])
        mix_k, mix_v = mix_sources(decays, writes, c, [grad_s, p])
        from_start = decays.from_start(c)
        far_s, far_p = from_start * grad_s, from_start * p
        grad_q.append(mm(mix_k, keys[:last], TN) + mm(far_s, slot_keys, TN))
        grad_k = add_chunks(grad_k, rows_of(mm(mix_k, query[here], NN)))
        grad_v = add_chunks(grad_v, rows_of(mm(mix_v, grad_read[here], NN)))
        direct_k = direct_k + mm(far_s, query[here], NN)
        direct_v = direct_v + mm(far_p, grad_read[here], NN)
        back = add_chunks(back, gather_back(decays, c, [grad_s, p], [affinity, pull]))
    grad_query = jnp.concatenate(grad_q, axis=0) * width**-0.5 * silu_slope(query_raw)
    return (
        grad_query,
        jnp.concatenate(grad_k, axis=0),
        jnp.concatenate(grad_v, axis=0),
        jnp.concatenate([direct_k, direct_v], axis=1),
        jnp.concatenate(back, axis=1),
        jnp.concatenate(own, axis=1),
    )


def piece_after(
    key_raw, value_raw, keep, true_keep, written, grad_k, grad_v, back, own, after, slots_end
):
    width = key_raw.shape[1]
    keys, values = silu(key_raw), silu(value_raw)
    decays = Decays(keep)
    writes = chunks_of(written)
    to_end = jnp.concatenate([decays.to_end(c) for c in range(decays.count)], axis=1)
    left = to_end * written
    grad_k = grad_k + mm(left, after[:, :width], TN)
    grad_v = grad_v + mm(left, after[:, width:], TN)
    pulled = mm_fine(after[:, :width], keys, NT)
    pulled = pulled + mm_fine(after[:, width:], values, NT)
    back = back + to_end * pulled
    flow = own - written * back
    held = jnp.sum(after * slots_end, axis=1, keepdims=True)
    parts = chunks_of(flow)
    outs = []
    for part in reversed(parts):
        place, total, step = column(part.shape), part, 1
        while step < CHUNK:
            total = total + jnp.where(place < CHUNK - step, turn(total, -step), 0.0)
            step *= 2
        outs.append(total + held)
        held = held + total[:, :1]
    grad_log = jnp.concatenate(outs[::-1], axis=1) - true_keep * back
    return grad_k * silu_slope(key_raw), grad_v * silu_slope(value_raw), grad_log


def tie(value, *after):
    if not after:
        return value

    def body(*refs):
        pass

    anywhere = pl.BlockSpec(memory_space=pl.ANY)
    return pl.pallas_call(
        body,
        in_specs=[anywhere] * (1 + len(after)),
        out_specs=anywhere,
        out_shape=jax.ShapeDtypeStruct(value.shape, value.dtype),
        input_output_aliases={0: 0},
        cost_estimate=pl.CostEstimate(flops=0, bytes_accessed=0, transcendentals=0),
    )(value, *after)


def per_stream(work, arrays, outs, flops):
    def body(*refs):
        results = work(*[ref[...] for ref in refs[: len(arrays)]])
        for ref, result in zip(refs[len(arrays) :], results):
            ref[...] = result.astype(ref.dtype)

    def whole(shape):
        return pl.BlockSpec((None,) + tuple(shape[1:]), lambda s: (s, 0, 0))

    streams = arrays[0].shape[0]
    outs = [jax.ShapeDtypeStruct((streams,) + shape, kind) for shape, kind in outs]
    return pl.pallas_call(
        body,
        grid=(streams,),
        in_specs=[whole(a.shape) for a in arrays],
        out_specs=[whole(o.shape) for o in outs],
        out_shape=outs,
        compiler_params=pltpu.CompilerParams(vmem_limit_bytes=40 * 1024 * 1024),
        cost_estimate=pl.CostEstimate(flops=flops, bytes_accessed=1 << 16, transcendentals=0),
    )(*arrays)


def inverse_rms(values):
    return lax.rsqrt(jnp.mean(values * values, axis=-1, keepdims=True) + EPSILON)


def norm_back(values, scale, gain, grad):
    pulled = gain * grad
    along = jnp.mean(values * pulled, axis=-1, keepdims=True)
    return scale * pulled - values * (scale * scale * scale) * along


def product(left, right, dims):
    return lax.dot_general(left, right, (dims, ((), ())), preferred_element_type=F32)


def chain(earlier, later):
    return (earlier[0] * later[0], later[0][..., None] * earlier[1] + later[1])


CORE, X, Y, NEAR, FAR = 1, 2, 4, 8, 16


class Place:
    def __init__(self):
        self.seq, self.tp = lax.axis_index("seq"), lax.axis_index("tp")
        self.core, self.x = self.tp % 2, self.tp // 2
        self.y, self.z = self.seq % 2, self.seq // 2
        self.near, self.far = self.z % 2, self.z // 2
        self.flat = self.seq * 4 + self.tp

    def partner(self, mask):
        seq, tp = self.seq, self.tp
        if mask & CORE:
            tp = tp + 1 - 2 * self.core
        if mask & X:
            tp = tp + 2 - 4 * self.x
        if mask & Y:
            seq = seq + 1 - 2 * self.y
        if mask & NEAR:
            seq = seq + 2 - 4 * self.near
        if mask & FAR:
            seq = seq + 4 - 8 * self.far
        return seq, tp

    def z_turn(self, index):
        low, high = index % 2, index // 2
        low = low + self.near - 2 * low * self.near
        high = high + self.far - 2 * high * self.far
        return 2 * high + low


class Wire:
    LATENCY, LINK, BESIDE, AHEAD = 2.5, 2 / 91e3, 1 / 400e3, 5.0

    def __init__(self, place, sends, receives, locals_):
        self.place, self.sends, self.receives, self.locals = place, sends, receives, locals_
        self.remote, self.near_by, self.seen = [], [], set()
        self.now, self.due, self.free, self.rank = 0.0, {}, {}, 0
        self.queues = {"x": [], "y": [], "side": [], "middle": []}

    def greet(self, masks):
        barrier = pltpu.get_barrier_semaphore()
        for mask in masks:
            pl.semaphore_signal(
                barrier,
                inc=1,
                device_id=self.place.partner(mask),
                device_id_type=pl.DeviceIdType.MESH,
            )
        pl.semaphore_wait(barrier, len(masks))

    def spend(self, time):
        self.now += time

    def issue(self, at):
        source, target, mask = self.remote[at]
        copy = pltpu.make_async_remote_copy(
            src_ref=source,
            dst_ref=target,
            send_sem=self.sends.at[at],
            recv_sem=self.receives.at[at],
            device_id=self.place.partner(mask),
            device_id_type=pl.DeviceIdType.MESH,
        )
        copy.start()
        self.remote[at] = copy
        size = math.prod(source.shape) * jnp.dtype(source.dtype).itemsize
        if mask == CORE:
            uses = (("core", size * self.BESIDE),)
        elif mask & X:
            uses = (("x", size * self.LINK),)
        elif mask == Y:
            uses = (("y", size * self.LINK),)
        elif mask == NEAR:
            uses = (("side", size * self.LINK),)
        else:
            uses = (("side", size * self.LINK), ("middle", 2 * size * self.LINK))
        end = 0.0
        for link, time in uses:
            self.free[link] = max(self.now, self.free.get(link, 0.0)) + time
            end = max(end, self.free[link])
        self.due["remote", at] = end + self.LATENCY

    def send(self, source, target, mask):
        at = len(self.remote)
        self.remote.append((source, target, mask))
        if mask == CORE:
            self.issue(at)
        else:
            link = {Y: "y", NEAR: "side", FAR: "middle"}.get(mask, "x")
            self.queues[link].append((self.rank, at))
        return ("remote", at)

    def feed(self, until):
        fed = False
        for link, queue in self.queues.items():
            while queue and self.free.get(link, 0.0) < until + self.AHEAD:
                first = min(queue)
                queue.remove(first)
                self.issue(first[1])
                fed = True
        return fed

    def keep(self, source, target):
        at = len(self.near_by)
        copy = pltpu.make_async_copy(source, target, self.locals.at[at])
        copy.start()
        self.near_by.append(copy)
        self.due["local", at] = self.now + 2.0
        return ("local", at)

    def arrived(self, *handles):
        for handle in handles:
            if handle in self.seen:
                continue
            self.seen.add(handle)
            self.now = max(self.now, self.due[handle])
            if handle[0] == "remote":
                self.remote[handle[1]].wait_recv()
            else:
                self.near_by[handle[1]].wait()

    def run(self, *tasks):
        live = []
        for rank, task in enumerate(tasks):
            self.rank = rank
            live.append([rank, task, next(task)])

        def waits(entry):
            return entry[2]() if callable(entry[2]) else entry[2]

        def when(entry):
            handles = waits(entry)
            if handles is None:
                return 1e9, entry[0]
            dues = [self.due.get(h, 1e9) for h in handles if h not in self.seen]
            return max([self.now] + dues), entry[0]

        while live:
            entry = min(live, key=when)
            if self.feed(min(when(entry)[0], self.now + 1e6)):
                continue
            self.arrived(*waits(entry))
            self.rank = entry[0]
            try:
                entry[2] = next(entry[1])
            except StopIteration:
                live.remove(entry)
        self.feed(1e9)

    def finish(self):
        for at, copy in enumerate(self.remote):
            self.arrived(("remote", at))
            copy.wait_send()
        for at in range(len(self.near_by)):
            self.arrived(("local", at))


class Flags:
    def __init__(self):
        self.set = {}

    def raised(self, key, handles=()):
        self.set[key] = list(handles)

    def wait(self, *keys, more=()):
        def ask():
            if any(key not in self.set for key in keys):
                return None
            return [h for key in keys for h in self.set[key]] + list(more)

        return ask


def comm_call(work, number, masks, arrays, in_vmem, outs, out_vmem, scratch, copies, stay, mb=48):
    def space(fast):
        return pl.BlockSpec(memory_space=pltpu.VMEM if fast else pl.ANY)

    def body(*refs):
        n, m = len(arrays), len(outs)
        place = Place()
        wire = Wire(place, *refs[-3:])
        wire.greet(masks)
        work(place, wire, refs[:n], refs[n : n + m], refs[n + m : -3])
        wire.finish()

    return pl.pallas_call(
        body,
        in_specs=[space(v) for v in in_vmem],
        out_specs=[space(v) for v in out_vmem],
        out_shape=[jax.ShapeDtypeStruct(shape, kind) for shape, kind in outs],
        scratch_shapes=list(scratch)
        + [
            pltpu.SemaphoreType.DMA((copies,)),
            pltpu.SemaphoreType.DMA((copies,)),
            pltpu.SemaphoreType.DMA((max(stay, 1),)),
        ],
        compiler_params=pltpu.CompilerParams(
            collective_id=number, has_side_effects=True, vmem_limit_bytes=mb * 1024 * 1024
        ),
        cost_estimate=pl.CostEstimate(flops=0, bytes_accessed=1 << 16, transcendentals=0),
    )(*arrays)


def head_gather(place, wire, weight, out, flags=None, key=None, alike=False):
    rows, width = weight.shape[0], out.shape[1]
    block = 4 * rows
    base = place.y * 4 * block

    def columns(tp):
        return weight if alike else weight.at[:, pl.ds(pl.multiple_of(tp * width, 128), width)]

    def part(m):
        return out.at[pl.ds(pl.multiple_of(base + m * block, 16), block)]

    own = out.at[pl.ds(pl.multiple_of(base + place.tp * rows, 16), rows)]
    handles = [wire.keep(columns(place.tp), own)]
    for mask in (X, X | CORE, CORE):
        handles.append(wire.send(columns(place.partner(mask)[1]), own, mask))
    yield handles
    far = wire.send(part(0), part(2), FAR)
    near = wire.send(part(0), part(1), NEAR)
    over = [wire.send(part(0), part(0), Y)]
    yield [far]
    last = wire.send(part(2), part(3), NEAR)
    over.append(wire.send(part(2), part(2), Y))
    yield [near]
    over.append(wire.send(part(1), part(1), Y))
    yield [last]
    over.append(wire.send(part(3), part(3), Y))
    yield over
    if flags is not None:
        flags.raised(key)


def output_gather(place, wire, block, out, flags, key):
    def part(m):
        return out.at[m, place.y]

    yield [wire.keep(block, part(0))]
    far = wire.send(part(0), part(2), FAR)
    near = wire.send(part(0), part(1), NEAR)
    over = [wire.send(part(0), part(0), Y)]
    yield [far]
    last = wire.send(part(2), part(3), NEAR)
    over.append(wire.send(part(2), part(2), Y))
    yield [near]
    over.append(wire.send(part(1), part(1), Y))
    yield [last]
    over.append(wire.send(part(3), part(3), Y))
    yield over
    flags.raised(key)


def ffn_trade(place, wire, weight, halves, out):
    cols = halves.shape[2]

    def to_cut(rows):
        for y in range(2):
            halves[y, rows] = weight[rows, y * cols : (y + 1) * cols]

    row_loop(weight.shape[0], 32, to_cut)
    own = out.at[0, place.y]
    yield [
        wire.send(halves.at[1 - place.y], own, Y),
        wire.keep(halves.at[place.y], own),
    ]


def ffn_gather(place, wire, weight, halves, out):
    yield from ffn_trade(place, wire, weight, halves, out)
    yield from ffn_spread(place, wire, None, out)


def ffn_spread(place, wire, block, out):
    start = out.at[0] if block is None else block
    waits = [] if block is None else [wire.keep(block, out.at[0])]
    far = [wire.send(start.at[y], out.at[2, y], FAR) for y in range(2)]
    waits += [wire.send(start.at[y], out.at[1, y], NEAR) for y in range(2)]
    for y in range(2):
        yield [far[y]]
        waits.append(wire.send(out.at[2, y], out.at[3, y], NEAR))
    yield waits


def rows_gather(place, wire, own, out):
    mine = out.at[:, place.tp]
    stay = wire.keep(own, mine)
    across = wire.send(own, mine, X)
    beside = wire.send(own, mine, CORE)
    yield [across]
    theirs = out.at[:, place.partner(X)[1]]
    yield [stay, beside, wire.send(theirs, theirs, CORE)]


def small_gather(place, wire, own, out):
    handles = [
        wire.keep(own, out.at[pl.ds(place.flat, 1)]),
        wire.send(own, out.at[pl.ds(place.flat, 1)], CORE),
    ]
    size = 2
    for mask in (X, Y, NEAR, FAR):
        yield handles
        part = out.at[pl.ds(place.flat // size * size, size)]
        handles = [wire.send(part, part, mask)]
        size *= 2
    yield handles


def plane_gather(place, wire, first, second, out, flags=None):
    line_a = [out.at[0, 0, m] for m in range(4)]
    line_b = [out.at[0, 1, m] for m in range(4)]
    beside = [[], []]

    def pass_on(half, m, source=None):
        source = out.at[0, half, m] if source is None else source
        beside[half].append(wire.send(source, out.at[1, half, m], CORE))

    a_x = wire.send(first, line_a[1], X)
    b_y = wire.send(second, line_b[1], Y)
    a_y = wire.send(first, line_a[2], Y)
    b_x = wire.send(second, line_b[2], X)
    stay = [wire.keep(first, line_a[0]), wire.keep(second, line_b[0])]
    pass_on(0, 0, first)
    pass_on(1, 0, second)
    yield [a_x]
    a_xy = wire.send(line_a[1], line_a[3], Y)
    pass_on(0, 1)
    yield [b_y]
    b_xy = wire.send(line_b[1], line_b[3], X)
    pass_on(1, 1)
    yield [a_y, b_x]
    pass_on(0, 2)
    pass_on(1, 2)
    if flags is not None:
        flags.raised((0, 0), [stay[0], a_xy])
        flags.raised((0, 1), [stay[1], b_xy])
    yield [a_xy]
    pass_on(0, 3)
    if flags is not None:
        flags.raised((1, 0), beside[0])
    yield [b_xy]
    pass_on(1, 3)
    if flags is not None:
        flags.raised((1, 1), beside[1])
    yield stay + beside[0] + beside[1]


def heads_trade(place, wire, branch, out):
    width = out.shape[1] // 4

    def columns(ref, index):
        return ref.at[:, pl.ds(pl.multiple_of(index * width, 128), width)]

    mine = columns(out, place.z_turn(place.tp))
    handles = [wire.keep(columns(branch, place.tp), mine)]
    for mask in (X, X | CORE, CORE):
        handles.append(wire.send(columns(branch, place.partner(mask)[1]), mine, mask))
    yield handles


def heads_return(place, wire, grads, out):
    width = out.shape[1] // 4

    def columns(ref, index):
        return ref.at[:, pl.ds(pl.multiple_of(index * width, 128), width)]

    mine = columns(out, place.tp)
    handles = [wire.keep(columns(grads, place.z_turn(place.tp)), mine)]
    for mask in (X, X | CORE, CORE):
        there = place.z_turn(place.partner(mask)[1])
        handles.append(wire.send(columns(grads, there), mine, mask))
    yield handles


def pieces_scan(place, wire, reverse, survive, state, out, bufs):
    send_s, send_b, got_s, got_b = bufs
    wide = state.shape[-1] // survive.shape[-1]
    total_s, total_b = survive[...], state[...]
    before_s = before_b = None

    def join(first_s, first_b, second_s, second_b):
        spread = jnp.concatenate([second_s] * wide, axis=-1)
        return first_s * second_s, spread * first_b + second_b

    for step, (mask, bit) in enumerate(((Y, place.y), (NEAR, place.near), (FAR, place.far))):
        send_s[step] = total_s
        send_b[step] = total_b.astype(BF)
        yield [
            wire.send(send_b.at[step], got_b.at[step], mask),
            wire.send(send_s.at[step], got_s.at[step], mask),
        ]
        other_s, other_b = got_s[step], got_b[step].astype(F32)
        later = bit == (0 if reverse else 1)
        if before_s is None:
            before_s = jnp.where(later, other_s, 1.0)
            before_b = jnp.where(later, other_b, 0.0)
        else:
            joined_s, joined_b = join(other_s, other_b, before_s, before_b)
            before_s = jnp.where(later, joined_s, before_s)
            before_b = jnp.where(later, joined_b, before_b)
        if mask != FAR:
            first_s, first_b = jnp.where(later, other_s, total_s), jnp.where(later, other_b, total_b)
            second_s = jnp.where(later, total_s, other_s)
            second_b = jnp.where(later, total_b, other_b)
            total_s, total_b = join(first_s, first_b, second_s, second_b)
    out[...] = before_b


def scan_buffers(state_shape, survive_shape):
    return [
        pltpu.VMEM((3,) + survive_shape, F32),
        pltpu.VMEM((3,) + state_shape, BF),
        pltpu.VMEM((3,) + survive_shape, F32),
        pltpu.VMEM((3,) + state_shape, BF),
    ]


def row_loop(count, step, work):
    def body(i, carry):
        work(pl.ds(pl.multiple_of(i * step, step), step))
        return carry

    lax.fori_loop(0, count // step, body, 0)


def rows_fold(place, wire, part, sums, got_core, got_x, finish):
    streams, count = part.shape[0], part.shape[3]
    other_x = 1 - place.x
    beside = [wire.send(part.at[s, :, 1 - place.core], got_core.at[s], CORE) for s in range(streams)]
    across = []
    for s in range(streams):
        yield [beside[s]]

        def to_send(rows, s=s):
            term = part[s, other_x, place.core, rows].astype(F32)
            sums[s, rows] = (term + got_core[s, other_x, rows].astype(F32)).astype(BF)

        row_loop(count, 16, to_send)
        across.append(wire.send(sums.at[s], got_x.at[s], X))
    for s in range(streams):
        yield [across[s]]

        def to_finish(rows, s=s):
            term = part[s, place.x, place.core, rows].astype(F32)
            term = term + got_core[s, place.x, rows].astype(F32)
            finish(s, rows, term + got_x[s, rows].astype(F32))

        row_loop(count, 16, to_finish)


def rows_buffers(part_shape):
    streams, _, _, count, width = part_shape
    return [
        pltpu.VMEM((streams, count, width), BF),
        pltpu.VMEM((streams, 2, count, width), BF),
        pltpu.VMEM((streams, count, width), BF),
    ]


def plane_fold(place, wire, near_part, far_part, bufs, finish, flags=None):
    got_core, send_two, got_two, send_one, got_one = bufs
    count = near_part.shape[2]
    if flags is None:
        flags = Flags()
        for h in range(2):
            flags.raised(("far", h))
            flags.raised(("near", h))
    beside = {}
    for h in range(2):
        yield flags.wait(("far", h))
        for m in (2, 3, 1, 0):
            beside[h, m] = wire.send(far_part.at[h, m], got_core.at[h, m], CORE)
    two, one = {}, {}
    for h in range(2):
        yield flags.wait(("near", h), more=[beside[h, 2], beside[h, 3]])

        def to_two(rows, h=h):
            for m in (2, 3):
                term = near_part[h, m, rows].astype(F32) + got_core[h, m, rows].astype(F32)
                send_two[h, m - 2, rows] = term.astype(BF)

        row_loop(count, 16, to_two)
        two[h] = wire.send(send_two.at[h], got_two.at[h], (Y, X)[h])
    for h in range(2):
        yield [beside[h, 1], two[h]]

        def to_one(rows, h=h):
            term = near_part[h, 1, rows].astype(F32) + got_core[h, 1, rows].astype(F32)
            send_one[h, rows] = (term + got_two[h, 1, rows].astype(F32)).astype(BF)

        row_loop(count, 16, to_one)
        one[h] = wire.send(send_one.at[h], got_one.at[h], (X, Y)[h])
    for h in range(2):
        yield [beside[h, 0], one[h]]

        def to_finish(rows, h=h):
            def load(columns):
                term = near_part[h, 0, rows, columns].astype(F32)
                term = term + got_core[h, 0, rows, columns].astype(F32)
                term = term + got_two[h, 0, rows, columns].astype(F32)
                return term + got_one[h, rows, columns].astype(F32)

            finish(h, rows, load)

        row_loop(count, 16, to_finish)


def plane_buffers(part_shape):
    halves, _, count, width = part_shape
    return [
        pltpu.VMEM(part_shape, BF),
        pltpu.VMEM((halves, 2, count, width), BF),
        pltpu.VMEM((halves, 2, count, width), BF),
        pltpu.VMEM((halves, count, width), BF),
        pltpu.VMEM((halves, count, width), BF),
    ]


def z_parts(place, load, width):
    size = width // 4
    parts = []
    for m in range(4):
        there = pl.multiple_of(place.z_turn(m) * size, 128)
        parts.append(load(pl.ds(there, size)))
    return jnp.concatenate(parts, axis=-1)


def add_into(target, terms, step=32):
    def work(rows):
        total = terms[0][rows].astype(F32)
        for term in terms[1:]:
            total = total + term[rows].astype(F32)
        target[rows] = total.astype(BF)

    row_loop(target.shape[0], step, work)


def ffn_fold(place, wire, part, bufs, out, flags=None):
    got_near, got_far, held = bufs
    first, second, far = [], [], []
    for z, handles in ((3, first), (1, second)):
        for y in range(2):
            if flags is not None:
                yield flags.wait((z, y))
            handles.append(wire.send(part.at[z, y], got_near.at[z // 2, y], NEAR))
    for y in range(2):
        yield [first[y]] if flags is None else flags.wait((2, y), more=[first[y]])
        add_into(held.at[0, y], [part.at[2, y], got_near.at[1, y]])
        far.append(wire.send(held.at[0, y], got_far.at[y], FAR))
    for y in range(2):
        yield [second[y], far[y]] if flags is None else flags.wait((0, y), more=[second[y], far[y]])
        add_into(held.at[1, y], [part.at[0, y], got_near.at[0, y], got_far.at[y]])
    mine = out.at[place.y]
    yield [
        wire.send(held.at[1, 1 - place.y], mine, Y),
        wire.keep(held.at[1, place.y], mine),
    ]


def weight_tiles(wire, rows_by, order, grads, put, flags=None):
    for key in order:
        yield []
        put(key, mm(rows_by(key), grads(), TN))
        wire.spend(1.2)
        if flags is not None:
            flags.raised(key)


def head_tiles(wire, rows, grads, part, flags):
    side = part.shape[2]
    for z in (3, 1, 2, 0):
        for y in range(2):
            yield []
            at = (y * 4 + z) * side
            part[y, z] = mm(rows[:, at : at + side], grads(), TN).astype(BF)
            wire.spend(0.6)
        flags.raised(z)


def ffn_buffers(part_shape):
    _, ys, rows, width = part_shape
    return [
        pltpu.VMEM((2, ys, rows, width), BF),
        pltpu.VMEM((ys, rows, width), BF),
        pltpu.VMEM((2, ys, rows, width), BF),
    ]


def line_fold(place, wire, mine, theirs, bufs, flags=None):
    got_y, got_near, got_far, held = bufs
    over = {}
    for m in (3, 1, 2, 0):
        if flags is not None:
            yield flags.wait(m)
        over[m] = wire.send(theirs(m), got_y.at[m], Y)
    yield [over[3]]
    add_into(held.at[1], [mine(3), got_y.at[3]])
    last = wire.send(held.at[1], got_near.at[1], NEAR)
    yield [over[1]]
    add_into(held.at[0], [mine(1), got_y.at[1]])
    near = wire.send(held.at[0], got_near.at[0], NEAR)
    yield [over[2], last]
    add_into(held.at[2], [mine(2), got_y.at[2], got_near.at[1]])
    far = wire.send(held.at[2], got_far, FAR)
    yield [over[0], near, far]
    add_into(held.at[3], [mine(0), got_y.at[0], got_near.at[0], got_far])


def line_buffers(rows, width):
    return [
        pltpu.VMEM((4, rows, width), BF),
        pltpu.VMEM((2, rows, width), BF),
        pltpu.VMEM((rows, width), BF),
        pltpu.VMEM((4, rows, width), BF),
    ]


def head_fold(place, wire, part, bufs, out, flags=None):
    yield from line_fold(
        place, wire, lambda m: part.at[place.y, m], lambda m: part.at[1 - place.y, m], bufs, flags
    )
    own = bufs[3].at[3]
    rows, width = out.shape[0], own.shape[1]

    def block(tp):
        return own.at[pl.ds(pl.multiple_of(tp * rows, 16), rows)]

    mine = out.at[:, pl.ds(pl.multiple_of(place.tp * width, 128), width)]
    handles = [wire.keep(block(place.tp), mine)]
    for mask in (X, X | CORE, CORE):
        handles.append(wire.send(block(place.partner(mask)[1]), mine, mask))
    yield handles


def output_fold(place, wire, part, bufs, out, flags=None):
    yield from line_fold(
        place, wire, lambda m: part.at[m, place.y], lambda m: part.at[m, 1 - place.y], bufs, flags
    )
    yield [wire.keep(bufs[3].at[3], out)]


def small_fold(place, wire, values, bufs, out):
    got, total = bufs
    source, start, size = values, 0, 16
    steps = ((FAR, place.far), (NEAR, place.near), (Y, place.y), (X, place.x), (CORE, place.core))
    for mask, bit in steps:
        here = pl.ds(start, size)
        theirs = pl.ds(source_start(start, size) + (1 - bit) * size, size)
        yield [wire.send(source.at[theirs], got.at[here], mask)]
        mine = pl.ds(source_start(start, size) + bit * size, size)
        total[here] = source[mine] + got[here]
        source, start, size = total, start + size, size // 2
    out[...] = total[pl.ds(start - 1, 1)]


def source_start(start, size):
    return 0 if start == 0 else start - 2 * size


class Bits:
    CORE, X, Y, NEAR, FAR = 1, 2, 4, 8, 16

    def __init__(self):
        seq, tp = lax.axis_index("seq"), lax.axis_index("tp")
        self.core, self.x = tp & 1, tp >> 1
        self.y, self.z = seq & 1, seq >> 1

    def steps(self):
        return (
            (self.CORE, self.core),
            (self.X, self.x),
            (self.Y, self.y),
            (self.NEAR, self.z & 1),
            (self.FAR, self.z >> 1),
        )


def swap(values, mask):
    pairs = [(i, i ^ mask) for i in range(32)]
    return lax.ppermute(values, ("seq", "tp"), pairs)


def half(values, axis, which):
    size = values.shape[axis] // 2
    return lax.dynamic_slice_in_dim(values, which * size, size, axis)


def trade(values, mask, bit, axis, kind=None):
    other = half(values, axis, 1 - bit)
    if kind is not None:
        other = other.astype(kind)
    return half(values, axis, bit), swap(other, mask)


def in_order(mine, theirs, bit):
    first = bit == 0
    return jnp.where(first, mine, theirs), jnp.where(first, theirs, mine)


def z_blocks(block):
    far = swap(block, Bits.FAR)
    return [block, swap(block, Bits.NEAR), far, swap(far, Bits.NEAR)]


def z_fold(blocks, kind=BF):
    first = blocks[0] + swap(blocks[1].astype(kind), Bits.NEAR).astype(F32)
    second = blocks[2] + swap(blocks[3].astype(kind), Bits.NEAR).astype(F32)
    return first + swap(second.astype(kind), Bits.FAR).astype(F32)


def z_relative(values, z, axis):
    size = values.shape[axis] // 4
    return jnp.concatenate(
        [lax.dynamic_slice_in_dim(values, (m ^ z) * size, size, axis) for m in range(4)], axis
    )


def spread_tp(values, at):
    streams, count, width = values.shape
    pair = jnp.stack(in_order(values, swap(values, Bits.X), at.x), axis=1)
    both = jnp.stack(in_order(pair, swap(pair, Bits.CORE), at.core), axis=2)
    return both.reshape(streams, 4 * count, width)


def fold_tp(part, at):
    streams, count, width = part.shape
    parts = part.reshape(streams, 2, 2, count // 4, width)
    mine, got = trade(parts, Bits.CORE, at.core, 2, BF)
    mine, got = trade(mine + got.astype(F32), Bits.X, at.x, 1, BF)
    return (mine + got.astype(F32)).reshape(streams, count // 4, width)


def spread_plane(rows):
    count = rows.shape[0] // 2
    first, second = rows[:count], rows[count:]
    first = jnp.concatenate([first, swap(first, Bits.X)], axis=0)
    second = jnp.concatenate([second, swap(second, Bits.Y)], axis=0)
    four = [first, swap(first, Bits.Y), second, swap(second, Bits.X)]
    four = jnp.concatenate(four, axis=0)
    return jnp.concatenate([four, swap(four, Bits.CORE)], axis=0)


def fold_half(part, mask):
    size = part.shape[0] // 2
    return part[:size] + swap(part[size:].astype(BF), mask).astype(F32)


def fold_plane(work):
    sent = swap(work(1).astype(BF), Bits.CORE)
    part = work(0) + sent.astype(F32)
    size = part.shape[0] // 2
    first = fold_half(fold_half(part[:size], Bits.Y), Bits.X)
    second = fold_half(fold_half(part[size:], Bits.X), Bits.Y)
    return jnp.concatenate([first, second], axis=0)


def gather_head(weight, at):
    rows, width = weight.shape
    mine, got = trade(weight, Bits.X, at.x, 1)
    both = jnp.stack(in_order(mine, got, at.x), axis=0)
    mine, got = trade(both, Bits.CORE, at.core, 2)
    both = jnp.stack(in_order(mine, got, at.core), axis=1).reshape(4 * rows, width // 4)
    line = jnp.concatenate(z_blocks(both), axis=0)
    return jnp.concatenate(in_order(line, swap(line, Bits.Y), at.y), axis=0)


def fold_head(grad, at):
    mine, got = trade(grad, Bits.Y, at.y, 0, BF)
    line = mine + got.astype(F32)
    rows = line.shape[0] // 4
    own = z_fold([line[m * rows : (m + 1) * rows] for m in range(4)])
    width = own.shape[1]
    own = own.reshape(2, 2, rows // 4, width)
    mine, got = trade(own, Bits.CORE, at.core, 1, BF)
    own = jnp.concatenate(in_order(mine, got.astype(F32), at.core), axis=-1)
    mine, got = trade(own, Bits.X, at.x, 0, BF)
    own = jnp.concatenate(in_order(mine, got.astype(F32), at.x), axis=-1)
    return own.reshape(rows // 4, 4 * width)


def turn_bits(values, back):
    pairs = []
    for i in range(32):
        z, y, x, core = i >> 3, (i >> 2) & 1, (i >> 1) & 1, i & 1
        there = z * 8 + core * 4 + y * 2 + x
        pairs.append((there, i) if back else (i, there))
    return lax.ppermute(values, ("seq", "tp"), pairs)


def gather_output(weight, at):
    block = turn_bits(weight, False)
    line = jnp.stack(z_blocks(block), axis=0)
    both = jnp.stack(in_order(line, swap(line, Bits.Y), at.y), axis=1)
    return both.reshape(8 * weight.shape[0], weight.shape[1])


def fold_output(grad, at):
    rows, width = grad.shape
    parts = grad.reshape(4, 2, rows // 8, width)
    mine, got = trade(parts, Bits.Y, at.y, 1, BF)
    line = (mine + got.astype(F32)).reshape(4, rows // 8, width)
    own = z_fold([line[m] for m in range(4)])
    return turn_bits(own.astype(BF), True).astype(F32)


def heads_to_rows(values, at):
    mine, got = trade(values, Bits.X, at.x, 1)
    both = jnp.stack(in_order(mine, got, at.x), axis=0)
    mine, got = trade(both, Bits.CORE, at.core, 2)
    both = jnp.stack(in_order(mine, got, at.core), axis=1)
    parts = both.reshape((4,) + both.shape[2:])
    return jnp.concatenate(
        [lax.dynamic_index_in_dim(parts, m ^ at.z, 0, False) for m in range(4)], axis=1
    )


def rows_to_heads(values, at):
    width = values.shape[1] // 4
    parts = jnp.stack(
        [
            lax.dynamic_slice_in_dim(values, (m ^ at.z) * width, width, 1)
            for m in range(4)
        ],
        axis=0,
    ).reshape(2, 2, values.shape[0], width)
    mine, got = trade(parts, Bits.X, at.x, 0)
    first, second = in_order(mine[0], got[0], at.x)
    both = jnp.stack([first, second], axis=0)
    mine, got = trade(both, Bits.CORE, at.core, 1)
    first, second = in_order(mine[:, 0], got[:, 0], at.core)
    both = jnp.stack([first, second], axis=1)
    return jnp.concatenate([both[0, 0], both[0, 1], both[1, 0], both[1, 1]], axis=1)


class FfnGather:
    def __init__(self, weight, at):
        mine, got = trade(weight, Bits.Y, at.y, 1)
        self.block = jnp.concatenate(in_order(mine, got, at.y), axis=0)

    def far(self, *after):
        self.block = tie(self.block, *after)
        self.far_block = swap(self.block, Bits.FAR)
        return (self.far_block,)

    def near(self, *after):
        self.block = tie(self.block, *after)
        self.near_block = swap(self.block, Bits.NEAR)
        self.last_block = swap(self.far_block, Bits.NEAR)
        return (self.near_block, self.last_block)

    def whole(self):
        parts = [self.block, self.near_block, self.far_block, self.last_block]
        return jnp.concatenate(parts, axis=0)


class FfnFold:
    def __init__(self, grad, at):
        self.at = at
        rows = grad.shape[0] // 4
        self.parts = [grad[m * rows : (m + 1) * rows] for m in range(4)]

    def near(self, *after):
        sent = [tie(self.parts[1].astype(BF), *after), self.parts[3].astype(BF)]
        self.got = [swap(s, Bits.NEAR) for s in sent]
        return tuple(self.got)

    def far(self, *after):
        second = self.parts[2] + self.got[1].astype(F32)
        self.last = swap(tie(second.astype(BF), *after), Bits.FAR)
        return (self.last,)

    def whole(self):
        own = self.parts[0] + self.got[0].astype(F32) + self.last.astype(F32)
        mine, got = trade(own, Bits.Y, self.at.y, 0, BF)
        return jnp.concatenate(in_order(mine, got.astype(F32), self.at.y), axis=1)


class PlainWhole:
    def __init__(self, value):
        self.value = value

    def far(self, *after):
        return ()

    near = far

    def whole(self):
        return self.value


def spread_all(values, at):
    for mask, bit in at.steps():
        values = jnp.concatenate(in_order(values, swap(values, mask), bit), axis=0)
    return values


def fold_all(values, at):
    for mask, bit in reversed(at.steps()):
        mine, got = trade(values, mask, bit, 0)
        values = mine + got
    return values


def scan_pieces(part, at, reverse):
    total, before = part, None
    steps = ((Bits.Y, at.y), (Bits.NEAR, at.z & 1), (Bits.FAR, at.z >> 1))
    for mask, bit in steps:
        other = (swap(total[0], mask), swap(total[1].astype(BF), mask).astype(F32))
        later = bit == (0 if reverse else 1)
        if before is None:
            before = (
                jnp.where(later, other[0], 1.0),
                jnp.where(later, other[1], 0.0),
            )
        else:
            joined = chain(other, before)
            before = tuple(jnp.where(later, a, b) for a, b in zip(joined, before))
        if mask != Bits.FAR:
            first = tuple(jnp.where(later, o, t) for o, t in zip(other, total))
            second = tuple(jnp.where(later, t, o) for o, t in zip(other, total))
            total = chain(first, second)
    return before


@dataclasses.dataclass
class Mixer:
    reading: jax.Array
    scores: jax.Array
    share: jax.Array
    branch: jax.Array
    rows: jax.Array
    normed: jax.Array
    low: jax.Array
    low_rank: jax.Array
    rank: jax.Array
    logits: jax.Array
    keep: jax.Array
    true_keep: jax.Array
    written: jax.Array
    survive: jax.Array
    slots_in: jax.Array
    slots_end: jax.Array
    weights: list
    raw: list
    output: jax.Array
    out_gain: jax.Array
    ffn_gain: jax.Array
    attn_gain: jax.Array


def alive_rows(seq_cuts, seq, length):
    positions = seq * length + jnp.arange(length)
    starts = (positions[None, :] == 0) | (positions[None, :] == seq_cuts[:, None])
    return jnp.where(starts, 0.0, 1.0).astype(F32)[:, None, :]


class Plain:
    def __init__(self):
        self.seq, self.tp = lax.axis_index("seq"), lax.axis_index("tp")
        self.seq_count, self.tp_count = lax.axis_size("seq"), lax.axis_size("tp")
        self.sharing = self.tp_count // H
        self.head, self.member = self.tp // self.sharing, self.tp % self.sharing


def plain_scan(part, at, reverse):
    gathered = (
        lax.all_gather(part[0], "seq"),
        lax.all_gather(part[1].astype(BF), "seq"),
    )
    state = (jnp.ones_like(part[0]), jnp.zeros_like(part[1]))

    def step(count, state):
        source = at.seq_count - 1 - count if reverse else count
        piece = tuple(lax.dynamic_index_in_dim(a, source, 0, False) for a in gathered)
        return chain(state, (piece[0], piece[1].astype(F32)))

    steps = at.seq_count - 1 - at.seq if reverse else at.seq
    return lax.fori_loop(0, steps, step, state)


class PlainMoves:
    def small(self, packed):
        return lax.all_gather(packed, ("seq", "tp"))

    def small_sum(self, packed):
        return lax.psum_scatter(packed, ("seq", "tp"), scatter_dimension=0, tiled=True)[0]

    def start(self, tokens, seq_cuts, weights, w_output, small, ffn, cotangent):
        self.ffn = ffn
        devices = self.at.seq_count * self.at.tp_count
        gathered = self.small(jnp.concatenate([a.reshape(-1) for a in small]))
        unpacked, taken = [], 0
        for a in small:
            part = gathered[:, taken : taken + a.size]
            unpacked.append(part.reshape((devices * a.shape[0],) + a.shape[1:]))
            taken += a.size
        low, full_rank, full_bias, attn, out, ffn_gain = unpacked
        slots = full_bias.shape[0] // H
        rank = lax.dynamic_slice_in_dim(full_rank, self.head * slots, slots, 0).astype(F32)
        bias = lax.dynamic_slice_in_dim(full_bias, self.head * slots, slots, 0).astype(F32)
        rows = self.piece(tokens)
        held, length, width = rows.shape
        inputs = rows.reshape(held * length, width).astype(F32)
        normed = (inputs * inverse_rms(inputs) * attn.astype(F32)).astype(BF)
        low_rank = product(normed, low, NN).reshape(held, length, -1)
        logits = jnp.einsum("mr,str->smt", rank, low_rank, precision=lax.Precision.HIGHEST)
        logits = logits + bias[None, :, None]
        true_keep, written = gates(logits)
        alive = self.own_streams(alive_rows(seq_cuts, self.at.seq, length))
        keep = true_keep * alive
        weights = [self.head_weight(w) for w in weights]
        raw = [product(normed, w, NN).reshape(held, length, -1) for w in weights]
        hd = raw[0].shape[-1]
        state, survive = per_stream(
            piece_state,
            [raw[0], raw[1], keep, written],
            [((slots, 2 * hd), F32), ((slots, 1), F32)],
            1 << 30,
        )
        slots_in = self.scan((survive[..., 0], state), False)[1]
        key_raw, value_raw, query_raw, gate_raw = raw
        reading, scores, share = per_stream(
            piece_read,
            [query_raw, key_raw, value_raw, keep, written, slots_in],
            [((length, hd), F32), ((slots, length), F32), ((slots, length), F32)],
            1 << 30,
        )
        read_normed = reading * inverse_rms(reading) * out.astype(F32)
        branch = (read_normed * silu(gate_raw)).astype(BF).reshape(held * length, hd)
        output = self.output_weight(w_output)
        self.mixed = product(branch, output, NN).reshape(held, length, width)
        return Mixer(
            reading=reading,
            scores=scores,
            share=share,
            branch=branch,
            rows=rows,
            normed=normed,
            low=low,
            low_rank=low_rank,
            rank=rank,
            logits=logits,
            keep=keep,
            true_keep=true_keep,
            written=written,
            survive=survive[..., 0],
            slots_in=slots_in,
            slots_end=survive * slots_in + state,
            weights=weights,
            raw=raw,
            output=output,
            out_gain=out.astype(F32),
            ffn_gain=ffn_gain.astype(F32),
            attn_gain=attn.astype(F32),
        )

    def feed_forward(self, tokens, gain, cotangent):
        streams, count, width = tokens.shape
        own_rows = streams * count
        hidden = (tokens.astype(F32) + self.sum_piece(self.mixed)).reshape(own_rows, width)
        scale = inverse_rms(hidden)
        ffn_in = self.ffn_rows((hidden * scale * gain).astype(BF))
        cot = self.ffn_rows(cotangent.reshape(own_rows, width))
        down, gate, up = [lax.all_gather(w, "seq", axis=0, tiled=True) for w in self.ffn]
        grad_product = product(cot, down, NN)
        gate_pre, up_pre = product(ffn_in, gate, NN), product(ffn_in, up, NN)
        sig = jax.nn.sigmoid(gate_pre)
        act = (gate_pre * sig * up_pre).astype(BF)
        slope = sig * (1.0 + gate_pre * (1.0 - sig))
        grad_gate = (grad_product * up_pre * slope).astype(BF)
        grad_up = (grad_product * gate_pre * sig).astype(BF)
        grad = self.ffn_sum(product(grad_gate, gate, NT) + product(grad_up, up, NT))
        self.gate_grad = self.ffn_grad(product(ffn_in, grad_gate, TN).astype(BF))
        self.up_grad = self.ffn_grad(product(ffn_in, grad_up, TN).astype(BF))
        self.down_sum = self.ffn_grad(product(cot, act, TN).astype(BF))
        self.result = (hidden + self.ffn_sum(product(act, down, NT))).astype(BF)
        gain_grad = jnp.sum(grad * hidden * scale, axis=0)
        grad_hidden = cotangent.reshape(own_rows, width).astype(F32)
        grad_hidden = grad_hidden + norm_back(hidden, scale, gain, grad)
        return grad_hidden, gain_grad, self.piece(grad_hidden.astype(BF).reshape(cotangent.shape))

    def ffn_grad(self, grad):
        own = lax.psum_scatter(grad, "seq", scatter_dimension=0, tiled=True)
        return own.astype(F32)

    def mixer_back(self, mixer, grad_mixed):
        reading, scores, share, branch_out = mixer.reading, mixer.scores, mixer.share, mixer.branch
        streams, length, hd = reading.shape
        slots = scores.shape[1]
        key_raw, value_raw, query_raw, gate_raw = mixer.raw
        grad_branch = product(grad_mixed, mixer.output, NT).reshape(reading.shape)
        self.output_sum = self.output_grad(product(branch_out, grad_mixed, TN))
        scale = inverse_rms(reading)
        normed = reading * scale * mixer.out_gain
        grad_gate = (grad_branch * normed * silu_slope(gate_raw)).astype(BF)
        grad = grad_branch * silu(gate_raw)
        gain_sum = jnp.sum(grad * reading * scale, axis=(0, 1))[None]
        grad_read = norm_back(reading, scale, mixer.out_gain, grad)
        grad_query, grad_k, grad_v, direct, back, own = per_stream(
            piece_back,
            [query_raw, key_raw, value_raw, mixer.keep, mixer.written]
            + [mixer.slots_in, scores, share, grad_read],
            [
                ((length, hd), BF),
                ((length, hd), F32),
                ((length, hd), F32),
                ((slots, 2 * hd), F32),
                ((slots, length), F32),
                ((slots, length), F32),
            ],
            1 << 30,
        )
        after = self.scan((mixer.survive, direct), True)[1]
        self.head_sums = [
            self.head_grad(product(mixer.normed, g.reshape(-1, hd), TN))
            for g in (grad_query, grad_gate)
        ]
        return after, gain_sum, grad_query, grad_gate, grad_k, grad_v, back, own

    def end(self, mixer, grads, normed_part, packed):
        hd = grads[0].shape[-1]
        heads = [
            self.head_grad(product(mixer.normed, g.reshape(-1, hd), TN)) for g in grads
        ]
        heads = heads + self.head_sums + [self.output_sum]
        return (
            heads,
            [self.gate_grad, self.up_grad, self.down_sum],
            self.sum_piece(normed_part),
            self.small_sum(packed),
            self.result,
        )

    def __init__(self):
        self.at = Plain()
        self.head, self.member = self.at.head, self.at.member

    def own_streams(self, values):
        count = values.shape[0] // self.at.sharing
        return lax.dynamic_slice_in_dim(values, self.member * count, count, 0)

    def piece(self, own):
        return self.own_streams(lax.all_gather(own, "tp", axis=1, tiled=True))

    def sum_piece(self, part):
        streams = part.shape[0] * self.at.sharing
        entire = jnp.zeros((streams,) + part.shape[1:], BF)
        entire = lax.dynamic_update_slice_in_dim(
            entire, part.astype(BF), self.member * part.shape[0], 0
        )
        own = lax.psum_scatter(entire, "tp", scatter_dimension=1, tiled=True)
        return own.astype(F32)

    def mixer_order(self, values):
        return values

    mixer_unorder = ffn_order = ffn_unorder = mixer_order

    def head_weight(self, weight):
        entire = lax.all_gather(weight, ("seq", "tp"), axis=0, tiled=True)
        width = entire.shape[1] // H
        return lax.dynamic_slice_in_dim(entire, self.head * width, width, 1)

    def head_grad(self, grad):
        entire = jnp.zeros((grad.shape[0], grad.shape[1] * H), BF)
        entire = lax.dynamic_update_slice_in_dim(
            entire, grad.astype(BF), self.head * grad.shape[1], 1
        )
        own = lax.psum_scatter(entire, ("seq", "tp"), scatter_dimension=0, tiled=True)
        return own.astype(F32)

    def output_weight(self, weight):
        entire = lax.all_gather(weight, ("seq", "tp"), axis=0, tiled=True)
        rows = entire.shape[0] // H
        return lax.dynamic_slice_in_dim(entire, self.head * rows, rows, 0)

    def output_grad(self, grad):
        entire = jnp.zeros((grad.shape[0] * H, grad.shape[1]), BF)
        entire = lax.dynamic_update_slice_in_dim(
            entire, grad.astype(BF), self.head * grad.shape[0], 0
        )
        own = lax.psum_scatter(entire, ("seq", "tp"), scatter_dimension=0, tiled=True)
        return own.astype(F32)

    def scan(self, part, reverse):
        return plain_scan(part, self.at, reverse)

    def ffn_rows(self, own):
        entire = lax.all_gather(own, "tp", axis=0)
        return entire.reshape((-1,) + own.shape[1:])

    def ffn_sum(self, part):
        parts = part.astype(BF).reshape((self.at.tp_count, -1) + part.shape[1:])
        own = lax.psum_scatter(parts, "tp", scatter_dimension=0, tiled=True)
        return own.reshape((-1,) + part.shape[1:]).astype(F32)


class BitMoves:
    def __init__(self):
        self.at = Bits()
        self.head, self.member = lax.axis_index("tp"), 0

    def start(self, tokens, seq_cuts, weights, w_output, small, ffn, cotangent):
        w_low, w_rank, bias, attn_gain, out_gain, ffn_gain = small
        rank = w_low.shape[1]
        gains = jnp.stack([attn_gain, ffn_gain], axis=1)
        pack = jnp.concatenate([w_low, gains], axis=1)
        pack = jnp.pad(pack, ((0, 0), (0, 128 - pack.shape[1])))
        tall = w_rank.shape[0]
        lines = jnp.concatenate([w_rank, bias[:, None]], axis=1)
        lines = jnp.pad(lines, ((0, 0), (0, 128 - lines.shape[1])))
        gain_line = jnp.pad(out_gain, (0, 128 - out_gain.shape[0]))[None]
        lines = jnp.concatenate([lines, gain_line], axis=0)
        lines = jnp.pad(lines, ((0, 16 - lines.shape[0]), (0, 0)))[None]
        streams, count, width = tokens.shape
        length = 4 * count
        hd = width // 4
        per = out_gain.shape[0]
        slots = 8 * tall
        head = (width, hd)
        cut = (2, ffn[0].shape[0], ffn[0].shape[1] // 2)
        ffn_shape = (4,) + cut
        block = turn_bits(w_output, False)
        alive = alive_rows(seq_cuts, lax.axis_index("seq"), length)
        state_shape, slim = (streams, slots, 2 * hd), (streams, slots, 128)
        gate_shape = (streams, slots, length)

        def work(place, wire, given, outs, scratch):
            pack, lines, tokens, alive, own_tokens = given[:5]
            given = given[1:]
            heads_in, block, ffn_in, cot = given[4:8], given[8], given[9:12], given[12]
            pack_out, lines_out, low_out, logits, keep, true_keep, written = outs[:7]
            survive, slots_in, slots_end, scores, share = outs[7:12]
            rows_out, normed_out, reading_out, branch_out, hidden_out = outs[12:17]
            heads_out, raws_out, output_out = outs[17:21], outs[21:25], outs[25]
            ffn_out, cot_out, ffn_rows, grad_product = outs[26:29], outs[29], outs[30], outs[31]
            rows, normed, state = scratch[:3]
            heads, raws, cuts, scan = scratch[3:7], scratch[7:11], scratch[11:14], scratch[14:18]
            output_w, reading, branch, traded, mixed = scratch[18:23]
            hidden, ready, gain_rows, cot_rows, down = scratch[23:28]
            fold_bufs = scratch[28:31]
            here = Flags()

            def fetch_rows():
                yield from rows_gather(place, wire, tokens, rows)
                here.raised("rows")
                wire.keep(rows, rows_out)

            def fetch_lines():
                yield from small_gather(place, wire, lines, lines_out)
                here.raised("lines")

            def norm():
                gain = jnp.transpose(pack_out[...].astype(F32))[rank : rank + 1]
                steps = count // 16

                def body(i, carry):
                    stream, tp, part = i // (4 * steps), i // steps % 4, i % steps
                    at = pl.multiple_of(part * 16, 16)
                    x = rows[stream, tp, pl.ds(at, 16)].astype(F32)
                    to = pl.multiple_of(i * 16, 16)
                    normed[pl.ds(to, 16)] = (x * inverse_rms(x) * gain).astype(BF)
                    return carry

                lax.fori_loop(0, streams * 4 * steps, body, 0)

            def project(index):
                for s in range(streams):
                    raws[index][s] = mm(normed[s * length : (s + 1) * length], heads[index][...], NN)
                wire.spend(3.0)
                here.raised(("raw", index))
                wire.keep(heads[index], heads_out[index])
                wire.keep(raws[index], raws_out[index])

            def gains():
                own = lines_out[...].astype(F32)[:, tall]
                spot, turn_of = row((128, hd)), column((128, hd))
                spread = jnp.where(spot == turn_of % per, 1.0, 0.0)
                wide = mm(own, spread, NN)
                here_is = row(wide.shape) == column(wide.shape) // per
                out_row = jnp.sum(jnp.where(here_is, wide, 0.0), axis=0, keepdims=True)
                gain_rows[0:1, :hd] = out_row
                ffn_row = jnp.transpose(pack_out[...].astype(F32))[rank + 1 : rank + 2]
                side = width // 8
                for y in range(2):
                    for m in range(4):
                        to = pl.multiple_of((place.z_turn(m) * 2 + y) * side, 128)
                        at = (y * 4 + m) * side
                        gain_rows[1:2, pl.ds(to, side)] = ffn_row[:, at : at + side]

            def read(s, carry):
                values = piece_read(
                    raws[2][s], raws[0][s], raws[1][s], keep[s], written[s], slots_in[s]
                )
                reading[s], scores[s], share[s] = values
                return carry

            def gated(s):
                def chunk(part):
                    at = pl.ds(pl.multiple_of(s * length + part.start, 16), part.size)
                    values = reading[s, part]
                    normed_read = values * inverse_rms(values) * gain_rows[0:1, :hd]
                    branch[at] = (normed_read * silu(raws[3][s, part])).astype(BF)

                row_loop(length, 32, chunk)

            def finish(stream, rows, part):
                values = own_tokens[stream, rows].astype(F32) + part
                hidden[stream, rows] = values
                normed = (values * inverse_rms(values) * gain_rows[1:2]).astype(BF)
                size = width // 4
                for m in range(4):
                    there = pl.ds(pl.multiple_of(place.z_turn(m) * size, 128), size)
                    ready[stream, rows, there] = normed[:, m * size : (m + 1) * size]

            def to_rows():
                yield here.wait("branch")
                yield from heads_trade(place, wire, branch, traded)
                here.raised("traded")
                wire.keep(traded, branch_out)
                yield here.wait("mixed")
                yield from rows_fold(place, wire, mixed, *fold_bufs, finish)
                wire.keep(hidden, hidden_out)
                yield from plane_gather(place, wire, ready.at[0], ready.at[1], ffn_rows)

            def fetch_down():
                yield from ffn_gather(place, wire, ffn_in[0], cuts[0], down)
                here.raised("down")
                wire.keep(down, ffn_out[0])

            def fetch_cot():
                yield from plane_gather(place, wire, cot.at[0], cot.at[1], cot_rows)
                here.raised("cot")
                wire.keep(cot_rows, cot_out)

            def product_grads():
                yield here.wait("down", "cot")
                for c in range(2):
                    for h in range(2):
                        values = cot_rows[c, h].reshape(4 * count, width)
                        total = mm(values, down[...].reshape(width, ffn_shape[-1]), NN)
                        grad_product[c, h] = total.astype(BF)
                        wire.spend(1.5)
                        yield []

            def compute():
                yield here.wait("rows", "pack")
                norm()
                wire.spend(3.0)
                wire.keep(normed, normed_out)
                yield here.wait("lines")
                own = lines_out[pl.ds(place.tp * 8, 8)].astype(F32)[:, :tall].reshape(slots, 128)
                factor = jnp.where(column(own.shape) < rank, own, 0.0)
                for s in range(streams):
                    low = mm(normed[s * length : (s + 1) * length], pack_out[...], NN)
                    low_out[s] = low
                    f = mm_fine(factor, low, NT) + own[:, rank : rank + 1]
                    logits[s] = f
                    kept, wrote = gates(f)
                    true_keep[s] = kept
                    written[s] = wrote
                    keep[s] = kept * alive[s]
                wire.spend(2.0)
                for index in range(2):
                    yield here.wait(index)
                    project(index)
                for s in range(streams):
                    part, left = piece_state(raws[0][s], raws[1][s], keep[s], written[s])
                    state[s] = part
                    survive[s] = jnp.broadcast_to(left, slim[1:])
                wire.spend(3.0)
                here.raised("state")
                for index in (2, 3):
                    yield here.wait(index)
                    project(index)
                gains()
                yield here.wait("slots")
                lax.fori_loop(0, streams, read, 0)
                wire.spend(10.0)
                for s in range(streams):
                    gated(s)
                wire.spend(2.0)
                here.raised("branch")
                wire.keep(reading, reading_out)
                yield here.wait("traded", 4)
                wire.keep(output_w, output_out)
                for s in range(streams):
                    rows_in = traded[s * length : (s + 1) * length]
                    total = mm(rows_in, output_w[...].reshape(hd, width), NN)
                    mixed[s] = total.astype(BF).reshape(mixed.shape[1:])
                wire.spend(2.5)
                here.raised("mixed")

            def exchange():
                yield here.wait("state")
                yield from pieces_scan(place, wire, False, survive, state, slots_in, scan)
                for s in range(streams):
                    slots_end[s] = survive[s][:, :1] * slots_in[s] + state[s]
                here.raised("slots")

            wire.run(
                fetch_lines(),
                head_gather(place, wire, pack, pack_out, here, "pack", True),
                fetch_rows(),
                exchange(),
                to_rows(),
                *[
                    head_gather(place, wire, w, o, here, i)
                    for i, (w, o) in enumerate(zip(heads_in, heads))
                ],
                output_gather(place, wire, block, output_w, here, 4),
                fetch_down(),
                fetch_cot(),
                ffn_gather(place, wire, ffn_in[1], cuts[1], ffn_out[1]),
                ffn_gather(place, wire, ffn_in[2], cuts[2], ffn_out[2]),
                product_grads(),
                compute(),
            )

        vmem = pltpu.VMEM
        plane = (2, 2, 4, count, width)
        flat = (streams * length, width)
        raw = (streams, length, hd)
        mixed_shape = (streams, 2, 2, count, width)
        group = (2, 2, length, ffn_shape[-1])
        outs = comm_call(
            work,
            1,
            (CORE, X, X | CORE, Y, NEAR, FAR),
            [pack, lines, self.mixer_order(tokens), alive, tokens]
            + list(weights)
            + [block]
            + list(ffn)
            + [self.ffn_order(cotangent)],
            [False, False, False, True, True] + [False] * 5 + [True] * 3 + [False],
            [
                ((width, 128), BF),
                ((32, 16, 128), BF),
                ((streams, length, 128), F32),
                (gate_shape, F32),
                (gate_shape, F32),
                (gate_shape, F32),
                (gate_shape, F32),
                (slim, F32),
                (state_shape, F32),
                (state_shape, F32),
                (gate_shape, F32),
                (gate_shape, F32),
                ((streams, 4, count, width), BF),
                (flat, BF),
                (raw, F32),
                ((flat[0], hd), BF),
                (tokens.shape, F32),
            ]
            + [(head, BF)] * 4
            + [(raw, F32)] * 4
            + [((4, 2) + block.shape, BF)]
            + [(ffn_shape, BF)] * 3
            + [(plane, BF)] * 2
            + [(group, BF)],
            [True] * 12 + [False] * 19 + [True],
            [vmem((streams, 4, count, width), BF), vmem(flat, BF), vmem(state_shape, F32)]
            + [vmem(head, BF)] * 4
            + [vmem(raw, F32)] * 4
            + [vmem(cut, BF)] * 3
            + scan_buffers(state_shape, slim)
            + [
                vmem((4, 2) + block.shape, BF),
                vmem(raw, F32),
                vmem((flat[0], hd), BF),
                vmem((flat[0], hd), BF),
                vmem(mixed_shape, BF),
                vmem(tokens.shape, F32),
                vmem(tokens.shape, BF),
                vmem((8, width), F32),
                vmem(plane, BF),
                vmem(ffn_shape, BF),
            ]
            + rows_buffers(mixed_shape),
            150,
            50,
            mb=63,
        )
        pack, lines, low_rank, logits, keep, true_keep, written = outs[:7]
        survive, slots_in, slots_end, scores, share = outs[7:12]
        rows, normed, reading, branch, self.hidden_rows = outs[12:17]
        self.down, self.gate, self.up = outs[26:29]
        self.cot, self.ffn_in, self.grad_product = outs[29:32]
        own = lax.dynamic_slice_in_dim(lines, self.head * 8, 8, 0)[:, :tall]
        gains = self.mixer_unorder(jnp.swapaxes(pack[:, rank : rank + 2], 0, 1)).astype(F32)
        return Mixer(
            reading=reading,
            scores=scores,
            share=share,
            branch=branch,
            rows=rows.reshape(streams, length, width),
            normed=normed,
            low=pack[:, :rank],
            low_rank=low_rank[..., :rank],
            rank=own[..., :rank].reshape(slots, rank).astype(F32),
            logits=logits,
            keep=keep,
            true_keep=true_keep,
            written=written,
            survive=survive[..., 0],
            slots_in=slots_in,
            slots_end=slots_end,
            weights=list(outs[17:21]),
            raw=list(outs[21:25]),
            output=outs[25].reshape(8 * block.shape[0], width),
            out_gain=lines[:, tall, : out_gain.shape[0]].reshape(-1).astype(F32),
            ffn_gain=gains[1],
            attn_gain=gains[0],
        )

    def feed_forward(self, tokens, gain, cotangent):
        streams, count, width = tokens.shape
        plane = (2, 2, 4, count, width)
        half = plane[1:]
        ffn = self.down.shape
        cols = ffn[-1]
        many = 4 * count
        group = (2, 2, many, cols)
        z_line = [(z, y) for z in (3, 1, 2, 0) for y in range(2)]
        side = ffn[2]

        def work(place, wire, given, outs, scratch):
            hidden, gain, cot, rows_in, grad_in, gate_in, up_in = given
            grad_hidden, gain_sum, act, rows_out, gate_out, up_out = outs
            ffn_in, turned, part, up_grad, gate, up, grad_gate, grad_up, gate_grad = scratch[:9]
            plane_bufs, gate_bufs = scratch[9:14], scratch[14:]
            loaded = Flags()
            for c in range(2):
                for h in range(2):
                    loaded.raised((c, h), [wire.keep(rows_in.at[c, h], ffn_in.at[c, h])])
                    if (c, h) == (0, 0):
                        loaded.raised("gate", [wire.keep(gate_in, gate)])
                        loaded.raised("up", [wire.keep(up_in, up)])
                        loaded.raised("grad", [wire.keep(grad_in, grad_up)])
            gain_sum[...] = jnp.zeros_like(gain_sum)

            made, gate_made = Flags(), Flags()

            def rows_of(ref, c, h):
                return ref[c, h].reshape(many, width)

            def weight(ref):
                return ref[...].reshape(width, cols)

            def compute():
                groups = [(c, h) for c in range(2) for h in range(2)]
                for c, h in groups:
                    yield loaded.wait((c, h), "gate", "up", "grad")
                    x = rows_of(ffn_in, c, h)
                    gate_pre = mm(x, weight(gate), NN)
                    up_pre = mm(x, weight(up), NN)
                    grad = grad_up[c, h].astype(F32)
                    sig = jax.nn.sigmoid(gate_pre)
                    act[c, h] = (gate_pre * sig * up_pre).astype(BF)
                    slope = sig * (1.0 + gate_pre * (1.0 - sig))
                    grad_gate[c, h] = (grad * up_pre * slope).astype(BF)
                    grad_up[c, h] = (grad * gate_pre * sig).astype(BF)
                    wire.spend(4.0)
                for c in (1, 0):
                    for h in range(2):
                        yield []
                        total = mm(grad_gate[c, h], weight(gate), NT)
                        total = total + mm(grad_up[c, h], weight(up), NT)
                        part[c, h] = total.astype(BF).reshape(half[1:])
                        wire.spend(3.0)
                        made.raised((("near", "far")[c], h))

                def columns(key):
                    at = (key[0] * 2 + key[1]) * side
                    return ffn_in[:, :, :, :, at : at + side].reshape(4 * many, side)

                def put(key, value):
                    gate_grad[key[0], key[1]] = value.astype(BF)

                def gate_rows():
                    return grad_gate[...].reshape(4 * many, cols)

                yield from weight_tiles(wire, columns, z_line, gate_rows, put, gate_made)

                def put_up(key, value):
                    up_grad[key[0], key[1]] = value.astype(BF)
                    wire.keep(up_grad.at[key[0], key[1]], up_out.at[key[0], key[1]])

                def up_rows_all():
                    return grad_up[...].reshape(4 * many, cols)

                yield from weight_tiles(wire, columns, z_line, up_rows_all, put_up)

            def finish_grad(stream, rows, load):
                part = z_parts(place, load, width)
                held = hidden[stream, rows]
                scale = inverse_rms(held)
                gain_sum[...] += jnp.sum(part * held * scale, axis=0, keepdims=True)
                total = cot[stream, rows].astype(F32) + norm_back(held, scale, gain[...], part)
                grad_hidden[stream, rows] = total
                turned[stream, rows] = total.astype(BF)

            def back_rows():
                yield from plane_fold(
                    place, wire, part.at[0], part.at[1], plane_bufs, finish_grad, made
                )
                yield from rows_gather(place, wire, turned, rows_out)

            wire.run(
                back_rows(),
                ffn_fold(place, wire, gate_grad, gate_bufs, gate_out, gate_made),
                compute(),
            )

        vmem = pltpu.VMEM
        outs = comm_call(
            work,
            3,
            (CORE, X, Y, NEAR, FAR),
            [self.hidden_rows, gain[None], cotangent, self.ffn_in, self.grad_product]
            + [self.gate, self.up],
            [True] * 3 + [False] * 4,
            [
                ((streams, count, width), F32),
                ((1, width), F32),
                (group, BF),
                ((streams, 4, count, width), BF),
                (ffn[1:], BF),
                (ffn, BF),
            ],
            [True] * 3 + [False] * 3,
            [
                vmem(plane, BF),
                vmem((streams, count, width), BF),
                vmem(plane, BF),
                vmem(ffn, BF),
                vmem(ffn, BF),
                vmem(ffn, BF),
                vmem(group, BF),
                vmem(group, BF),
                vmem(ffn, BF),
            ]
            + plane_buffers(half)
            + ffn_buffers(ffn),
            60,
            24,
            mb=63,
        )
        grad_hidden, gain_grad, self.act = outs[:3]
        rows, self.gate_grad, self.up_part = outs[3:]
        rows = rows.reshape(streams, 4 * count, width)
        return grad_hidden.reshape(streams * count, width), gain_grad[0], rows

    def own_streams(self, values):
        return values

    def mixer_order(self, values):
        lead, width = values.shape[:-1], values.shape[-1]
        parts = jnp.swapaxes(values.reshape(lead + (4, 2, width // 8)), -3, -2)
        return z_relative(parts, self.at.z, len(lead) + 1).reshape(lead + (width,))

    def mixer_unorder(self, values):
        lead, width = values.shape[:-1], values.shape[-1]
        parts = z_relative(values.reshape(lead + (2, 4, width // 8)), self.at.z, len(lead) + 1)
        return jnp.swapaxes(parts, -3, -2).reshape(lead + (width,))

    def ffn_order(self, values):
        return z_relative(values, self.at.z, values.ndim - 1)

    def mixer_back(self, mixer, grad_mixed):
        reading, scores, share, branch_out = mixer.reading, mixer.scores, mixer.share, mixer.branch
        streams, length, hd = reading.shape
        rows, width = grad_mixed.shape
        slots = scores.shape[1]
        state_shape, slim = (streams, slots, 2 * hd), (streams, slots, 128)
        ffn = self.up_part.shape
        line = (4, 2, hd // 8, width)
        head = (2, 4, width // 8, hd)
        own = (head[2] // 4, width)
        raw, gate_shape = (streams, length, hd), (streams, slots, length)
        survive = jnp.broadcast_to(mixer.survive[..., None], slim)
        key_raw, value_raw, query_raw, gate_raw = mixer.raw

        def work(place, wire, given, outs, scratch):
            grad_mixed, output_w, survive, out_gain = given[:4]
            after, gain_sum, grad_query, grad_gate, grad_k, grad_v, back, own_flow = outs[:8]
            up_out, output_out, query_out, gate_out = outs[8:]
            loads = {
                key: (source, target)
                for key, source, target in zip(
                    ("reading", "gate", "query", "key", "value", "keep", "written")
                    + ("scores", "share", "slots", "branch", "normed", "up"),
                    given[4:],
                    scratch,
                )
            }
            here, up_made, lines_made = Flags(), Flags(), Flags()
            heads_made = [Flags(), Flags()]

            def load(*keys):
                for key in keys:
                    here.raised(key, [wire.keep(*loads[key])])

            kept = {key: pair[1] for key, pair in loads.items()}
            sent, got, grad_read, direct, output_part, query_part, gate_part = scratch[13:20]
            scan, up_bufs = scratch[20:24], scratch[24:27]
            lines, query_bufs, gate_bufs = scratch[27:31], scratch[31:35], scratch[35:39]
            load("up", "branch", "reading", "gate", "normed", "query", "key", "value")
            load("keep", "written", "scores", "share", "slots")
            gain_sum[...] = jnp.zeros_like(gain_sum)

            def returned():
                yield here.wait("sent")
                yield from heads_return(place, wire, sent, got)
                here.raised("got")

            def scanned():
                yield here.wait("direct")
                yield from pieces_scan(place, wire, True, survive, direct, after, scan)

            def up_rows():
                yield here.wait("up")
                yield from ffn_fold(place, wire, kept["up"], up_bufs, up_out)

            def gated(s):
                def chunk(part):
                    at = pl.ds(pl.multiple_of(s * length + part.start, 16), part.size)
                    values, opened = kept["reading"][s, part], kept["gate"][s, part]
                    grad = got[at].astype(F32)
                    scale = inverse_rms(values)
                    normed = values * scale * out_gain[...]
                    grad_gate[s, part] = (grad * normed * silu_slope(opened)).astype(BF)
                    grad = grad * silu(opened)
                    gain_sum[...] += jnp.sum(grad * values * scale, axis=0, keepdims=True)
                    grad_read[s, part] = norm_back(values, scale, out_gain[...], grad)

                row_loop(length, 32, chunk)

            def streams_back(s, carry):
                results = piece_back(
                    *[kept[key][s] for key in ("query", "key", "value", "keep", "written")],
                    *[kept[key][s] for key in ("slots", "scores", "share")],
                    grad_read[s],
                )
                targets = (grad_query, grad_k, grad_v, direct, back, own_flow)
                for target, result in zip(targets, results):
                    target[s] = result.astype(target.dtype)
                return carry

            def compute():
                half = rows // 2
                for at in (0, half):
                    part = mm(grad_mixed[at : at + half], output_w[...], NT)
                    sent[at : at + half] = part.astype(BF)
                wire.spend(3.0)
                here.raised("sent")
                yield here.wait("branch")
                block = hd // 4
                for m in (3, 1, 2, 0):
                    yield []
                    cols = kept["branch"][:, m * block : (m + 1) * block]
                    total = mm(cols, grad_mixed[...], TN)
                    output_part[m] = total.astype(BF).reshape(line[1:])
                    wire.spend(1.2)
                    lines_made.raised(m)
                yield here.wait("got", "reading", "gate")
                for s in range(streams):
                    gated(s)
                wire.spend(2.0)
                yield here.wait("normed")
                yield from head_tiles(
                    wire,
                    kept["normed"],
                    lambda: grad_gate[...].reshape(rows, hd),
                    gate_part,
                    heads_made[1],
                )
                yield here.wait("query", "key", "value", "keep", "written", "scores", "share", "slots")
                lax.fori_loop(0, streams, streams_back, 0)
                wire.spend(13.0)
                here.raised("direct")
                yield from head_tiles(
                    wire,
                    kept["normed"],
                    lambda: grad_query[...].reshape(rows, hd),
                    query_part,
                    heads_made[0],
                )

            wire.run(
                returned(),
                scanned(),
                up_rows(),
                output_fold(place, wire, output_part, lines, output_out, lines_made),
                head_fold(place, wire, gate_part, gate_bufs, gate_out, heads_made[1]),
                head_fold(place, wire, query_part, query_bufs, query_out, heads_made[0]),
                compute(),
            )

        vmem = pltpu.VMEM
        later = [
            reading,
            gate_raw,
            query_raw,
            key_raw,
            value_raw,
            mixer.keep,
            mixer.written,
            scores,
            share,
            mixer.slots_in,
            branch_out,
            mixer.normed,
            self.up_part,
        ]
        outs = comm_call(
            work,
            7,
            (CORE, X, X | CORE, Y, NEAR, FAR),
            [grad_mixed, mixer.output, survive, mixer.out_gain[None]] + later,
            [True] * 4 + [False] * len(later),
            [
                (state_shape, F32),
                ((1, hd), F32),
                (raw, BF),
                (raw, BF),
                (raw, F32),
                (raw, F32),
                (gate_shape, F32),
                (gate_shape, F32),
                (ffn[1:], BF),
                (line[2:], BF),
                (own, BF),
                (own, BF),
            ],
            [True] * 8 + [False] * 4,
            [vmem(a.shape, a.dtype) for a in later]
            + [
                vmem((rows, hd), BF),
                vmem((rows, hd), BF),
                vmem(raw, F32),
                vmem(state_shape, F32),
                vmem(line, BF),
                vmem(head, BF),
                vmem(head, BF),
            ]
            + scan_buffers(state_shape, slim)
            + ffn_buffers(ffn)
            + line_buffers(line[2], line[3])
            + line_buffers(head[2], head[3])
            + line_buffers(head[2], head[3]),
            60,
            30,
            mb=62,
        )
        self.up_grad, output_sum, query_sum, gate_sum = outs[8:]
        self.output_sum = turn_bits(output_sum, True)
        self.head_sums = [query_sum, gate_sum]
        return outs[:8]

    def end(self, mixer, grads, normed_part, packed):
        streams, positions, width = normed_part.shape
        count = positions // 4
        part_shape = (streams, 2, 2, count, width)
        hd = grads[0].shape[-1]
        rows = streams * positions
        head = (2, 4, width // 8, hd)
        own = (head[2] // 4, width)
        length = -(-packed.shape[1] // 2048) * 16
        packed = jnp.pad(packed, ((0, 0), (0, length * 128 - packed.shape[1])))
        plane, group, ffn = self.cot.shape, self.act.shape, self.down.shape
        half, cols, side = plane[1:], ffn[-1], ffn[2]
        many = half[1] * half[2]
        z_line = [(z, y) for z in (3, 1, 2, 0) for y in range(2)]

        def work(place, wire, given, outs, scratch):
            normed_part, packed, values = given[:3]
            normed_out, small_out, result, key_out, value_out, down_out = outs
            loads = dict(
                zip(("key", "value", "normed", "act", "cot", "down"), zip(given[3:], scratch))
            )
            kept = {key: pair[1] for key, pair in loads.items()}
            down_grad, parts = scratch[6], scratch[7:9]
            small, sums = scratch[9:11], scratch[11:14]
            lines = [scratch[14:18], scratch[18:22]]
            plane_bufs, fold_bufs = scratch[22:27], scratch[27:]
            part = kept["cot"]
            here, made, down_made = Flags(), Flags(), Flags()
            heads_made = [Flags(), Flags()]
            for key in ("cot", "act", "key", "normed", "value", "down"):
                here.raised(key, [wire.keep(*loads[key])])

            def finish(stream, rows, total):
                normed_out[stream, rows] = total

            def finish_result(stream, rows, load):
                total = values[stream, rows] + z_parts(place, load, width)
                result[stream, rows] = total.astype(BF)

            def compute():
                yield here.wait("cot", "act")

                def columns(key):
                    at = (key[0] * 2 + key[1]) * side
                    return kept["cot"][:, :, :, :, at : at + side].reshape(4 * many, side)

                def put(key, value):
                    down_grad[key[0], key[1]] = value.astype(BF)

                def act_rows():
                    return kept["act"][...].reshape(4 * many, cols)

                yield from weight_tiles(wire, columns, z_line, act_rows, put, down_made)
                yield here.wait("normed", "key", "value")
                for index, key in enumerate(("key", "value")):
                    grad = kept[key]
                    yield from head_tiles(
                        wire,
                        kept["normed"],
                        lambda: grad[...].reshape(rows, hd),
                        parts[index],
                        heads_made[index],
                    )
                yield here.wait("down")
                for c in (1, 0):
                    for h in range(2):
                        total = mm(kept["act"][c, h], kept["down"][...].reshape(width, cols), NT)
                        part[c, h] = total.astype(BF).reshape(half[1:])
                        wire.spend(2.0)
                        made.raised((("near", "far")[c], h))
                        yield []

            wire.run(
                rows_fold(place, wire, normed_part, *sums, finish),
                small_fold(place, wire, packed, small, small_out),
                ffn_fold(place, wire, down_grad, fold_bufs, down_out, down_made),
                head_fold(place, wire, parts[0], lines[0], key_out, heads_made[0]),
                head_fold(place, wire, parts[1], lines[1], value_out, heads_made[1]),
                plane_fold(place, wire, part.at[0], part.at[1], plane_bufs, finish_result, made),
                compute(),
            )

        vmem = pltpu.VMEM
        later = list(grads) + [mixer.normed, self.act, self.cot, self.down]
        normed, small, result, key_sum, value_sum, self.down_grad = comm_call(
            work,
            8,
            (CORE, X, X | CORE, Y, NEAR, FAR),
            [normed_part.reshape(part_shape), packed.reshape(32, length, 128), self.hidden_rows]
            + later,
            [True] * 3 + [False] * len(later),
            [
                ((streams, count, width), F32),
                ((1, length, 128), F32),
                (self.hidden_rows.shape, BF),
                (own, BF),
                (own, BF),
                (ffn[1:], BF),
            ],
            [True] * 3 + [False] * 3,
            [vmem(a.shape, a.dtype) for a in later]
            + [vmem(ffn, BF), vmem(head, BF), vmem(head, BF)]
            + [vmem((32, length, 128), F32)] * 2
            + rows_buffers(part_shape)
            + line_buffers(head[2], head[3])
            + line_buffers(head[2], head[3])
            + plane_buffers(half)
            + ffn_buffers(ffn),
            80,
            16,
            mb=62,
        )

        def both(parts):
            return jnp.concatenate([parts[0], parts[1]], axis=1).astype(F32)

        heads = [key_sum, value_sum] + self.head_sums + [self.output_sum]
        heads = [h.astype(F32) for h in heads]
        ffn_grads = [both(g) for g in (self.gate_grad, self.up_grad, self.down_grad)]
        return heads, ffn_grads, normed, small.reshape(-1), result


def on_device(
    tokens,
    seq_cuts,
    w_query,
    w_key,
    w_value,
    w_gate_out,
    w_output,
    w_low,
    w_rank,
    gate_bias,
    attn_gain,
    out_gain,
    ffn_gain,
    w_gate,
    w_up,
    w_down,
    cotangent,
):
    seq_count, tp_count = lax.axis_size("seq"), lax.axis_size("tp")
    devices = seq_count * tp_count
    move = BitMoves() if (seq_count, tp_count) == (8, 4) else PlainMoves()
    streams, local_len, width = tokens.shape
    small = (w_low, w_rank, gate_bias, attn_gain, out_gain, ffn_gain)
    mixer = move.start(
        tokens,
        seq_cuts,
        (w_key, w_value, w_query, w_gate_out),
        w_output,
        small,
        (w_down, w_gate, w_up),
        cotangent,
    )
    key_rows, value_rows = mixer.raw[:2]
    key_w, value_w, query_w, gate_w = mixer.weights
    keep, true_keep, written = mixer.keep, mixer.true_keep, mixer.written
    slots_end = mixer.slots_end
    ffn_vec, attn_vec = mixer.ffn_gain, mixer.attn_gain
    normed, low_rank = mixer.normed, mixer.low_rank
    held, piece_len, hd = key_rows.shape
    slots, rank = keep.shape[1], low_rank.shape[-1]
    flat = held * piece_len
    inputs = mixer.rows.reshape(flat, width).astype(F32)
    attn_scale = inverse_rms(inputs)
    gflop = 1000 * 1000 * 1000
    own_tokens = tokens.astype(F32)

    grad_hidden, grad_ffn_gain, grad_mixed = move.feed_forward(tokens, ffn_vec, cotangent)

    after, grad_out_gain, grad_query, grad_gate, grad_k, grad_v, back, own = move.mixer_back(
        mixer, grad_mixed.reshape(flat, width)
    )
    grad_out_gain = grad_out_gain[0]
    grad_key, grad_value, grad_log = per_stream(
        piece_after,
        [
            key_rows,
            value_rows,
            keep,
            true_keep,
            written,
            grad_k,
            grad_v,
            back,
            own,
            after,
            slots_end,
        ],
        [((piece_len, hd), BF), ((piece_len, hd), BF), ((slots, piece_len), F32)],
        gflop,
    )
    grad_f = grad_log * jax.nn.sigmoid(-mixer.logits) / GATE_SCALE
    grad_bias = jnp.sum(grad_f, axis=(0, 2))
    highest = lax.Precision.HIGHEST
    grad_rank = jnp.einsum("smt,str->mr", grad_f, low_rank, precision=highest)
    grad_low_rank = jnp.einsum("smt,mr->str", grad_f, mixer.rank, precision=highest)
    grad_low_rank = grad_low_rank.reshape(flat, rank)
    grads = [g.reshape(flat, hd) for g in (grad_query, grad_key, grad_value, grad_gate)]
    grad_normed = sum(
        product(g, w, NT) for g, w in zip(grads, (query_w, key_w, value_w, gate_w))
    )
    grad_normed = grad_normed + product(grad_low_rank, mixer.low.astype(F32), NT)
    attn_part = jnp.sum(grad_normed * inputs * attn_scale, axis=0)
    grad_low = product(grad_low_rank, normed.astype(F32), TN)
    grad_low = jnp.swapaxes(move.mixer_unorder(grad_low), 0, 1)

    def placed(part):
        entire = jnp.zeros((part.shape[0] * H,) + part.shape[1:], F32)
        return lax.dynamic_update_slice_in_dim(entire, part, move.head * part.shape[0], 0)

    sums = (
        grad_low,
        placed(grad_rank),
        placed(grad_bias),
        move.mixer_unorder(attn_part),
        grad_out_gain,
        grad_ffn_gain,
    )
    packed = jnp.concatenate([a.reshape(devices, -1) for a in sums], axis=1)
    heads, ffn_grads, grad_normed, own_sums, result = move.end(
        mixer,
        [grad_key, grad_value],
        grad_normed.astype(BF).reshape(held, piece_len, width),
        packed,
    )
    grad_w_key, grad_w_value, grad_w_query, grad_w_gate_out, grad_w_output = heads
    grad_normed = move.mixer_unorder(grad_normed)
    own_scale = inverse_rms(own_tokens)
    grad_tokens = grad_hidden.reshape(tokens.shape)
    grad_tokens = grad_tokens + norm_back(own_tokens, own_scale, attn_vec, grad_normed)
    small_grads, taken = [], 0
    for a in small:
        small_grads.append(own_sums[taken : taken + a.size].reshape(a.shape))
        taken += a.size
    return (
        (result.reshape(tokens.shape), grad_tokens)
        + (grad_w_query, grad_w_key, grad_w_value, grad_w_gate_out, grad_w_output)
        + tuple(small_grads)
        + tuple(ffn_grads)
    )


def solution(mesh):
    both, row_split, line = ("seq", "tp"), P(("seq", "tp"), None), P(("seq", "tp"))
    tokens_at, ffn_at = P(None, both, None), P("seq", "tp")
    params = (row_split,) * 7 + (line,) * 4 + (ffn_at,) * 3
    return jax.shard_map(
        on_device,
        mesh=mesh,
        in_specs=(tokens_at, P()) + params + (tokens_at,),
        out_specs=(tokens_at, tokens_at) + params,
        check_vma=False,
    )
```

```python
import dataclasses
import math

import jax
import jax.numpy as jnp
from jax import lax
from jax.experimental import pallas as pl
from jax.experimental.pallas import tpu as pltpu
from jax.sharding import PartitionSpec as P

SEQ, TP = "seq", "tp"


class Key:
    x, y, side, middle, core, remote = range(100, 106)
    local, far, near, done, rows, lines = range(106, 112)
    raw, branch, traded, mixed, trade, pack = range(112, 118)
    state, slots, gate, up, cot, down = range(118, 124)
    block, reading, query, key, value, keep = range(124, 130)
    written, scores, share, normed, query_w, gate_w = range(130, 136)
    sent, got, direct, grad_k, grad_v, part = range(136, 142)
    key_w, value_w, hidden_grad, down_2, normed_part, sheet = range(142, 148)


H = 4
GATE_SCALE = 8.0
EPSILON = 1e-05
BF = jnp.bfloat16
F32 = jnp.float32
CHUNK = 128
SUB = 16
HALVES = (16, 32, 64)


def mm(left, right, dims):
    return lax.dot_general(
        left.astype(BF), right.astype(BF), (dims, ((), ())), preferred_element_type=F32
    )


def mm_fine(left, right, dims):
    left_hi, right_hi = left.astype(BF), right.astype(BF)
    left_lo = (left - left_hi.astype(F32)).astype(BF)
    right_lo = (right - right_hi.astype(F32)).astype(BF)

    def part(a, b):
        return lax.dot_general(a, b, (dims, ((), ())), preferred_element_type=F32)

    return part(left_hi, right_hi) + (part(left_hi, right_lo) + part(left_lo, right_hi))


NN = ((1,), (0,))
NT = ((1,), (1,))
TN = ((0,), (0,))


def turn(values, amount):
    return pltpu.roll(values, amount % values.shape[1], 1)


def column(shape):
    return lax.broadcasted_iota(jnp.int32, shape, 1)


def row(shape):
    return lax.broadcasted_iota(jnp.int32, shape, 0)


def ahead_product(keep, size):
    place = column(keep.shape) & (size - 1)
    total, step = keep, 1
    while step < size:
        total = total * jnp.where(place >= step, turn(total, step), 1.0)
        step *= 2
    return total


def behind_product(keep, size):
    place = column(keep.shape) & (size - 1)
    total = jnp.where(place == size - 1, 1.0, turn(keep, -1))
    step = 1
    while step < size:
        total = total * jnp.where(place < size - step, turn(total, -step), 1.0)
        step *= 2
    return total


def chunks_of(values):
    return [values[:, at : at + CHUNK] for at in range(0, values.shape[1], CHUNK)]


def rows_of(values):
    return [values[at : at + CHUNK] for at in range(0, values.shape[0], CHUNK)]


class Decays:
    def __init__(self, keep):
        self.keep = chunks_of(keep)
        self.count = len(self.keep)
        self.ahead = [ahead_product(k, CHUNK) for k in self.keep]
        self.behind = [behind_product(k, CHUNK) for k in self.keep]
        self.total = [a[:, CHUNK - 1 :] for a in self.ahead]

    def levels(self):
        self.ahead_in = [{h: ahead_product(k, h) for h in HALVES} for k in self.keep]
        self.behind_in = [{h: behind_product(k, h) for h in HALVES} for k in self.keep]
        inside = (column(self.keep[0].shape) & (SUB - 1)) != 0
        self.short = [jnp.where(inside, k, 0.0) for k in self.keep]

    def from_start(self, c):
        out = self.ahead[c]
        for earlier in range(c):
            out = out * self.total[earlier]
        return out

    def to_end(self, c):
        out = self.behind[c]
        for later in range(c + 1, self.count):
            out = out * self.total[later]
        return out

    def to_chunk(self, c):
        parts = []
        for earlier in range(c):
            out = self.behind[earlier]
            for between in range(earlier + 1, c):
                out = out * self.total[between]
            parts.append(out)
        return parts

    def survive(self):
        out = self.total[0]
        for t in self.total[1:]:
            out = out * t
        return out


def level_mask(half):
    shape = (CHUNK, CHUNK)
    source, target = row(shape) // half, column(shape) // half
    return ((source & 1) == 0) & (target == source + 1)


def diagonals(square):
    shape = (SUB, CHUNK)
    group = column(shape) // SUB
    out = jnp.zeros(shape, F32)
    for b in range(CHUNK // SUB):
        out = out + jnp.where(group == b, square[b * SUB : (b + 1) * SUB], 0.0)
    return out


def at_lag(compact, lag):
    shape = (SUB, CHUNK)
    hit = row(shape) == (column(shape) & (SUB - 1)) - lag
    return jnp.sum(jnp.where(hit, compact, 0.0), axis=0, keepdims=True)


def undiagonal(lagged):
    shape = (SUB, CHUNK)
    place = (column(shape) & (SUB - 1)) - row(shape)
    compact = jnp.zeros(shape, F32)
    for lag, values in enumerate(lagged):
        compact = jnp.where(place == lag, values, compact)
    group = column(shape) // SUB
    return jnp.concatenate(
        [jnp.where(group == b, compact, 0.0) for b in range(CHUNK // SUB)], axis=0
    )


def read_slots(decays, written, c, affinity, entering, dot):
    near = affinity[c * CHUNK :]
    out = decays.from_start(c) * entering
    if c > 0:
        far = jnp.concatenate(
            [b * w for b, w in zip(decays.to_chunk(c), written[:c])], axis=1
        )
        out = out + decays.ahead[c] * dot(far, affinity[: c * CHUNK], NN)
    for h in HALVES:
        part = dot(decays.behind_in[c][h] * written[c], jnp.where(level_mask(h), near, 0.0), NN)
        out = out + decays.ahead_in[c][h] * part
    compact = diagonals(near)
    weight = written[c]
    for lag in range(SUB):
        out = out + weight * at_lag(compact, lag)
        if lag + 1 < SUB:
            weight = decays.short[c] * turn(weight, 1)
    return out


def mix_sources(decays, written, c, shares):
    lagged = [[] for _ in shares]
    weight = written[c]
    for lag in range(SUB):
        for place, share in enumerate(shares):
            lagged[place].append(jnp.sum(weight * share, axis=0, keepdims=True))
        if lag + 1 < SUB:
            weight = decays.short[c] * turn(weight, 1)
    outs = []
    for place, share in enumerate(shares):
        near = undiagonal(lagged[place])
        for h in HALVES:
            part = mm(decays.behind_in[c][h] * written[c], decays.ahead_in[c][h] * share, TN)
            near = near + jnp.where(level_mask(h), part, 0.0)
        if c > 0:
            far = jnp.concatenate(
                [b * w for b, w in zip(decays.to_chunk(c), written[:c])], axis=1
            )
            near = jnp.concatenate([mm(far, decays.ahead[c] * share, TN), near], axis=0)
        outs.append(near)
    return outs


def gather_back(decays, c, shares, affinities):
    outs = []
    if c > 0:
        pulled = sum(
            mm_fine(decays.ahead[c] * s, a[: c * CHUNK], NT) for s, a in zip(shares, affinities)
        )
        outs = [b * p for b, p in zip(decays.to_chunk(c), chunks_of(pulled))]
    nears = [a[c * CHUNK :] for a in affinities]
    own = 0.0
    for h in HALVES:
        mask = level_mask(h)
        pulled = sum(
            mm_fine(decays.ahead_in[c][h] * s, jnp.where(mask, a, 0.0), NT)
            for s, a in zip(shares, nears)
        )
        own = own + decays.behind_in[c][h] * pulled
    compacts = [diagonals(a) for a in nears]
    held = 0.0
    for lag in range(SUB - 1, -1, -1):
        if lag < SUB - 1:
            held = turn(decays.short[c] * held, -1)
        for s, a in zip(shares, compacts):
            held = held + s * at_lag(a, lag)
    outs.append(own + held)
    return outs


def silu(x):
    return x * jax.nn.sigmoid(x)


def silu_slope(x):
    sig = jax.nn.sigmoid(x)
    return sig * (1.0 + x * (1.0 - sig))


def gates(logits):
    small = jnp.exp(-jnp.abs(logits))
    ratio = small / (2.0 + small)
    square = ratio * ratio
    series = jnp.full_like(square, 1.0 / 17.0)
    for odd in (15, 13, 11, 9, 7, 5, 3, 1):
        series = series * square + 1.0 / odd
    log_keep = (jnp.minimum(logits, 0.0) - 2.0 * ratio * series) / GATE_SCALE
    keep = jnp.exp(log_keep)
    near = jnp.ones_like(log_keep)
    for order in (9, 8, 7, 6, 5, 4, 3, 2):
        near = 1.0 + log_keep / order * near
    return keep, jnp.where(log_keep > -0.5, -log_keep * near, 1.0 - keep)


def piece_state(key_raw, value_raw, keep, written):
    decays = Decays(keep)
    left = jnp.concatenate(
        [decays.to_end(c) * w for c, w in enumerate(chunks_of(written))], axis=1
    )
    keys, values = mm_fine(left, silu(key_raw), NN), mm_fine(left, silu(value_raw), NN)
    state = jnp.concatenate([keys, values], axis=1)
    return state, decays.survive()


def piece_read(query_raw, key_raw, value_raw, keep, written, slots_in):
    width = query_raw.shape[1]
    query, keys, values = silu(query_raw) * width**-0.5, silu(key_raw), silu(value_raw)
    slot_keys, slot_values = slots_in[:, :width], slots_in[:, width:]
    decays = Decays(keep)
    decays.levels()
    writes = chunks_of(written)
    entering = mm_fine(slot_keys, query, NT)
    readings, scores_all, shares = [], [], []
    for c in range(decays.count):
        last = (c + 1) * CHUNK
        affinity = mm_fine(keys[:last], query[c * CHUNK : last], NT)
        scores = read_slots(
            decays, writes, c, affinity, chunks_of(entering)[c], mm_fine
        )
        spread = jnp.exp(scores - jnp.max(scores, axis=0, keepdims=True))
        share = spread / jnp.sum(spread, axis=0, keepdims=True)
        (mixing,) = mix_sources(decays, writes, c, [share])
        reading = mm(mixing, values[:last], TN)
        reading = reading + mm(decays.from_start(c) * share, slot_values, TN)
        readings.append(reading)
        scores_all.append(scores)
        shares.append(share)
    return (
        jnp.concatenate(readings, axis=0),
        jnp.concatenate(scores_all, axis=1),
        jnp.concatenate(shares, axis=1),
    )


def add_chunks(total, extra):
    return [t + e for t, e in zip(total, extra)] + total[len(extra) :]


def piece_back(query_raw, key_raw, value_raw, keep, written, slots_in, scores, share, grad_read):
    width = query_raw.shape[1]
    query, keys, values = silu(query_raw) * width**-0.5, silu(key_raw), silu(value_raw)
    slot_keys, slot_values = slots_in[:, :width], slots_in[:, width:]
    decays = Decays(keep)
    decays.levels()
    writes = chunks_of(written)
    count = decays.count
    entering = chunks_of(mm_fine(slot_values, grad_read, NT))
    grad_q = []
    grad_k = [jnp.zeros((CHUNK, width), F32)] * count
    grad_v = [jnp.zeros((CHUNK, width), F32)] * count
    back = [jnp.zeros(writes[0].shape, F32)] * count
    direct_k, direct_v, own = 0.0, 0.0, []
    for c in range(count):
        last = (c + 1) * CHUNK
        here = slice(c * CHUNK, last)
        p = chunks_of(share)[c]
        affinity = mm_fine(keys[:last], query[here], NT)
        pull = mm_fine(values[:last], grad_read[here], NT)
        grad_p = read_slots(decays, writes, c, pull, entering[c], mm_fine)
        weighed = p * grad_p
        grad_s = weighed - p * jnp.sum(weighed, axis=0, keepdims=True)
        own.append(weighed + grad_s * chunks_of(scores)[c])
        mix_k, mix_v = mix_sources(decays, writes, c, [grad_s, p])
        from_start = decays.from_start(c)
        far_s, far_p = from_start * grad_s, from_start * p
        grad_q.append(mm(mix_k, keys[:last], TN) + mm(far_s, slot_keys, TN))
        grad_k = add_chunks(grad_k, rows_of(mm(mix_k, query[here], NN)))
        grad_v = add_chunks(grad_v, rows_of(mm(mix_v, grad_read[here], NN)))
        direct_k = direct_k + mm(far_s, query[here], NN)
        direct_v = direct_v + mm(far_p, grad_read[here], NN)
        back = add_chunks(back, gather_back(decays, c, [grad_s, p], [affinity, pull]))
    grad_query = jnp.concatenate(grad_q, axis=0) * width**-0.5 * silu_slope(query_raw)
    return (
        grad_query,
        jnp.concatenate(grad_k, axis=0),
        jnp.concatenate(grad_v, axis=0),
        jnp.concatenate([direct_k, direct_v], axis=1),
        jnp.concatenate(back, axis=1),
        jnp.concatenate(own, axis=1),
    )


def piece_after(
    key_raw, value_raw, keep, written, grad_k, grad_v, back, own, after, slots_end
):
    width = key_raw.shape[1]
    keys, values = silu(key_raw), silu(value_raw)
    decays = Decays(keep)
    writes = chunks_of(written)
    to_end = jnp.concatenate([decays.to_end(c) for c in range(decays.count)], axis=1)
    left = to_end * written
    grad_k = grad_k + mm(left, after[:, :width], TN)
    grad_v = grad_v + mm(left, after[:, width:], TN)
    pulled = mm_fine(after[:, :width], keys, NT)
    pulled = pulled + mm_fine(after[:, width:], values, NT)
    back = back + to_end * pulled
    flow = own - written * back
    held = jnp.sum(after * slots_end, axis=1, keepdims=True)
    parts = chunks_of(flow)
    outs = []
    for part in reversed(parts):
        place, total, step = column(part.shape), part, 1
        while step < CHUNK:
            total = total + jnp.where(place < CHUNK - step, turn(total, -step), 0.0)
            step *= 2
        outs.append(total + held)
        held = held + total[:, :1]
    grad_log = jnp.concatenate(outs[::-1], axis=1) - (1.0 - written) * back
    return grad_k * silu_slope(key_raw), grad_v * silu_slope(value_raw), grad_log


def tie(value, *after):
    if not after:
        return value

    def body(*refs):
        pass

    anywhere = pl.BlockSpec(memory_space=pl.ANY)
    return pl.pallas_call(
        body,
        in_specs=[anywhere] * (1 + len(after)),
        out_specs=anywhere,
        out_shape=jax.ShapeDtypeStruct(value.shape, value.dtype),
        input_output_aliases={0: 0},
        cost_estimate=pl.CostEstimate(flops=0, bytes_accessed=0, transcendentals=0),
    )(value, *after)


def per_stream(work, arrays, outs, flops):
    def body(*refs):
        results = work(*[ref[...] for ref in refs[: len(arrays)]])
        for ref, result in zip(refs[len(arrays) :], results):
            ref[...] = result.astype(ref.dtype)

    def whole(shape):
        return pl.BlockSpec((None,) + tuple(shape[1:]), lambda s: (s, 0, 0))

    streams = arrays[0].shape[0]
    outs = [jax.ShapeDtypeStruct((streams,) + shape, kind) for shape, kind in outs]
    return pl.pallas_call(
        body,
        grid=(streams,),
        in_specs=[whole(a.shape) for a in arrays],
        out_specs=[whole(o.shape) for o in outs],
        out_shape=outs,
        compiler_params=pltpu.CompilerParams(vmem_limit_bytes=40 * 1024 * 1024),
        cost_estimate=pl.CostEstimate(flops=flops, bytes_accessed=1 << 16, transcendentals=0),
    )(*arrays)


def inverse_rms(values):
    return lax.rsqrt(jnp.mean(values * values, axis=-1, keepdims=True) + EPSILON)


def norm_back(values, scale, gain, grad):
    pulled = gain * grad
    along = jnp.mean(values * pulled, axis=-1, keepdims=True)
    return scale * pulled - values * (scale * scale * scale) * along


def product(left, right, dims):
    return lax.dot_general(left, right, (dims, ((), ())), preferred_element_type=F32)


def chain(earlier, later):
    return (earlier[0] * later[0], later[0][..., None] * earlier[1] + later[1])


CORE, X, Y, NEAR, FAR = 1, 2, 4, 8, 16


class Place:
    def __init__(self):
        self.seq, self.tp = lax.axis_index(SEQ), lax.axis_index(TP)
        self.core, self.x = self.tp % 2, self.tp // 2
        self.y, self.z = self.seq % 2, self.seq // 2
        self.near, self.far = self.z % 2, self.z // 2
        self.flat = self.seq * 4 + self.tp

    def partner(self, mask):
        seq, tp = self.seq, self.tp
        if mask & CORE:
            tp = tp + 1 - 2 * self.core
        if mask & X:
            tp = tp + 2 - 4 * self.x
        if mask & Y:
            seq = seq + 1 - 2 * self.y
        if mask & NEAR:
            seq = seq + 2 - 4 * self.near
        if mask & FAR:
            seq = seq + 4 - 8 * self.far
        return seq, tp

    def z_turn(self, index):
        low, high = index % 2, index // 2
        low = low + self.near - 2 * low * self.near
        high = high + self.far - 2 * high * self.far
        return 2 * high + low


class Wire:
    def __init__(self, place, sends, receives, locals_, pace):
        latency, link, beside, self.AHEAD = pace
        self.LATENCY, self.LINK, self.BESIDE = latency, 2e-3 / link, 1e-3 / beside
        self.place, self.sends, self.receives, self.locals = place, sends, receives, locals_
        self.remote, self.near_by, self.seen = [], [], set()
        self.now, self.due, self.free, self.rank = 0.0, {}, {}, 0
        self.queues = {Key.x: [], Key.y: [], Key.side: [], Key.middle: []}

    def greet(self, masks):
        barrier = pltpu.get_barrier_semaphore()
        for mask in masks:
            pl.semaphore_signal(
                barrier,
                inc=1,
                device_id=self.place.partner(mask),
                device_id_type=pl.DeviceIdType.MESH,
            )
        pl.semaphore_wait(barrier, len(masks))

    def spend(self, time):
        self.now += time

    def issue(self, at):
        source, target, mask = self.remote[at]
        copy = pltpu.make_async_remote_copy(
            src_ref=source,
            dst_ref=target,
            send_sem=self.sends.at[at],
            recv_sem=self.receives.at[at],
            device_id=self.place.partner(mask),
            device_id_type=pl.DeviceIdType.MESH,
        )
        copy.start()
        self.remote[at] = copy
        size = math.prod(source.shape) * jnp.dtype(source.dtype).itemsize
        if mask == CORE:
            uses = ((Key.core, size * self.BESIDE),)
        elif mask & X:
            uses = ((Key.x, size * self.LINK),)
        elif mask == Y:
            uses = ((Key.y, size * self.LINK),)
        elif mask == NEAR:
            uses = ((Key.side, size * self.LINK),)
        else:
            uses = ((Key.side, size * self.LINK), (Key.middle, 2 * size * self.LINK))
        end = 0.0
        for link, time in uses:
            self.free[link] = max(self.now, self.free.get(link, 0.0)) + time
            end = max(end, self.free[link])
        self.due[Key.remote, at] = end + self.LATENCY

    def send(self, source, target, mask):
        at = len(self.remote)
        self.remote.append((source, target, mask))
        if mask == CORE:
            self.issue(at)
        else:
            link = {Y: Key.y, NEAR: Key.side, FAR: Key.middle}.get(mask, Key.x)
            self.queues[link].append((self.rank, at))
        return (Key.remote, at)

    def feed(self, until):
        fed = False
        for link, queue in self.queues.items():
            while queue and self.free.get(link, 0.0) < until + self.AHEAD:
                first = min(queue)
                queue.remove(first)
                self.issue(first[1])
                fed = True
        return fed

    def keep(self, source, target):
        at = len(self.near_by)
        copy = pltpu.make_async_copy(source, target, self.locals.at[at])
        copy.start()
        self.near_by.append(copy)
        self.due[Key.local, at] = self.now + 2.0
        return (Key.local, at)

    def arrived(self, *handles):
        for handle in handles:
            if handle in self.seen:
                continue
            self.seen.add(handle)
            self.now = max(self.now, self.due[handle])
            if handle[0] == Key.remote:
                self.remote[handle[1]].wait_recv()
            else:
                self.near_by[handle[1]].wait()

    def run(self, *tasks):
        live = []
        for rank, task in enumerate(tasks):
            self.rank = rank
            live.append([rank, task, next(task)])

        def waits(entry):
            return entry[2]() if callable(entry[2]) else entry[2]

        def when(entry):
            handles = waits(entry)
            if handles is None:
                return 1e9, entry[0]
            dues = [self.due.get(h, 1e9) for h in handles if h not in self.seen]
            return max([self.now] + dues), entry[0]

        while live:
            entry = min(live, key=when)
            if self.feed(min(when(entry)[0], self.now + 1e6)):
                continue
            self.arrived(*waits(entry))
            self.rank = entry[0]
            try:
                entry[2] = next(entry[1])
            except StopIteration:
                live.remove(entry)
        self.feed(1e9)

    def finish(self):
        for at, copy in enumerate(self.remote):
            self.arrived((Key.remote, at))
            copy.wait_send()
        for at in range(len(self.near_by)):
            self.arrived((Key.local, at))


class Flags:
    def __init__(self):
        self.set = {}

    def raised(self, key, handles=()):
        self.set[key] = list(handles)

    def wait(self, *keys, more=()):
        def ask():
            if any(key not in self.set for key in keys):
                return None
            return [h for key in keys for h in self.set[key]] + list(more)

        return ask


FAST, STEADY = (2.5, 91, 400, 5.0), (3.5, 86, 300, 6.0)
KEEN, EARLY = (2.5, 91, 400, 2.0), (2.5, 91, 400, 15.0)


def comm_call(work, number, masks, arrays, in_vmem, outs, out_vmem, scratch, copies, stay, mb=48, pace=FAST):
    def space(fast):
        return pl.BlockSpec(memory_space=pltpu.VMEM if fast else pl.ANY)

    def body(*refs):
        n, m = len(arrays), len(outs)
        place = Place()
        wire = Wire(place, *refs[-3:], pace)
        wire.greet(masks)
        work(place, wire, refs[:n], refs[n : n + m], refs[n + m : -3])
        wire.finish()

    return pl.pallas_call(
        body,
        in_specs=[space(v) for v in in_vmem],
        out_specs=[space(v) for v in out_vmem],
        out_shape=[jax.ShapeDtypeStruct(shape, kind) for shape, kind in outs],
        scratch_shapes=list(scratch)
        + [
            pltpu.SemaphoreType.DMA((copies,)),
            pltpu.SemaphoreType.DMA((copies,)),
            pltpu.SemaphoreType.DMA((max(stay, 1),)),
        ],
        compiler_params=pltpu.CompilerParams(
            collective_id=number, has_side_effects=True, vmem_limit_bytes=int(mb * 1024 * 1024)
        ),
        cost_estimate=pl.CostEstimate(flops=0, bytes_accessed=1 << 16, transcendentals=0),
    )(*arrays)


def head_gather(place, wire, weight, out, flags=None, key=None, alike=False):
    rows, width = weight.shape[0], out.shape[1]
    block = 4 * rows
    base = place.y * 4 * block

    def columns(tp):
        return weight if alike else weight.at[:, pl.ds(pl.multiple_of(tp * width, 128), width)]

    def part(m):
        return out.at[pl.ds(pl.multiple_of(base + m * block, 16), block)]

    own = out.at[pl.ds(pl.multiple_of(base + place.tp * rows, 16), rows)]
    handles = [wire.keep(columns(place.tp), own)]
    for mask in (X, X | CORE, CORE):
        handles.append(wire.send(columns(place.partner(mask)[1]), own, mask))
    yield handles
    far = wire.send(part(0), part(2), FAR)
    near = wire.send(part(0), part(1), NEAR)
    over = [wire.send(part(0), part(0), Y)]
    yield [far]
    last = wire.send(part(2), part(3), NEAR)
    over.append(wire.send(part(2), part(2), Y))
    yield [near]
    over.append(wire.send(part(1), part(1), Y))
    yield [last]
    over.append(wire.send(part(3), part(3), Y))
    yield over
    if flags is not None:
        flags.raised(key)


def output_gather(place, wire, block, out, flags, key):
    def part(m):
        return out.at[m, place.y]

    yield [wire.keep(block, part(0))]
    far = wire.send(part(0), part(2), FAR)
    near = wire.send(part(0), part(1), NEAR)
    over = [wire.send(part(0), part(0), Y)]
    yield [far]
    last = wire.send(part(2), part(3), NEAR)
    over.append(wire.send(part(2), part(2), Y))
    yield [near]
    over.append(wire.send(part(1), part(1), Y))
    yield [last]
    over.append(wire.send(part(3), part(3), Y))
    yield over
    flags.raised(key)


def ffn_trade(place, wire, weight, halves, out):
    cols = halves.shape[2]

    def to_cut(rows):
        for y in range(2):
            halves[y, rows] = weight[rows, y * cols : (y + 1) * cols]

    row_loop(weight.shape[0], 32, to_cut)
    own = out.at[0, place.y]
    yield [
        wire.send(halves.at[1 - place.y], own, Y),
        wire.keep(halves.at[place.y], own),
    ]


def ffn_traded(place, wire, weight, halves, out, flags, key):
    yield from ffn_trade(place, wire, weight, halves, out)
    flags.raised(key)


def far_spread(wire, out, flags, first):
    yield flags.wait(first)
    far = [wire.send(out.at[0, y], out.at[2, y], FAR) for y in range(2)]
    yield far + [wire.send(out.at[0, y], out.at[1, y], NEAR) for y in range(2)]


def last_spread(place, wire, blocks, out):
    waits = [wire.keep(blocks.at[z], out.at[z]) for z in range(3)]
    yield waits + [wire.send(blocks.at[2, y], out.at[3, y], NEAR) for y in range(2)]


def ffn_spread(place, wire, out, flags, first, then):
    yield flags.wait(first)
    waits = [wire.send(out.at[0, y], out.at[1, y], NEAR) for y in range(2)]
    yield flags.wait(then)
    far = [wire.send(out.at[0, y], out.at[2, y], FAR) for y in range(2)]
    for y in range(2):
        yield [far[y]]
        waits.append(wire.send(out.at[2, y], out.at[3, y], NEAR))
    yield waits


def rows_gather(place, wire, own, out):
    mine = out.at[:, place.tp]
    stay = wire.keep(own, mine)
    across = wire.send(own, mine, X)
    beside = wire.send(own, mine, CORE)
    yield [across]
    theirs = out.at[:, place.partner(X)[1]]
    yield [stay, beside, wire.send(theirs, theirs, CORE)]


def small_gather(place, wire, own, out):
    handles = [
        wire.keep(own, out.at[pl.ds(place.flat, 1)]),
        wire.send(own, out.at[pl.ds(place.flat, 1)], CORE),
    ]
    size = 2
    for mask in (X, Y, NEAR, FAR):
        yield handles
        part = out.at[pl.ds(place.flat // size * size, size)]
        handles = [wire.send(part, part, mask)]
        size *= 2
    yield handles


def plane_gather(place, wire, first, second, out, flags=None):
    line_a = [out.at[0, 0, m] for m in range(4)]
    line_b = [out.at[0, 1, m] for m in range(4)]
    beside = [[], []]

    def pass_on(half, m, source=None):
        source = out.at[0, half, m] if source is None else source
        beside[half].append(wire.send(source, out.at[1, half, m], CORE))

    a_x = wire.send(first, line_a[1], X)
    b_y = wire.send(second, line_b[1], Y)
    a_y = wire.send(first, line_a[2], Y)
    b_x = wire.send(second, line_b[2], X)
    stay = [wire.keep(first, line_a[0]), wire.keep(second, line_b[0])]
    pass_on(0, 0, first)
    pass_on(1, 0, second)
    yield [a_x]
    a_xy = wire.send(line_a[1], line_a[3], Y)
    pass_on(0, 1)
    yield [b_y]
    b_xy = wire.send(line_b[1], line_b[3], X)
    pass_on(1, 1)
    yield [a_y, b_x]
    pass_on(0, 2)
    pass_on(1, 2)
    if flags is not None:
        flags.raised((0, 0), [stay[0], a_xy])
        flags.raised((0, 1), [stay[1], b_xy])
    yield [a_xy]
    pass_on(0, 3)
    if flags is not None:
        flags.raised((1, 0), beside[0])
    yield [b_xy]
    pass_on(1, 3)
    if flags is not None:
        flags.raised((1, 1), beside[1])
    yield stay + beside[0] + beside[1]


def by_tp(values, count, side):
    first, second = count
    order = [(a * second + b) * side for b in range(second) for a in range(first)]
    return jnp.concatenate([values[:, at : at + side] for at in order], axis=1)


def heads_trade(place, wire, branch, out):
    width = out.shape[1] // 4

    def columns(ref, index):
        return ref.at[:, pl.ds(pl.multiple_of(index * width, 128), width)]

    mine = columns(out, place.z_turn(place.tp))
    handles = [wire.keep(columns(branch, place.tp), mine)]
    for mask in (X, X | CORE, CORE):
        handles.append(wire.send(columns(branch, place.partner(mask)[1]), mine, mask))
    yield handles


def heads_return(place, wire, grads, out):
    width = out.shape[1] // 4

    def columns(ref, index):
        return ref.at[:, pl.ds(pl.multiple_of(index * width, 128), width)]

    mine = columns(out, place.tp)
    handles = [wire.keep(columns(grads, place.z_turn(place.tp)), mine)]
    for mask in (X, X | CORE, CORE):
        there = place.z_turn(place.partner(mask)[1])
        handles.append(wire.send(columns(grads, there), mine, mask))
    yield handles


def pieces_scan(place, wire, reverse, survive, state, out, bufs):
    send_s, send_b, got_s, got_b = bufs
    wide = state.shape[-1] // survive.shape[-1]
    total_s, total_b = survive[...], state[...]
    before_s = before_b = None

    def join(first_s, first_b, second_s, second_b):
        spread = jnp.concatenate([second_s] * wide, axis=-1)
        return first_s * second_s, spread * first_b + second_b

    for step, (mask, bit) in enumerate(((Y, place.y), (NEAR, place.near), (FAR, place.far))):
        send_s[step] = total_s
        send_b[step] = total_b.astype(BF)
        yield [
            wire.send(send_b.at[step], got_b.at[step], mask),
            wire.send(send_s.at[step], got_s.at[step], mask),
        ]
        other_s, other_b = got_s[step], got_b[step].astype(F32)
        later = bit == (0 if reverse else 1)
        if before_s is None:
            before_s = jnp.where(later, other_s, 1.0)
            before_b = jnp.where(later, other_b, 0.0)
        else:
            joined_s, joined_b = join(other_s, other_b, before_s, before_b)
            before_s = jnp.where(later, joined_s, before_s)
            before_b = jnp.where(later, joined_b, before_b)
        if mask != FAR:
            first_s, first_b = jnp.where(later, other_s, total_s), jnp.where(later, other_b, total_b)
            second_s = jnp.where(later, total_s, other_s)
            second_b = jnp.where(later, total_b, other_b)
            total_s, total_b = join(first_s, first_b, second_s, second_b)
    out[...] = before_b


def scan_buffers(state_shape, survive_shape):
    return [
        pltpu.VMEM((3,) + survive_shape, F32),
        pltpu.VMEM((3,) + state_shape, BF),
        pltpu.VMEM((3,) + survive_shape, F32),
        pltpu.VMEM((3,) + state_shape, BF),
    ]


def row_loop(count, step, work):
    def body(i, carry):
        work(pl.ds(pl.multiple_of(i * step, step), step))
        return carry

    lax.fori_loop(0, count // step, body, 0)


def rows_fold(place, wire, part, sums, got_core, got_x, finish):
    streams, count = part.shape[0], part.shape[3]
    other_x = 1 - place.x
    beside = [wire.send(part.at[s, :, 1 - place.core], got_core.at[s], CORE) for s in range(streams)]
    across = []
    for s in range(streams):
        yield [beside[s]]

        def to_send(rows, s=s):
            term = part[s, other_x, place.core, rows].astype(F32)
            sums[s, rows] = (term + got_core[s, other_x, rows].astype(F32)).astype(BF)

        row_loop(count, 16, to_send)
        across.append(wire.send(sums.at[s], got_x.at[s], X))
    for s in range(streams):
        yield [across[s]]

        def to_finish(rows, s=s):
            term = part[s, place.x, place.core, rows].astype(F32)
            term = term + got_core[s, place.x, rows].astype(F32)
            finish(s, rows, term + got_x[s, rows].astype(F32))

        row_loop(count, 16, to_finish)


def rows_buffers(part_shape):
    streams, _, _, count, width = part_shape
    return [
        pltpu.VMEM((streams, count, width), BF),
        pltpu.VMEM((streams, 2, count, width), BF),
        pltpu.VMEM((streams, count, width), BF),
    ]


def plane_fold(place, wire, near_part, far_part, bufs, finish, flags=None):
    got_core, send_two, got_two, send_one, got_one = bufs
    count = near_part.shape[2]
    if flags is None:
        flags = Flags()
        for h in range(2):
            flags.raised((Key.far, h))
            flags.raised((Key.near, h))
    beside = {}
    for h in range(2):
        yield flags.wait((Key.far, h))
        for m in (2, 3, 1, 0):
            beside[h, m] = wire.send(far_part.at[h, m], got_core.at[h, m], CORE)
    two, one = {}, {}
    for h in range(2):
        for m in (3, 2):
            yield flags.wait((Key.near, h), more=[beside[h, m]])

            def to_two(rows, h=h, m=m):
                term = near_part[h, m, rows].astype(F32) + got_core[h, m, rows].astype(F32)
                send_two[h, m - 2, rows] = term.astype(BF)

            row_loop(count, 16, to_two)
            two[h, m] = wire.send(send_two.at[h, m - 2], got_two.at[h, m - 2], (Y, X)[h])
    for h in range(2):
        yield [beside[h, 1], two[h, 3]]

        def to_one(rows, h=h):
            term = near_part[h, 1, rows].astype(F32) + got_core[h, 1, rows].astype(F32)
            send_one[h, rows] = (term + got_two[h, 1, rows].astype(F32)).astype(BF)

        row_loop(count, 16, to_one)
        one[h] = wire.send(send_one.at[h], got_one.at[h], (X, Y)[h])
    for h in range(2):
        yield [beside[h, 0], two[h, 2], one[h]]

        def to_finish(rows, h=h):
            def load(columns):
                term = near_part[h, 0, rows, columns].astype(F32)
                term = term + got_core[h, 0, rows, columns].astype(F32)
                term = term + got_two[h, 0, rows, columns].astype(F32)
                return term + got_one[h, rows, columns].astype(F32)

            finish(h, rows, load)

        row_loop(count, 16, to_finish)
        flags.raised((Key.done, h))


def plane_buffers(part_shape):
    halves, _, count, width = part_shape
    return [
        pltpu.VMEM(part_shape, BF),
        pltpu.VMEM((halves, 2, count, width), BF),
        pltpu.VMEM((halves, 2, count, width), BF),
        pltpu.VMEM((halves, count, width), BF),
        pltpu.VMEM((halves, count, width), BF),
    ]


def z_parts(place, load, width):
    size = width // 4
    parts = []
    for m in range(4):
        there = pl.multiple_of(place.z_turn(m) * size, 128)
        parts.append(load(pl.ds(there, size)))
    return jnp.concatenate(parts, axis=-1)


def add_into(target, terms, step=32):
    def work(rows):
        total = terms[0][rows].astype(F32)
        for term in terms[1:]:
            total = total + term[rows].astype(F32)
        target[rows] = total.astype(BF)

    row_loop(target.shape[0], step, work)


def ffn_fold(place, wire, part, bufs, out, flags=None, added=None):
    added = (part.at[0], part.at[2]) if added is None else (added.at[0], added.at[1])
    got_near, got_far, held = bufs
    first, second, far = [], [], []
    for z, handles in ((3, first), (1, second)):
        for y in range(2):
            if flags is not None:
                yield flags.wait((z, y))
            handles.append(wire.send(part.at[z, y], got_near.at[z // 2, y], NEAR))
    for y in range(2):
        yield [first[y]] if flags is None else flags.wait((2, y), more=[first[y]])
        add_into(held.at[0, y], [added[1].at[y], got_near.at[1, y]])
        far.append(wire.send(held.at[0, y], got_far.at[y], FAR))
    for y in range(2):
        yield [second[y], far[y]] if flags is None else flags.wait((0, y), more=[second[y], far[y]])
        add_into(held.at[1, y], [added[0].at[y], got_near.at[0, y], got_far.at[y]])
    mine = out.at[place.y]
    yield [
        wire.send(held.at[1, 1 - place.y], mine, Y),
        wire.keep(held.at[1, place.y], mine),
    ]


def weight_tiles(wire, rows_by, order, grads, put, flags=None):
    for key in order:
        yield []
        put(key, mm(rows_by(key), grads(), TN))
        wire.spend(1.2)
        if flags is not None:
            flags.raised(key)


def head_tiles(wire, rows, grads, part, flags):
    side = part.shape[2]
    for z in (3, 1, 2, 0):
        for y in range(2):
            yield []
            at = (y * 4 + z) * side
            part[y, z] = mm(rows[:, at : at + side], grads(), TN).astype(BF)
            wire.spend(0.6)
        flags.raised(z)


def ffn_buffers(part_shape):
    _, ys, rows, width = part_shape
    return [
        pltpu.VMEM((2, ys, rows, width), BF),
        pltpu.VMEM((ys, rows, width), BF),
        pltpu.VMEM((2, ys, rows, width), BF),
    ]


def line_fold(place, wire, mine, theirs, bufs, flags=None):
    got_y, got_near, got_far, held = bufs
    over = {}
    for m in (3, 1, 2, 0):
        if flags is not None:
            yield flags.wait(m)
        over[m] = wire.send(theirs(m), got_y.at[m], Y)
    yield [over[3]]
    add_into(held.at[1], [mine(3), got_y.at[3]])
    last = wire.send(held.at[1], got_near.at[1], NEAR)
    yield [over[1]]
    add_into(held.at[0], [mine(1), got_y.at[1]])
    near = wire.send(held.at[0], got_near.at[0], NEAR)
    yield [over[2], last]
    add_into(held.at[2], [mine(2), got_y.at[2], got_near.at[1]])
    far = wire.send(held.at[2], got_far, FAR)
    yield [over[0], near, far]
    add_into(held.at[3], [mine(0), got_y.at[0], got_near.at[0], got_far])


def line_buffers(rows, width):
    return [
        pltpu.VMEM((4, rows, width), BF),
        pltpu.VMEM((2, rows, width), BF),
        pltpu.VMEM((rows, width), BF),
        pltpu.VMEM((4, rows, width), BF),
    ]


def head_fold(place, wire, part, bufs, out, flags=None):
    yield from line_fold(
        place, wire, lambda m: part.at[place.y, m], lambda m: part.at[1 - place.y, m], bufs, flags
    )
    own = bufs[3].at[3]
    rows, width = out.shape[0], own.shape[1]

    def block(tp):
        return own.at[pl.ds(pl.multiple_of(tp * rows, 16), rows)]

    mine = out.at[:, pl.ds(pl.multiple_of(place.tp * width, 128), width)]
    handles = [wire.keep(block(place.tp), mine)]
    for mask in (X, X | CORE, CORE):
        handles.append(wire.send(block(place.partner(mask)[1]), mine, mask))
    yield handles


def output_fold(place, wire, part, bufs, out, flags=None):
    yield from line_fold(
        place, wire, lambda m: part.at[m, place.y], lambda m: part.at[m, 1 - place.y], bufs, flags
    )
    yield [wire.keep(bufs[3].at[3], out)]


def small_fold(place, wire, values, bufs, out):
    got, total = bufs
    source, start, size = values, 0, 16
    steps = ((FAR, place.far), (NEAR, place.near), (Y, place.y), (X, place.x), (CORE, place.core))
    for mask, bit in steps:
        here = pl.ds(start, size)
        theirs = pl.ds(source_start(start, size) + (1 - bit) * size, size)
        yield [wire.send(source.at[theirs], got.at[here], mask)]
        mine = pl.ds(source_start(start, size) + bit * size, size)
        total[here] = source[mine] + got[here]
        source, start, size = total, start + size, size // 2
    out[...] = total[pl.ds(start - 1, 1)]


def source_start(start, size):
    return 0 if start == 0 else start - 2 * size


class Bits:
    CORE, X, Y, NEAR, FAR = 1, 2, 4, 8, 16

    def __init__(self):
        seq, tp = lax.axis_index(SEQ), lax.axis_index(TP)
        self.core, self.x = tp & 1, tp >> 1
        self.y, self.z = seq & 1, seq >> 1

    def steps(self):
        return (
            (self.CORE, self.core),
            (self.X, self.x),
            (self.Y, self.y),
            (self.NEAR, self.z & 1),
            (self.FAR, self.z >> 1),
        )


def swap(values, mask):
    pairs = [(i, i ^ mask) for i in range(32)]
    return lax.ppermute(values, (SEQ, TP), pairs)


def half(values, axis, which):
    size = values.shape[axis] // 2
    return lax.dynamic_slice_in_dim(values, which * size, size, axis)


def trade(values, mask, bit, axis, kind=None):
    other = half(values, axis, 1 - bit)
    if kind is not None:
        other = other.astype(kind)
    return half(values, axis, bit), swap(other, mask)


def in_order(mine, theirs, bit):
    first = bit == 0
    return jnp.where(first, mine, theirs), jnp.where(first, theirs, mine)


def z_blocks(block):
    far = swap(block, Bits.FAR)
    return [block, swap(block, Bits.NEAR), far, swap(far, Bits.NEAR)]


def z_fold(blocks, kind=BF):
    first = blocks[0] + swap(blocks[1].astype(kind), Bits.NEAR).astype(F32)
    second = blocks[2] + swap(blocks[3].astype(kind), Bits.NEAR).astype(F32)
    return first + swap(second.astype(kind), Bits.FAR).astype(F32)


def z_relative(values, z, axis):
    size = values.shape[axis] // 4
    return jnp.concatenate(
        [lax.dynamic_slice_in_dim(values, (m ^ z) * size, size, axis) for m in range(4)], axis
    )


def spread_tp(values, at):
    streams, count, width = values.shape
    pair = jnp.stack(in_order(values, swap(values, Bits.X), at.x), axis=1)
    both = jnp.stack(in_order(pair, swap(pair, Bits.CORE), at.core), axis=2)
    return both.reshape(streams, 4 * count, width)


def fold_tp(part, at):
    streams, count, width = part.shape
    parts = part.reshape(streams, 2, 2, count // 4, width)
    mine, got = trade(parts, Bits.CORE, at.core, 2, BF)
    mine, got = trade(mine + got.astype(F32), Bits.X, at.x, 1, BF)
    return (mine + got.astype(F32)).reshape(streams, count // 4, width)


def spread_plane(rows):
    count = rows.shape[0] // 2
    first, second = rows[:count], rows[count:]
    first = jnp.concatenate([first, swap(first, Bits.X)], axis=0)
    second = jnp.concatenate([second, swap(second, Bits.Y)], axis=0)
    four = [first, swap(first, Bits.Y), second, swap(second, Bits.X)]
    four = jnp.concatenate(four, axis=0)
    return jnp.concatenate([four, swap(four, Bits.CORE)], axis=0)


def fold_half(part, mask):
    size = part.shape[0] // 2
    return part[:size] + swap(part[size:].astype(BF), mask).astype(F32)


def fold_plane(work):
    sent = swap(work(1).astype(BF), Bits.CORE)
    part = work(0) + sent.astype(F32)
    size = part.shape[0] // 2
    first = fold_half(fold_half(part[:size], Bits.Y), Bits.X)
    second = fold_half(fold_half(part[size:], Bits.X), Bits.Y)
    return jnp.concatenate([first, second], axis=0)


def gather_head(weight, at):
    rows, width = weight.shape
    mine, got = trade(weight, Bits.X, at.x, 1)
    both = jnp.stack(in_order(mine, got, at.x), axis=0)
    mine, got = trade(both, Bits.CORE, at.core, 2)
    both = jnp.stack(in_order(mine, got, at.core), axis=1).reshape(4 * rows, width // 4)
    line = jnp.concatenate(z_blocks(both), axis=0)
    return jnp.concatenate(in_order(line, swap(line, Bits.Y), at.y), axis=0)


def fold_head(grad, at):
    mine, got = trade(grad, Bits.Y, at.y, 0, BF)
    line = mine + got.astype(F32)
    rows = line.shape[0] // 4
    own = z_fold([line[m * rows : (m + 1) * rows] for m in range(4)])
    width = own.shape[1]
    own = own.reshape(2, 2, rows // 4, width)
    mine, got = trade(own, Bits.CORE, at.core, 1, BF)
    own = jnp.concatenate(in_order(mine, got.astype(F32), at.core), axis=-1)
    mine, got = trade(own, Bits.X, at.x, 0, BF)
    own = jnp.concatenate(in_order(mine, got.astype(F32), at.x), axis=-1)
    return own.reshape(rows // 4, 4 * width)


def turn_bits(values, back):
    pairs = []
    for i in range(32):
        z, y, x, core = i >> 3, (i >> 2) & 1, (i >> 1) & 1, i & 1
        there = z * 8 + core * 4 + y * 2 + x
        pairs.append((there, i) if back else (i, there))
    return lax.ppermute(values, (SEQ, TP), pairs)


def gather_output(weight, at):
    block = turn_bits(weight, False)
    line = jnp.stack(z_blocks(block), axis=0)
    both = jnp.stack(in_order(line, swap(line, Bits.Y), at.y), axis=1)
    return both.reshape(8 * weight.shape[0], weight.shape[1])


def fold_output(grad, at):
    rows, width = grad.shape
    parts = grad.reshape(4, 2, rows // 8, width)
    mine, got = trade(parts, Bits.Y, at.y, 1, BF)
    line = (mine + got.astype(F32)).reshape(4, rows // 8, width)
    own = z_fold([line[m] for m in range(4)])
    return turn_bits(own.astype(BF), True).astype(F32)


def heads_to_rows(values, at):
    mine, got = trade(values, Bits.X, at.x, 1)
    both = jnp.stack(in_order(mine, got, at.x), axis=0)
    mine, got = trade(both, Bits.CORE, at.core, 2)
    both = jnp.stack(in_order(mine, got, at.core), axis=1)
    parts = both.reshape((4,) + both.shape[2:])
    return jnp.concatenate(
        [lax.dynamic_index_in_dim(parts, m ^ at.z, 0, False) for m in range(4)], axis=1
    )


def rows_to_heads(values, at):
    width = values.shape[1] // 4
    parts = jnp.stack(
        [
            lax.dynamic_slice_in_dim(values, (m ^ at.z) * width, width, 1)
            for m in range(4)
        ],
        axis=0,
    ).reshape(2, 2, values.shape[0], width)
    mine, got = trade(parts, Bits.X, at.x, 0)
    first, second = in_order(mine[0], got[0], at.x)
    both = jnp.stack([first, second], axis=0)
    mine, got = trade(both, Bits.CORE, at.core, 1)
    first, second = in_order(mine[:, 0], got[:, 0], at.core)
    both = jnp.stack([first, second], axis=1)
    return jnp.concatenate([both[0, 0], both[0, 1], both[1, 0], both[1, 1]], axis=1)


class FfnGather:
    def __init__(self, weight, at):
        mine, got = trade(weight, Bits.Y, at.y, 1)
        self.block = jnp.concatenate(in_order(mine, got, at.y), axis=0)

    def far(self, *after):
        self.block = tie(self.block, *after)
        self.far_block = swap(self.block, Bits.FAR)
        return (self.far_block,)

    def near(self, *after):
        self.block = tie(self.block, *after)
        self.near_block = swap(self.block, Bits.NEAR)
        self.last_block = swap(self.far_block, Bits.NEAR)
        return (self.near_block, self.last_block)

    def whole(self):
        parts = [self.block, self.near_block, self.far_block, self.last_block]
        return jnp.concatenate(parts, axis=0)


class FfnFold:
    def __init__(self, grad, at):
        self.at = at
        rows = grad.shape[0] // 4
        self.parts = [grad[m * rows : (m + 1) * rows] for m in range(4)]

    def near(self, *after):
        sent = [tie(self.parts[1].astype(BF), *after), self.parts[3].astype(BF)]
        self.got = [swap(s, Bits.NEAR) for s in sent]
        return tuple(self.got)

    def far(self, *after):
        second = self.parts[2] + self.got[1].astype(F32)
        self.last = swap(tie(second.astype(BF), *after), Bits.FAR)
        return (self.last,)

    def whole(self):
        own = self.parts[0] + self.got[0].astype(F32) + self.last.astype(F32)
        mine, got = trade(own, Bits.Y, self.at.y, 0, BF)
        return jnp.concatenate(in_order(mine, got.astype(F32), self.at.y), axis=1)


class PlainWhole:
    def __init__(self, value):
        self.value = value

    def far(self, *after):
        return ()

    near = far

    def whole(self):
        return self.value


def spread_all(values, at):
    for mask, bit in at.steps():
        values = jnp.concatenate(in_order(values, swap(values, mask), bit), axis=0)
    return values


def fold_all(values, at):
    for mask, bit in reversed(at.steps()):
        mine, got = trade(values, mask, bit, 0)
        values = mine + got
    return values


def scan_pieces(part, at, reverse):
    total, before = part, None
    steps = ((Bits.Y, at.y), (Bits.NEAR, at.z & 1), (Bits.FAR, at.z >> 1))
    for mask, bit in steps:
        other = (swap(total[0], mask), swap(total[1].astype(BF), mask).astype(F32))
        later = bit == (0 if reverse else 1)
        if before is None:
            before = (
                jnp.where(later, other[0], 1.0),
                jnp.where(later, other[1], 0.0),
            )
        else:
            joined = chain(other, before)
            before = tuple(jnp.where(later, a, b) for a, b in zip(joined, before))
        if mask != Bits.FAR:
            first = tuple(jnp.where(later, o, t) for o, t in zip(other, total))
            second = tuple(jnp.where(later, t, o) for o, t in zip(other, total))
            total = chain(first, second)
    return before


@dataclasses.dataclass
class Mixer:
    reading: jax.Array
    scores: jax.Array
    share: jax.Array
    branch: jax.Array
    normed: jax.Array
    logits: jax.Array
    keep: jax.Array
    written: jax.Array
    slots_in: jax.Array
    slots_end: jax.Array
    weights: list
    raw: list
    output: jax.Array
    rows: jax.Array = None
    low: jax.Array = None
    low_rank: jax.Array = None
    rank: jax.Array = None
    survive: jax.Array = None
    out_gain: jax.Array = None
    ffn_gain: jax.Array = None
    attn_gain: jax.Array = None


def alive_rows(seq_cuts, seq, length):
    positions = seq * length + jnp.arange(length)
    starts = (positions[None, :] == 0) | (positions[None, :] == seq_cuts[:, None])
    return jnp.where(starts, 0.0, 1.0).astype(F32)[:, None, :]


class Plain:
    def __init__(self):
        self.seq, self.tp = lax.axis_index(SEQ), lax.axis_index(TP)
        self.seq_count, self.tp_count = lax.axis_size(SEQ), lax.axis_size(TP)
        self.sharing = self.tp_count // H
        self.head, self.member = self.tp // self.sharing, self.tp % self.sharing


def plain_scan(part, at, reverse):
    gathered = (
        lax.all_gather(part[0], SEQ),
        lax.all_gather(part[1].astype(BF), SEQ),
    )
    state = (jnp.ones_like(part[0]), jnp.zeros_like(part[1]))

    def step(count, state):
        source = at.seq_count - 1 - count if reverse else count
        piece = tuple(lax.dynamic_index_in_dim(a, source, 0, False) for a in gathered)
        return chain(state, (piece[0], piece[1].astype(F32)))

    steps = at.seq_count - 1 - at.seq if reverse else at.seq
    return lax.fori_loop(0, steps, step, state)


class PlainMoves:
    def small(self, packed):
        return lax.all_gather(packed, (SEQ, TP))

    def small_sum(self, packed):
        return lax.psum_scatter(packed, (SEQ, TP), scatter_dimension=0, tiled=True)[0]

    def start(self, tokens, seq_cuts, weights, w_output, small, ffn, cotangent):
        self.ffn = ffn
        devices = self.at.seq_count * self.at.tp_count
        gathered = self.small(jnp.concatenate([a.reshape(-1) for a in small]))
        unpacked, taken = [], 0
        for a in small:
            part = gathered[:, taken : taken + a.size]
            unpacked.append(part.reshape((devices * a.shape[0],) + a.shape[1:]))
            taken += a.size
        low, full_rank, full_bias, attn, out, ffn_gain = unpacked
        slots = full_bias.shape[0] // H
        rank = lax.dynamic_slice_in_dim(full_rank, self.head * slots, slots, 0).astype(F32)
        bias = lax.dynamic_slice_in_dim(full_bias, self.head * slots, slots, 0).astype(F32)
        rows = self.piece(tokens)
        held, length, width = rows.shape
        inputs = rows.reshape(held * length, width).astype(F32)
        normed = (inputs * inverse_rms(inputs) * attn.astype(F32)).astype(BF)
        low_rank = product(normed, low, NN).reshape(held, length, -1)
        logits = jnp.einsum("mr,str->smt", rank, low_rank, precision=lax.Precision.HIGHEST)
        logits = logits + bias[None, :, None]
        true_keep, written = gates(logits)
        alive = self.own_streams(alive_rows(seq_cuts, self.at.seq, length))
        keep = true_keep * alive
        weights = [self.head_weight(w) for w in weights]
        raw = [product(normed, w, NN).reshape(held, length, -1) for w in weights]
        hd = raw[0].shape[-1]
        state, survive = per_stream(
            piece_state,
            [raw[0], raw[1], keep, written],
            [((slots, 2 * hd), F32), ((slots, 1), F32)],
            1 << 30,
        )
        slots_in = self.scan((survive[..., 0], state), False)[1]
        key_raw, value_raw, query_raw, gate_raw = raw
        reading, scores, share = per_stream(
            piece_read,
            [query_raw, key_raw, value_raw, keep, written, slots_in],
            [((length, hd), F32), ((slots, length), F32), ((slots, length), F32)],
            1 << 30,
        )
        read_normed = reading * inverse_rms(reading) * out.astype(F32)
        branch = (read_normed * silu(gate_raw)).astype(BF).reshape(held * length, hd)
        output = self.output_weight(w_output)
        self.mixed = product(branch, output, NN).reshape(held, length, width)
        return Mixer(
            reading=reading,
            scores=scores,
            share=share,
            branch=branch,
            rows=rows,
            normed=normed,
            low=low,
            low_rank=low_rank,
            rank=rank,
            logits=logits,
            keep=keep,
            written=written,
            survive=survive[..., 0],
            slots_in=slots_in,
            slots_end=survive * slots_in + state,
            weights=weights,
            raw=raw,
            output=output,
            out_gain=out.astype(F32),
            ffn_gain=ffn_gain.astype(F32),
            attn_gain=attn.astype(F32),
        )

    def feed_forward(self, tokens, gain, cotangent):
        streams, count, width = tokens.shape
        own_rows = streams * count
        hidden = (tokens.astype(F32) + self.sum_piece(self.mixed)).reshape(own_rows, width)
        scale = inverse_rms(hidden)
        ffn_in = self.ffn_rows((hidden * scale * gain).astype(BF))
        cot = self.ffn_rows(cotangent.reshape(own_rows, width))
        down, gate, up = [lax.all_gather(w, SEQ, axis=0, tiled=True) for w in self.ffn]
        grad_product = product(cot, down, NN)
        gate_pre, up_pre = product(ffn_in, gate, NN), product(ffn_in, up, NN)
        sig = jax.nn.sigmoid(gate_pre)
        act = (gate_pre * sig * up_pre).astype(BF)
        slope = sig * (1.0 + gate_pre * (1.0 - sig))
        grad_gate = (grad_product * up_pre * slope).astype(BF)
        grad_up = (grad_product * gate_pre * sig).astype(BF)
        grad = self.ffn_sum(product(grad_gate, gate, NT) + product(grad_up, up, NT))
        self.gate_grad = self.ffn_grad(product(ffn_in, grad_gate, TN).astype(BF))
        self.up_grad = self.ffn_grad(product(ffn_in, grad_up, TN).astype(BF))
        self.down_sum = self.ffn_grad(product(cot, act, TN).astype(BF))
        self.result = (hidden + self.ffn_sum(product(act, down, NT))).astype(BF)
        gain_grad = jnp.sum(grad * hidden * scale, axis=0)
        grad_hidden = cotangent.reshape(own_rows, width).astype(F32)
        grad_hidden = grad_hidden + norm_back(hidden, scale, gain, grad)
        return grad_hidden, gain_grad, self.piece(grad_hidden.astype(BF).reshape(cotangent.shape))

    def ffn_grad(self, grad):
        own = lax.psum_scatter(grad, SEQ, scatter_dimension=0, tiled=True)
        return own.astype(F32)

    def mixer_back(self, mixer, grad_mixed):
        reading, scores, share, branch_out = mixer.reading, mixer.scores, mixer.share, mixer.branch
        streams, length, hd = reading.shape
        slots = scores.shape[1]
        key_raw, value_raw, query_raw, gate_raw = mixer.raw
        grad_branch = product(grad_mixed, mixer.output, NT).reshape(reading.shape)
        self.output_sum = self.output_grad(product(branch_out, grad_mixed, TN))
        scale = inverse_rms(reading)
        normed = reading * scale * mixer.out_gain
        grad_gate = (grad_branch * normed * silu_slope(gate_raw)).astype(BF)
        grad = grad_branch * silu(gate_raw)
        gain_sum = jnp.sum(grad * reading * scale, axis=(0, 1))[None]
        grad_read = norm_back(reading, scale, mixer.out_gain, grad)
        grad_query, grad_k, grad_v, direct, back, own = per_stream(
            piece_back,
            [query_raw, key_raw, value_raw, mixer.keep, mixer.written]
            + [mixer.slots_in, scores, share, grad_read],
            [
                ((length, hd), BF),
                ((length, hd), F32),
                ((length, hd), F32),
                ((slots, 2 * hd), F32),
                ((slots, length), F32),
                ((slots, length), F32),
            ],
            1 << 30,
        )
        after = self.scan((mixer.survive, direct), True)[1]
        self.head_sums = [
            self.head_grad(product(mixer.normed, g.reshape(-1, hd), TN))
            for g in (grad_query, grad_gate)
        ]
        return after, gain_sum, grad_query, grad_gate, grad_k, grad_v, back, own

    def finish(self, mixer, back, tokens, grad_hidden, ffn_gain_grad, small):
        after, out_gain_grad, grad_query, grad_gate, grad_k, grad_v, pulled, flow = back
        held, length, hd = grad_k.shape
        width, slots = tokens.shape[-1], flow.shape[1]
        grad_key, grad_value, grad_log = per_stream(
            piece_after,
            [mixer.raw[0], mixer.raw[1], mixer.keep, mixer.written]
            + [grad_k, grad_v, pulled, flow, after, mixer.slots_end],
            [((length, hd), BF), ((length, hd), BF), ((slots, length), F32)],
            1 << 30,
        )
        highest = lax.Precision.HIGHEST
        grad_f = grad_log * jax.nn.sigmoid(-mixer.logits) / GATE_SCALE
        grad_bias = jnp.sum(grad_f, axis=(0, 2))
        grad_rank = jnp.einsum("smt,str->mr", grad_f, mixer.low_rank, precision=highest)
        low_grad = jnp.einsum("smt,mr->str", grad_f, mixer.rank, precision=highest)
        low_grad = low_grad.reshape(held * length, -1)
        grads = [g.reshape(-1, hd) for g in (grad_key, grad_value, grad_query, grad_gate)]
        grad_normed = sum(product(g, w, NT) for g, w in zip(grads, mixer.weights))
        grad_normed = grad_normed + product(low_grad, mixer.low.astype(F32), NT)
        inputs = mixer.rows.reshape(-1, width).astype(F32)
        attn_grad = jnp.sum(grad_normed * inputs * inverse_rms(inputs), axis=0)
        grad_low = product(mixer.normed.astype(F32), low_grad, TN)

        def placed(part):
            entire = jnp.zeros((part.shape[0] * H,) + part.shape[1:], F32)
            return lax.dynamic_update_slice_in_dim(entire, part, self.head * part.shape[0], 0)

        sums = (grad_low, placed(grad_rank), placed(grad_bias), attn_grad)
        sums = sums + (out_gain_grad[0], ffn_gain_grad)
        devices = self.at.seq_count * self.at.tp_count
        packed = jnp.concatenate([a.reshape(devices, -1) for a in sums], axis=1)
        own = self.small_sum(packed)
        small_grads, taken = [], 0
        for a in small:
            small_grads.append(own[taken : taken + a.size].reshape(a.shape))
            taken += a.size
        heads = [self.head_grad(product(mixer.normed, g, TN)) for g in grads[:2]]
        heads = heads + self.head_sums + [self.output_sum]
        x = tokens.astype(F32)
        total = self.sum_piece(grad_normed.reshape(held, length, width))
        grad_tokens = norm_back(x, inverse_rms(x), mixer.attn_gain, total)
        grad_tokens = grad_tokens + grad_hidden.reshape(x.shape)
        ffn_grads = [self.gate_grad, self.up_grad, self.down_sum]
        return heads, ffn_grads, grad_tokens, self.result, small_grads

    def __init__(self):
        self.at = Plain()
        self.head, self.member = self.at.head, self.at.member

    def own_streams(self, values):
        count = values.shape[0] // self.at.sharing
        return lax.dynamic_slice_in_dim(values, self.member * count, count, 0)

    def piece(self, own):
        return self.own_streams(lax.all_gather(own, TP, axis=1, tiled=True))

    def sum_piece(self, part):
        streams = part.shape[0] * self.at.sharing
        entire = jnp.zeros((streams,) + part.shape[1:], BF)
        entire = lax.dynamic_update_slice_in_dim(
            entire, part.astype(BF), self.member * part.shape[0], 0
        )
        own = lax.psum_scatter(entire, TP, scatter_dimension=1, tiled=True)
        return own.astype(F32)

    def mixer_order(self, values):
        return values

    mixer_unorder = ffn_order = ffn_unorder = mixer_order

    def head_weight(self, weight):
        entire = lax.all_gather(weight, (SEQ, TP), axis=0, tiled=True)
        width = entire.shape[1] // H
        return lax.dynamic_slice_in_dim(entire, self.head * width, width, 1)

    def head_grad(self, grad):
        entire = jnp.zeros((grad.shape[0], grad.shape[1] * H), BF)
        entire = lax.dynamic_update_slice_in_dim(
            entire, grad.astype(BF), self.head * grad.shape[1], 1
        )
        own = lax.psum_scatter(entire, (SEQ, TP), scatter_dimension=0, tiled=True)
        return own.astype(F32)

    def output_weight(self, weight):
        entire = lax.all_gather(weight, (SEQ, TP), axis=0, tiled=True)
        rows = entire.shape[0] // H
        return lax.dynamic_slice_in_dim(entire, self.head * rows, rows, 0)

    def output_grad(self, grad):
        entire = jnp.zeros((grad.shape[0] * H, grad.shape[1]), BF)
        entire = lax.dynamic_update_slice_in_dim(
            entire, grad.astype(BF), self.head * grad.shape[0], 0
        )
        own = lax.psum_scatter(entire, (SEQ, TP), scatter_dimension=0, tiled=True)
        return own.astype(F32)

    def scan(self, part, reverse):
        return plain_scan(part, self.at, reverse)

    def ffn_rows(self, own):
        entire = lax.all_gather(own, TP, axis=0)
        return entire.reshape((-1,) + own.shape[1:])

    def ffn_sum(self, part):
        parts = part.astype(BF).reshape((self.at.tp_count, -1) + part.shape[1:])
        own = lax.psum_scatter(parts, TP, scatter_dimension=0, tiled=True)
        return own.reshape((-1,) + part.shape[1:]).astype(F32)


class BitMoves:
    def __init__(self):
        self.at = Bits()
        self.head, self.member = lax.axis_index(TP), 0

    def start(self, tokens, seq_cuts, weights, w_output, small, ffn, cotangent):
        w_low, w_rank, bias, attn_gain, out_gain, ffn_gain = small
        rank = w_low.shape[1]
        gains = jnp.stack([attn_gain, ffn_gain], axis=1)
        pack = jnp.concatenate([w_low, gains], axis=1)
        pack = jnp.pad(pack, ((0, 0), (0, 128 - pack.shape[1])))
        tall = w_rank.shape[0]
        lines = jnp.concatenate([w_rank, bias[:, None]], axis=1)
        lines = jnp.pad(lines, ((0, 0), (0, 128 - lines.shape[1])))
        gain_line = jnp.pad(out_gain, (0, 128 - out_gain.shape[0]))[None]
        lines = jnp.concatenate([lines, gain_line], axis=0)
        lines = jnp.pad(lines, ((0, 16 - lines.shape[0]), (0, 0)))[None]
        streams, count, width = tokens.shape
        length = 4 * count
        hd = width // 4
        per = out_gain.shape[0]
        slots = 8 * tall
        head = (width, hd)
        cut = (2, ffn[0].shape[0], ffn[0].shape[1] // 2)
        ffn_shape = (4,) + cut
        block = w_output
        alive = alive_rows(seq_cuts, lax.axis_index(SEQ), length)
        state_shape, slim = (streams, slots, 2 * hd), (streams, slots, 128)
        gate_shape = (streams, slots, length)

        def work(place, wire, given, outs, scratch):
            pack, lines, tokens, alive, own_tokens = given[:5]
            given = given[1:]
            heads_in, block, ffn_in, cot = given[4:8], given[8], given[9:12], given[12]
            pack_out, lines_out, low_out, logits, keep, written = outs[:6]
            survive, slots_in, slots_end, scores, share = outs[6:11]
            factor_out, normed_out, reading_out, branch_out, hidden_out = outs[11:16]
            gain_rows = outs[30]
            heads_out, raws_out, output_out = outs[16:20], outs[20:24], outs[24]
            ffn_out, cot_out, ffn_rows = outs[25:28], outs[28], outs[29]
            rows, normed, state = scratch[:3]
            heads, raws, cuts, scan = scratch[3:7], scratch[7:11], scratch[11:14], scratch[14:18]
            output_w, reading, branch, traded, mixed = scratch[18:23]
            hidden, ready = scratch[23:25]
            fold_bufs, cot_own = scratch[25:28], scratch[28]
            here = Flags()

            def fetch_rows():
                yield from rows_gather(place, wire, tokens, rows)
                here.raised(Key.rows)

            def fetch_lines():
                yield from small_gather(place, wire, lines, lines_out)
                here.raised(Key.lines)

            def across(row_at):
                side = width // 8
                for y in range(2):
                    for m in range(4):
                        to = pl.multiple_of((place.z_turn(m) * 2 + y) * side, 128)
                        yield pl.ds(to, side), slice((y * 4 + m) * side, (y * 4 + m + 1) * side)

            def norm():
                tall_rows = jnp.transpose(pack_out[...].astype(F32))
                gain_rows[2:3] = tall_rows[rank : rank + 1]
                for there, at in across(0):
                    gain_rows[3:4, there] = tall_rows[rank : rank + 1, at]
                    gain_rows[1:2, there] = tall_rows[rank + 1 : rank + 2, at]
                steps = count // 16

                def body(i, carry):
                    stream, tp, part = i // (4 * steps), i // steps % 4, i % steps
                    at = pl.multiple_of(part * 16, 16)
                    x = rows[stream, tp, pl.ds(at, 16)].astype(F32)
                    to = pl.ds(pl.multiple_of(i * 16, 16), 16)
                    scale = inverse_rms(x)
                    for there, here_at in across(0):
                        part = rows[stream, tp, pl.ds(at, 16), there].astype(F32)
                        part = part * scale * gain_rows[2:3, here_at]
                        normed[to, here_at] = part.astype(BF)
                    return carry

                lax.fori_loop(0, streams * 4 * steps, body, 0)

            def project(index):
                for s in range(streams):
                    raws[index][s] = mm(normed[s * length : (s + 1) * length], heads[index][...], NN)
                wire.spend(3.0)
                here.raised((Key.raw, index))
                wire.keep(heads[index], heads_out[index])
                wire.keep(raws[index], raws_out[index])

            def gains():
                own = lines_out[...].astype(F32)[:, tall]
                spot, turn_of = row((128, hd)), column((128, hd))
                spread = jnp.where(spot == turn_of % per, 1.0, 0.0)
                wide = mm(own, spread, NN)
                here_is = row(wide.shape) == column(wide.shape) // per
                out_row = jnp.sum(jnp.where(here_is, wide, 0.0), axis=0, keepdims=True)
                gain_rows[0:1, :hd] = out_row

            def read(s, carry):
                values = piece_read(
                    raws[2][s], raws[0][s], raws[1][s], keep[s], written[s], slots_in[s]
                )
                reading[s], scores[s], share[s] = values
                return carry

            def gated(s):
                def chunk(part):
                    at = pl.ds(pl.multiple_of(s * length + part.start, 16), part.size)
                    values = reading[s, part]
                    normed_read = values * inverse_rms(values) * gain_rows[0:1, :hd]
                    opened = normed_read * silu(raws[3][s, part])
                    branch[at] = by_tp(opened, (2, 4), hd // 8).astype(BF)

                row_loop(length, 32, chunk)

            def finish(stream, rows, part):
                values = own_tokens[stream, rows].astype(F32) + part
                hidden[stream, rows] = values
                normed = (values * inverse_rms(values) * gain_rows[1:2]).astype(BF)
                size = width // 4
                for m in range(4):
                    there = pl.ds(pl.multiple_of(place.z_turn(m) * size, 128), size)
                    ready[stream, rows, there] = normed[:, m * size : (m + 1) * size]

            def to_rows():
                yield here.wait(Key.branch)
                yield from heads_trade(place, wire, branch, traded)
                here.raised(Key.traded)
                wire.keep(traded, branch_out)
                yield here.wait(Key.mixed)
                yield from rows_fold(place, wire, mixed, *fold_bufs, finish)
                wire.keep(hidden, hidden_out)
                yield from plane_gather(place, wire, ready.at[0], ready.at[1], ffn_rows)

            def trade(i):
                return ffn_traded(place, wire, ffn_in[i], cuts[i], ffn_out[i], here, (Key.trade, i))

            def fetch_cot():
                side = width // 4

                def turn_row(at, stream):
                    for m in range(4):
                        there = pl.ds(pl.multiple_of(place.z_turn(m) * side, 128), side)
                        cot_own[stream, at, m * side : (m + 1) * side] = cot[stream, at, there]

                for stream in range(streams):
                    row_loop(count, 16, lambda at, stream=stream: turn_row(at, stream))
                yield from plane_gather(place, wire, cot_own.at[0], cot_own.at[1], cot_out)

            def compute():
                yield here.wait(Key.rows, Key.pack)
                norm()
                wire.spend(3.0)
                wire.keep(normed, normed_out)
                yield here.wait(Key.lines)
                own = lines_out[pl.ds(place.tp * 8, 8)].astype(F32)[:, :tall].reshape(slots, 128)
                factor = jnp.where(column(own.shape) < rank, own, 0.0)
                factor_out[...] = factor
                for s in range(streams):
                    low = mm(normed[s * length : (s + 1) * length], pack_out[...], NN)
                    low_out[s] = low
                    f = mm_fine(factor, low, NT) + own[:, rank : rank + 1]
                    logits[s] = f
                    kept, wrote = gates(f)
                    written[s] = wrote
                    keep[s] = kept * alive[s]
                wire.spend(2.0)
                for index in range(2):
                    yield here.wait(index)
                    project(index)
                for s in range(streams):
                    part, left = piece_state(raws[0][s], raws[1][s], keep[s], written[s])
                    state[s] = part
                    survive[s] = jnp.broadcast_to(left, slim[1:])
                wire.spend(3.0)
                here.raised(Key.state)
                for index in (2, 3):
                    yield here.wait(index)
                    project(index)
                gains()
                yield here.wait(Key.slots)
                lax.fori_loop(0, streams, read, 0)
                wire.spend(10.0)
                for s in range(streams):
                    gated(s)
                wire.spend(2.0)
                here.raised(Key.branch)
                wire.keep(reading, reading_out)
                yield here.wait(Key.traded, 4)
                wire.keep(output_w, output_out)
                for s in range(streams):
                    rows_in = traded[s * length : (s + 1) * length]
                    total = mm(rows_in, output_w[...].reshape(hd, width), NN)
                    mixed[s] = total.astype(BF).reshape(mixed.shape[1:])
                wire.spend(2.5)
                here.raised(Key.mixed)

            def exchange():
                yield here.wait(Key.state)
                yield from pieces_scan(place, wire, False, survive, state, slots_in, scan)
                for s in range(streams):
                    slots_end[s] = survive[s][:, :1] * slots_in[s] + state[s]
                here.raised(Key.slots)

            wire.run(
                fetch_lines(),
                head_gather(place, wire, pack, pack_out, here, Key.pack, True),
                exchange(),
                to_rows(),
                *[
                    head_gather(place, wire, w, o, here, i)
                    for i, (w, o) in enumerate(zip(heads_in, heads))
                ],
                fetch_rows(),
                trade(0),
                trade(1),
                output_gather(place, wire, block, output_w, here, 4),
                trade(2),
                far_spread(wire, ffn_out[0], here, (Key.trade, 0)),
                ffn_spread(place, wire, ffn_out[1], here, (Key.trade, 1), Key.slots),
                ffn_spread(place, wire, ffn_out[2], here, (Key.trade, 2), Key.slots),
                fetch_cot(),
                compute(),
            )

        vmem = pltpu.VMEM
        plane = (2, 2, 4, count, width)
        flat = (streams * length, width)
        raw = (streams, length, hd)
        mixed_shape = (streams, 2, 2, count, width)
        outs = comm_call(
            work,
            1,
            (CORE, X, X | CORE, Y, NEAR, FAR),
            [pack, lines, tokens, alive, tokens]
            + list(weights)
            + [block]
            + list(ffn)
            + [cotangent],
            [False, False, False, True, True] + [False] * 5 + [True] * 4,
            [
                ((width, 128), BF),
                ((32, 16, 128), BF),
                ((streams, length, 128), F32),
                (gate_shape, F32),
                (gate_shape, F32),
                (gate_shape, F32),
                (slim, F32),
                (state_shape, F32),
                (state_shape, F32),
                (gate_shape, F32),
                (gate_shape, F32),
                ((slots, 128), F32),
                (flat, BF),
                (raw, F32),
                ((flat[0], hd), BF),
                (tokens.shape, F32),
            ]
            + [(head, BF)] * 4
            + [(raw, F32)] * 4
            + [((4, 2) + block.shape, BF)]
            + [(ffn_shape, BF)] * 3
            + [(plane, BF)] * 2
            + [((8, width), F32)],
            [True] * 12 + [False] * 18 + [True],
            [vmem((streams, 4, count, width), BF), vmem(flat, BF), vmem(state_shape, F32)]
            + [vmem(head, BF)] * 4
            + [vmem(raw, F32)] * 4
            + [vmem(cut, BF)] * 3
            + scan_buffers(state_shape, slim)
            + [
                vmem((4, 2) + block.shape, BF),
                vmem(raw, F32),
                vmem((flat[0], hd), BF),
                vmem((flat[0], hd), BF),
                vmem(mixed_shape, BF),
                vmem(tokens.shape, F32),
                vmem(tokens.shape, BF),
            ]
            + rows_buffers(mixed_shape)
            + [vmem(tokens.shape, BF)],
            150,
            50,
            mb=63,
            pace=STEADY,
        )
        pack, lines, low_rank, logits, keep, written = outs[:6]
        survive, slots_in, slots_end, scores, share = outs[6:11]
        self.ranks, normed, reading, branch, self.hidden_rows = outs[11:16]
        self.down, self.gate, self.up = outs[25:28]
        self.cot, self.ffn_in, self.gains = outs[28:31]
        self.low_rank, self.pack, self.survive = low_rank, pack, survive
        return Mixer(
            reading=reading,
            scores=scores,
            share=share,
            branch=branch,
            normed=normed,
            logits=logits,
            keep=keep,
            written=written,
            slots_in=slots_in,
            slots_end=slots_end,
            weights=list(outs[16:20]),
            raw=list(outs[20:24]),
            output=outs[24].reshape(8 * block.shape[0], width),
        )

    def feed_forward(self, tokens, gain, cotangent):
        streams, count, width = tokens.shape
        plane = (2, 2, 4, count, width)
        half = plane[1:]
        ffn = self.down.shape
        cols = ffn[-1]
        many = 4 * count
        group = (2, 2, many, cols)
        z_line = [(z, y) for z in (3, 1, 2, 0) for y in range(2)]
        side = ffn[2]

        def work(place, wire, given, outs, scratch):
            hidden, gains, cot, rows_in, gate_in, up_in, cot_in, down_in = given
            grad_hidden, gain_sum, rows_out, gate_out, up_out, down_out, result_out = outs
            ffn_in, turned, part, up_grad, gate, up, grad_gate, grad_up, gate_grad = scratch[:9]
            act, cot_rows, down, tile, block = scratch[9:14]
            plane_bufs, gate_bufs = scratch[14:19], scratch[19:]
            loaded = Flags()
            for c in range(2):
                for h in range(2):
                    loaded.raised((c, h), [wire.keep(rows_in.at[c, h], ffn_in.at[c, h])])
                    if (c, h) == (0, 0):
                        loaded.raised(Key.gate, [wire.keep(gate_in, gate)])
                        loaded.raised(Key.up, [wire.keep(up_in, up)])
            loaded.raised(Key.cot, [wire.keep(cot_in, cot_rows)])
            gain_sum[...] = jnp.zeros_like(gain_sum)

            made, gate_made = Flags(), Flags()

            def down_rows():
                yield from last_spread(place, wire, down_in, down)
                loaded.raised(Key.down)

            def rows_of(ref, c, h):
                return ref[c, h].reshape(many, width)

            def weight(ref):
                return ref[...].reshape(width, cols)

            def compute():
                groups = [(c, h) for c in range(2) for h in range(2)]

                def columns(key):
                    at = (key[0] * 2 + key[1]) * side
                    return ffn_in[:, :, :, :, at : at + side].reshape(4 * many, side)

                def put(key, value):
                    gate_grad[key[0], key[1]] = value.astype(BF)

                def gate_rows():
                    return grad_gate[...].reshape(4 * many, cols)

                for c, h in groups:
                    yield loaded.wait((c, h), Key.gate, Key.up)
                    x = rows_of(ffn_in, c, h)
                    grad_gate[c, h] = mm(x, weight(gate), NN).astype(BF)
                    act[c, h] = mm(x, weight(up), NN).astype(BF)
                    wire.spend(3.2)
                yield loaded.wait(Key.cot, Key.down)
                for c, h in groups:
                    yield []
                    grad = mm(rows_of(cot_rows, c, h), weight(down), NN)
                    gate_pre = grad_gate[c, h].astype(F32)
                    up_pre = act[c, h].astype(F32)
                    sig = jax.nn.sigmoid(gate_pre)
                    act[c, h] = (gate_pre * sig * up_pre).astype(BF)
                    slope = sig * (1.0 + gate_pre * (1.0 - sig))
                    grad_gate[c, h] = (grad * up_pre * slope).astype(BF)
                    grad_up[c, h] = (grad * gate_pre * sig).astype(BF)
                    wire.spend(2.3)
                yield from weight_tiles(wire, columns, z_line[:2], gate_rows, put, gate_made)
                for c in (1, 0):
                    for h in range(2):
                        yield []
                        total = mm(grad_gate[c, h], weight(gate), NT)
                        total = total + mm(grad_up[c, h], weight(up), NT)
                        part[c, h] = total.astype(BF).reshape(half[1:])
                        wire.spend(3.0)
                        made.raised(((Key.near, Key.far)[c], h))

                yield from weight_tiles(wire, columns, z_line[2:], gate_rows, put, gate_made)

                def put_up(key, value):
                    up_grad[key[0], key[1]] = value.astype(BF)
                    wire.keep(up_grad.at[key[0], key[1]], up_out.at[key[0], key[1]])

                def up_rows_all():
                    return grad_up[...].reshape(4 * many, cols)

                yield from weight_tiles(wire, columns, z_line, up_rows_all, put_up)
                busy = {}

                def cot_columns(key):
                    at = (key[0] * 2 + key[1]) * side
                    return cot_rows[:, :, :, :, at : at + side].reshape(4 * many, side)

                def put_down(key, value):
                    slot = key[1]
                    wire.arrived(*busy.get(slot, ()))
                    tile[slot] = value.astype(BF)
                    busy[slot] = [wire.keep(tile.at[slot], down_out.at[key[0], key[1]])]

                def act_rows():
                    return act[...].reshape(4 * many, cols)

                yield from weight_tiles(wire, cot_columns, z_line, act_rows, put_down)
                for c in (1, 0):
                    for h in range(2):
                        yield []
                        wire.arrived(*busy.get(Key.block, ()))
                        total = mm(act[c, h], weight(down), NT)
                        block[...] = total.astype(BF).reshape(half[1:])
                        busy[Key.block] = [wire.keep(block, result_out.at[c, h])]
                        wire.spend(2.0)

            def finish_grad(stream, rows, load):
                part = z_parts(place, load, width)
                held = hidden[stream, rows]
                scale = inverse_rms(held)
                gain_sum[...] += jnp.sum(part * held * scale, axis=0, keepdims=True)
                total = cot[stream, rows].astype(F32) + norm_back(held, scale, gains[1:2], part)
                grad_hidden[stream, rows] = total
                turned[stream, rows] = total.astype(BF)

            def back_rows():
                yield from plane_fold(
                    place, wire, part.at[0], part.at[1], plane_bufs, finish_grad, made
                )

            def back_stream(h):
                here = pl.ds(h, 1)
                yield made.wait((Key.done, h))
                yield from rows_gather(place, wire, turned.at[here], rows_out.at[here])

            wire.run(
                down_rows(),
                back_stream(0),
                back_stream(1),
                back_rows(),
                ffn_fold(place, wire, gate_grad, gate_bufs, gate_out, gate_made),
                compute(),
            )

        vmem = pltpu.VMEM
        outs = comm_call(
            work,
            3,
            (CORE, X, Y, NEAR, FAR),
            [self.hidden_rows, self.gains, cotangent, self.ffn_in]
            + [self.gate, self.up, self.cot, self.down],
            [True] * 3 + [False] * 5,
            [
                ((streams, count, width), F32),
                ((1, width), F32),
                ((streams, 4, count, width), BF),
                (ffn[1:], BF),
                (ffn, BF),
                (ffn, BF),
                (plane, BF),
            ],
            [True] * 2 + [False] * 5,
            [
                vmem(plane, BF),
                vmem((streams, count, width), BF),
                vmem(plane, BF),
                vmem(ffn, BF),
                vmem(ffn, BF),
                vmem(ffn, BF),
                vmem(group, BF),
                vmem(group, BF),
                vmem(ffn, BF),
                vmem(group, BF),
                vmem(plane, BF),
                vmem(ffn, BF),
                vmem((2,) + ffn[2:], BF),
                vmem(half[1:], BF),
            ]
            + plane_buffers(half)
            + ffn_buffers(ffn),
            60,
            40,
            mb=63,
            pace=KEEN,
        )
        grad_hidden, gain_grad, rows, self.gate_grad = outs[:4]
        self.up_part, self.down_part, self.result_part = outs[4:]
        rows = rows.reshape(streams, 4 * count, width)
        return grad_hidden.reshape(streams * count, width), gain_grad[0], rows

    def own_streams(self, values):
        return values

    def mixer_order(self, values):
        lead, width = values.shape[:-1], values.shape[-1]
        parts = jnp.swapaxes(values.reshape(lead + (4, 2, width // 8)), -3, -2)
        return z_relative(parts, self.at.z, len(lead) + 1).reshape(lead + (width,))

    def mixer_unorder(self, values):
        lead, width = values.shape[:-1], values.shape[-1]
        parts = z_relative(values.reshape(lead + (2, 4, width // 8)), self.at.z, len(lead) + 1)
        return jnp.swapaxes(parts, -3, -2).reshape(lead + (width,))

    def ffn_order(self, values):
        return z_relative(values, self.at.z, values.ndim - 1)

    def mixer_back(self, mixer, grad_mixed):
        reading, scores, share, branch_out = mixer.reading, mixer.scores, mixer.share, mixer.branch
        streams, length, hd = reading.shape
        rows, width = grad_mixed.shape
        slots = scores.shape[1]
        state_shape, slim = (streams, slots, 2 * hd), (streams, slots, 128)
        ffn = self.up_part.shape
        line = (4, 2, hd // 8, width)
        head = (2, 4, width // 8, hd)
        own = (head[2] // 4, width)
        raw, gate_shape = (streams, length, hd), (streams, slots, length)
        key_raw, value_raw, query_raw, gate_raw = mixer.raw

        def work(place, wire, given, outs, scratch):
            grad_mixed, output_w, survive, gains = given[:4]
            out_gain = gains.at[0:1, :hd]
            after, gain_sum, grad_query, grad_gate, grad_k, grad_v, back, own_flow = outs[:8]
            up_out, output_out, query_out, gate_out, part_out = outs[8:]
            loads = {
                key: (source, target)
                for key, source, target in zip(
                    (Key.reading, Key.gate, Key.query, Key.key, Key.value, Key.keep, Key.written)
                    + (Key.scores, Key.share, Key.slots, Key.branch, Key.normed, Key.up)
                    + (Key.query_w, Key.gate_w),
                    given[4:],
                    scratch,
                )
            }
            here, up_made, lines_made = Flags(), Flags(), Flags()
            heads_made = [Flags(), Flags()]

            def load(*keys):
                for key in keys:
                    here.raised(key, [wire.keep(*loads[key])])

            kept = {key: pair[1] for key, pair in loads.items()}
            sent, got, grad_read, direct, output_part, query_part, gate_part = scratch[15:22]
            scan, up_bufs = scratch[22:26], scratch[26:29]
            lines, query_bufs, gate_bufs = scratch[29:33], scratch[33:37], scratch[37:41]
            normed_part = scratch[41]
            load(Key.up, Key.branch, Key.reading, Key.gate, Key.normed, Key.query, Key.key, Key.value)
            load(Key.keep, Key.written, Key.scores, Key.share, Key.slots, Key.query_w, Key.gate_w)
            gain_sum[...] = jnp.zeros_like(gain_sum)

            def returned():
                yield here.wait(Key.sent)
                yield from heads_return(place, wire, sent, got)
                here.raised(Key.got)

            def scanned():
                yield here.wait(Key.direct)
                yield from pieces_scan(place, wire, True, survive, direct, after, scan)

            def up_rows():
                yield here.wait(Key.up)
                yield from ffn_fold(place, wire, kept[Key.up], up_bufs, up_out)

            def gated(s):
                def chunk(part):
                    at = pl.ds(pl.multiple_of(s * length + part.start, 16), part.size)
                    values, opened = kept[Key.reading][s, part], kept[Key.gate][s, part]
                    grad = by_tp(got[at].astype(F32), (4, 2), hd // 8)
                    scale = inverse_rms(values)
                    normed = values * scale * out_gain[...]
                    grad_gate[s, part] = (grad * normed * silu_slope(opened)).astype(BF)
                    grad = grad * silu(opened)
                    gain_sum[...] += jnp.sum(grad * values * scale, axis=0, keepdims=True)
                    grad_read[s, part] = norm_back(values, scale, out_gain[...], grad)

                row_loop(length, 32, chunk)

            def streams_back(s, carry):
                results = piece_back(
                    *[kept[key][s] for key in (Key.query, Key.key, Key.value, Key.keep, Key.written)],
                    *[kept[key][s] for key in (Key.slots, Key.scores, Key.share)],
                    grad_read[s],
                )
                targets = (grad_query, grad_k, grad_v, direct, back, own_flow)
                for target, result in zip(targets, results):
                    target[s] = result.astype(target.dtype)
                return carry

            def compute():
                half = rows // 2
                for at in (0, half):
                    part = mm(grad_mixed[at : at + half], output_w[...], NT)
                    sent[at : at + half] = part.astype(BF)
                wire.spend(3.0)
                here.raised(Key.sent)
                yield here.wait(Key.branch)
                block = hd // 4
                for m in (3, 1, 2, 0):
                    yield []
                    cols = kept[Key.branch][:, m * block : (m + 1) * block]
                    total = mm(cols, grad_mixed[...], TN)
                    output_part[m] = total.astype(BF).reshape(line[1:])
                    wire.spend(1.2)
                    lines_made.raised(m)
                yield here.wait(Key.got, Key.reading, Key.gate)
                for s in range(streams):
                    gated(s)
                wire.spend(2.0)
                yield here.wait(Key.normed)
                yield from head_tiles(
                    wire,
                    kept[Key.normed],
                    lambda: grad_gate[...].reshape(rows, hd),
                    gate_part,
                    heads_made[1],
                )
                yield here.wait(Key.query, Key.key, Key.value, Key.keep, Key.written, Key.scores, Key.share, Key.slots)
                lax.fori_loop(0, streams, streams_back, 0)
                wire.spend(13.0)
                here.raised(Key.direct)
                yield from head_tiles(
                    wire,
                    kept[Key.normed],
                    lambda: grad_query[...].reshape(rows, hd),
                    query_part,
                    heads_made[0],
                )
                yield here.wait(Key.query_w, Key.gate_w)
                for s in range(streams):
                    yield []
                    total = mm(grad_query[s], kept[Key.query_w][...], NT)
                    total = total + mm(grad_gate[s], kept[Key.gate_w][...], NT)
                    normed_part[s] = total.astype(BF)
                    wire.keep(normed_part.at[s], part_out.at[s])
                    wire.spend(2.5)

            wire.run(
                returned(),
                scanned(),
                up_rows(),
                output_fold(place, wire, output_part, lines, output_out, lines_made),
                head_fold(place, wire, gate_part, gate_bufs, gate_out, heads_made[1]),
                head_fold(place, wire, query_part, query_bufs, query_out, heads_made[0]),
                compute(),
            )

        vmem = pltpu.VMEM
        later = [
            reading,
            gate_raw,
            query_raw,
            key_raw,
            value_raw,
            mixer.keep,
            mixer.written,
            scores,
            share,
            mixer.slots_in,
            branch_out,
            mixer.normed,
            self.up_part,
            mixer.weights[2],
            mixer.weights[3],
        ]
        outs = comm_call(
            work,
            7,
            (CORE, X, X | CORE, Y, NEAR, FAR),
            [grad_mixed, mixer.output, self.survive, self.gains] + later,
            [True] * 4 + [False] * len(later),
            [
                (state_shape, F32),
                ((1, hd), F32),
                (raw, BF),
                (raw, BF),
                (raw, BF),
                (raw, BF),
                (gate_shape, F32),
                (gate_shape, F32),
                (ffn[1:], BF),
                (line[2:], BF),
                (own, BF),
                (own, BF),
                ((streams, length, width), BF),
            ],
            [True] * 8 + [False] * 5,
            [vmem(a.shape, a.dtype) for a in later]
            + [
                vmem((rows, hd), BF),
                vmem((rows, hd), BF),
                vmem(raw, F32),
                vmem(state_shape, F32),
                vmem(line, BF),
                vmem(head, BF),
                vmem(head, BF),
            ]
            + scan_buffers(state_shape, slim)
            + ffn_buffers(ffn)
            + line_buffers(line[2], line[3])
            + line_buffers(head[2], head[3])
            + line_buffers(head[2], head[3])
            + [vmem((streams, length, width), BF)],
            60,
            30,
            mb=63,
            pace=EARLY,
        )
        self.up_grad, output_sum, query_sum, gate_sum, self.normed_part = outs[8:]
        self.output_sum = output_sum
        self.head_sums = [query_sum, gate_sum]
        return outs[:8]

    def finish(self, mixer, back, tokens, grad_hidden, ffn_gain_grad, small):
        after, out_gain_grad, unused, unused, grad_k, grad_v, pulled, flow = back
        streams, count, width = tokens.shape
        slots, length = flow.shape[1:]
        rank, hd = small[0].shape[1], grad_k.shape[-1]
        rows = streams * length
        part_shape = (streams, 2, 2, count, width)
        head = (2, 4, width // 8, hd)
        own = (head[2] // 4, width)
        plane, ffn = self.cot.shape, self.down.shape
        half = plane[1:]
        raw = (streams, length, hd)
        sheet = (24, width + H * slots)
        key_raw, value_raw = mixer.raw[:2]

        def work(place, wire, given, outs, scratch):
            after, slots_end, keep, written, pulled, flow, logits = given[:7]
            low, ranks, gains, tokens, hidden, ffn_sum, out_sum = given[7:14]
            result_in, down_in, hidden_grad = given[14:17]
            far_in = result_in.at[1]
            grad_tokens, result, total_out, key_out, value_out, down_out = outs
            names = (Key.key, Key.value, Key.grad_k, Key.grad_v, Key.normed, Key.part, Key.key_w, Key.value_w)
            names = names + (Key.pack,)
            loads = dict(zip(names, zip(given[17:], scratch)))
            loads[Key.near] = (result_in.at[0], scratch[9])
            loads[Key.down] = (down_in.at[0], scratch[10].at[0])
            kept = {key: pair[1] for key, pair in loads.items()}
            kept[Key.down] = scratch[10]
            grads, parts, grad_f = scratch[11:13], scratch[13:15], scratch[15]
            normed_part, sums, tidy = scratch[16], scratch[17:20], scratch[20]
            lines = [scratch[21:25], scratch[25:29]]
            plane_bufs, fold_bufs = scratch[29:34], scratch[34:37]
            sheets, got_sheets, far_row = scratch[37], scratch[38], scratch[39]
            here, made = Flags(), Flags()
            heads_made = [Flags(), Flags()]
            for key in (Key.down, Key.key, Key.value, Key.grad_k, Key.grad_v, Key.normed, Key.near, Key.part):
                here.raised(key, [wire.keep(*loads[key])])
            for key in (Key.pack, Key.key_w, Key.value_w):
                here.raised(key, [wire.keep(*loads[key])])
            here.raised(Key.hidden_grad, [wire.keep(hidden_grad, grad_tokens)])
            here.raised(Key.down_2, [wire.keep(down_in.at[2], scratch[10].at[1])])
            made.raised((Key.far, 0))
            made.raised((Key.far, 1))

            def down_rows():
                yield here.wait(Key.down, Key.down_2)
                yield from ffn_fold(
                    place, wire, down_in, fold_bufs, down_out, None, kept[Key.down]
                )

            def result_rows():
                yield here.wait(Key.near)
                made.raised((Key.near, 0))
                made.raised((Key.near, 1))
                yield from plane_fold(
                    place, wire, kept[Key.near], far_in, plane_bufs, finish_result, made
                )

            def finish_result(stream, rows, load):
                total = hidden[stream, rows] + z_parts(place, load, width)
                result[stream, rows] = total.astype(BF)

            def finish_tokens(stream, rows, total):
                side = width // 8
                for y in range(2):
                    for m in range(4):
                        to = pl.multiple_of((place.z_turn(m) * 2 + y) * side, 128)
                        at = (y * 4 + m) * side
                        tidy[:, pl.ds(to, side)] = total[:, at : at + side]
                x = tokens[stream, rows].astype(F32)
                grad = norm_back(x, inverse_rms(x), gains[3:4], tidy[...])
                grad_tokens[stream, rows] += grad

            def token_rows():
                yield here.wait(Key.normed_part, Key.hidden_grad)
                yield from rows_fold(place, wire, normed_part, *sums, finish_tokens)

            def all_sums():
                yield here.wait(Key.sheet)
                total = sheets.at[0]
                for step, mask in enumerate((CORE, X, Y, NEAR, FAR)):
                    yield [wire.send(total, got_sheets.at[step], mask)]
                    got_sheets[step] += total[...]
                    total = got_sheets.at[step]
                total_out[...] = total[...]

            def ending(s, carry):
                results = piece_after(
                    *[kept[key][s] for key in (Key.key, Key.value)],
                    *[ref[s] for ref in (keep, written)],
                    *[kept[key][s] for key in (Key.grad_k, Key.grad_v)],
                    *[ref[s] for ref in (pulled, flow, after, slots_end)],
                )
                for target, value in zip((grads[0], grads[1], grad_f), results):
                    target[s] = value.astype(target.dtype)
                grad_f[s] = grad_f[s] * jax.nn.sigmoid(-logits[s]) / GATE_SCALE
                return carry

            def unorder(target_row, count, values):
                side = width // 8
                for y in range(2):
                    for m in range(4):
                        to = pl.multiple_of((place.z_turn(m) * 2 + y) * side, 128)
                        at = (y * 4 + m) * side
                        there = (0, slice(target_row, target_row + count), pl.ds(to, side))
                        sheets[there] = values[:, at : at + side]

            def compute():
                yield here.wait(Key.key, Key.value, Key.grad_k, Key.grad_v)
                lax.fori_loop(0, streams, ending, 0)
                wire.spend(6.0)
                yield here.wait(Key.normed)
                for index in range(2):
                    yield from head_tiles(
                        wire,
                        kept[Key.normed],
                        lambda: grads[index][...].reshape(rows, hd),
                        parts[index],
                        heads_made[index],
                    )
                yield here.wait(Key.part, Key.pack, Key.key_w, Key.value_w)
                sheets[0] = jnp.zeros(sheet, F32)
                far_row[...] = jnp.zeros_like(far_row)
                low_sum, rank_sum, bias_sum = 0.0, 0.0, 0.0
                for s in range(streams):
                    normed = kept[Key.normed][s * length : (s + 1) * length]
                    f = grad_f[s]
                    low_grad = mm_fine(f, ranks[...], TN)
                    total = kept[Key.part][s].astype(F32)
                    total = total + mm(grads[0][s], kept[Key.key_w][...], NT)
                    total = total + mm(grads[1][s], kept[Key.value_w][...], NT)
                    total = total + mm(low_grad, kept[Key.pack][...], NT)
                    normed_part[s] = total.astype(BF).reshape(part_shape[1:])
                    far_row[...] += jnp.sum(total * normed.astype(F32), axis=0, keepdims=True)
                    wire.spend(4.0)
                    yield []
                    low_sum = low_sum + mm_fine(low_grad, normed, TN)
                    rank_sum = rank_sum + mm_fine(f, low[s], NN)
                    bias_sum = bias_sum + jnp.sum(f, axis=1, keepdims=True)
                    wire.spend(2.0)
                here.raised(Key.normed_part)
                wide = (slots, H * slots)
                spot = column(wide) - place.tp * slots
                spread = jnp.where(row(wide) == spot, 1.0, 0.0)
                unorder(0, rank, low_sum[:rank])
                unorder(16, 1, far_row[...] / gains[2:3])
                sheets[0, 0:rank, width:] = mm_fine(rank_sum, spread, TN)[:rank]
                bias_sum = jnp.broadcast_to(bias_sum, (slots, 128))
                sheets[0, 16:17, width:] = mm_fine(bias_sum, spread, TN)[:1]
                sheets[0, 17:18, :width] = ffn_sum[...]
                sheets[0, 18:19, :hd] = out_sum[...]
                here.raised(Key.sheet)

            wire.run(
                token_rows(),
                all_sums(),
                head_fold(place, wire, parts[0], lines[0], key_out, heads_made[0]),
                head_fold(place, wire, parts[1], lines[1], value_out, heads_made[1]),
                down_rows(),
                result_rows(),
                compute(),
            )

        vmem = pltpu.VMEM
        soon = [after, mixer.slots_end, mixer.keep, mixer.written, pulled, flow]
        soon = soon + [mixer.logits, self.low_rank, self.ranks, self.gains, tokens]
        soon = soon + [self.hidden_rows]
        soon = soon + [ffn_gain_grad[None], out_gain_grad]
        later = [key_raw, value_raw, grad_k, grad_v, mixer.normed, self.normed_part]
        later = later + [mixer.weights[0], mixer.weights[1], self.pack]
        aside = [self.result_part, self.down_part, grad_hidden.reshape(tokens.shape)]
        grad_tokens, result, total, key_sum, value_sum, down_grad = comm_call(
            work,
            8,
            (CORE, X, X | CORE, Y, NEAR, FAR),
            soon + aside + later,
            [True] * len(soon) + [False] * (len(aside) + len(later)),
            [
                (tokens.shape, F32),
                (tokens.shape, BF),
                (sheet, F32),
                (own, BF),
                (own, BF),
                (ffn[1:], BF),
            ],
            [True] * 3 + [False] * 3,
            [vmem(a.shape, a.dtype) for a in later]
            + [vmem(half, BF), vmem((2,) + ffn[1:], BF)]
            + [vmem(raw, BF)] * 2
            + [vmem(head, BF)] * 2
            + [vmem((streams, slots, length), F32), vmem(part_shape, BF)]
            + rows_buffers(part_shape)
            + [vmem((16, width), F32)]
            + line_buffers(head[2], head[3])
            + line_buffers(head[2], head[3])
            + plane_buffers(half)
            + ffn_buffers(ffn)
            + [vmem((1,) + sheet, F32), vmem((5,) + sheet, F32), vmem((1, width), F32)],
            80,
            20,
            mb=63.5,
        )
        heads = [h.astype(F32) for h in [key_sum, value_sum] + self.head_sums + [self.output_sum]]

        def both(parts):
            return jnp.concatenate([parts[0], parts[1]], axis=1).astype(F32)

        ffn_grads = [both(g) for g in (self.gate_grad, self.up_grad, down_grad)]
        seq, tp = lax.axis_index(SEQ), lax.axis_index(TP)

        def share_of(values, size):
            return lax.dynamic_slice_in_dim(values, (seq * 4 + tp) * size, size, 1)

        w_low, w_rank, bias, attn_gain, out_gain, ffn_gain = small
        in_low = share_of(total[:, :width], w_low.shape[0])
        in_rank = share_of(total[:, width:], w_rank.shape[0])
        small_grads = (
            jnp.swapaxes(in_low[:rank], 0, 1),
            jnp.swapaxes(in_rank[:rank], 0, 1),
            in_rank[16],
            in_low[16],
            share_of(total[18:19, :hd], out_gain.shape[0])[0],
            in_low[17],
        )
        return heads, ffn_grads, grad_tokens, result, small_grads


def on_device(
    tokens,
    seq_cuts,
    w_query,
    w_key,
    w_value,
    w_gate_out,
    w_output,
    w_low,
    w_rank,
    gate_bias,
    attn_gain,
    out_gain,
    ffn_gain,
    w_gate,
    w_up,
    w_down,
    cotangent,
):
    sizes = lax.axis_size(SEQ), lax.axis_size(TP)
    move = BitMoves() if sizes == (8, 4) else PlainMoves()
    small = (w_low, w_rank, gate_bias, attn_gain, out_gain, ffn_gain)
    mixer = move.start(
        tokens,
        seq_cuts,
        (w_key, w_value, w_query, w_gate_out),
        w_output,
        small,
        (w_down, w_gate, w_up),
        cotangent,
    )
    grad_hidden, grad_ffn_gain, grad_mixed = move.feed_forward(
        tokens, mixer.ffn_gain, cotangent
    )
    back = move.mixer_back(mixer, grad_mixed.reshape(-1, tokens.shape[-1]))
    heads, ffn_grads, grad_tokens, result, small_grads = move.finish(
        mixer, back, tokens, grad_hidden, grad_ffn_gain, small
    )
    grad_w_key, grad_w_value, grad_w_query, grad_w_gate_out, grad_w_output = heads
    return (
        (result.reshape(tokens.shape), grad_tokens)
        + (grad_w_query, grad_w_key, grad_w_value, grad_w_gate_out, grad_w_output)
        + tuple(small_grads)
        + tuple(ffn_grads)
    )


def solution(mesh):
    both, row_split, line = (SEQ, TP), P((SEQ, TP), None), P((SEQ, TP))
    tokens_at, ffn_at = P(None, both, None), P(SEQ, TP)
    params = (row_split,) * 7 + (line,) * 4 + (ffn_at,) * 3
    return jax.shard_map(
        on_device,
        mesh=mesh,
        in_specs=(tokens_at, P()) + params + (tokens_at,),
        out_specs=(tokens_at, tokens_at) + params,
        check_vma=False,
    )
```

```python
import dataclasses
import math

import jax
import jax.numpy as jnp
from jax import lax
from jax.experimental import pallas as pl
from jax.experimental.pallas import tpu as pltpu
from jax.sharding import PartitionSpec as P

SEQ, TP = "seq", "tp"


class Key:
    x, y, side, middle, core, remote = range(100, 106)
    local, far, near, done, rows, lines = range(106, 112)
    raw, branch, traded, mixed, trade, pack = range(112, 118)
    state, slots, gate, up, cot, down = range(118, 124)
    block, reading, query, key, value, keep = range(124, 130)
    written, scores, share, normed, query_w, gate_w = range(130, 136)
    sent, got, direct, grad_k, grad_v, part = range(136, 142)
    key_w, value_w, hidden_grad, down_2, normed_part, sheet = range(142, 148)


H = 4
GATE_SCALE = 8.0
EPSILON = 1e-05
BF = jnp.bfloat16
F32 = jnp.float32
CHUNK = 128
SUB = 16
HALVES = (16, 32, 64)


def mm(left, right, dims):
    return lax.dot_general(
        left.astype(BF), right.astype(BF), (dims, ((), ())), preferred_element_type=F32
    )


def mm_fine(left, right, dims):
    left_hi, right_hi = left.astype(BF), right.astype(BF)
    left_lo = (left - left_hi.astype(F32)).astype(BF)
    right_lo = (right - right_hi.astype(F32)).astype(BF)

    def part(a, b):
        return lax.dot_general(a, b, (dims, ((), ())), preferred_element_type=F32)

    return part(left_hi, right_hi) + (part(left_hi, right_lo) + part(left_lo, right_hi))


NN = ((1,), (0,))
NT = ((1,), (1,))
TN = ((0,), (0,))


def turn(values, amount):
    return pltpu.roll(values, amount % values.shape[1], 1)


def column(shape):
    return lax.broadcasted_iota(jnp.int32, shape, 1)


def row(shape):
    return lax.broadcasted_iota(jnp.int32, shape, 0)


def ahead_product(keep, size):
    place = column(keep.shape) & (size - 1)
    total, step = keep, 1
    while step < size:
        total = total * jnp.where(place >= step, turn(total, step), 1.0)
        step *= 2
    return total


def behind_product(keep, size):
    place = column(keep.shape) & (size - 1)
    total = jnp.where(place == size - 1, 1.0, turn(keep, -1))
    step = 1
    while step < size:
        total = total * jnp.where(place < size - step, turn(total, -step), 1.0)
        step *= 2
    return total


def chunks_of(values):
    return [values[:, at : at + CHUNK] for at in range(0, values.shape[1], CHUNK)]


def rows_of(values):
    return [values[at : at + CHUNK] for at in range(0, values.shape[0], CHUNK)]


class Decays:
    def __init__(self, keep):
        self.keep = chunks_of(keep)
        self.count = len(self.keep)
        self.ahead = [ahead_product(k, CHUNK) for k in self.keep]
        self.behind = [behind_product(k, CHUNK) for k in self.keep]
        self.total = [a[:, CHUNK - 1 :] for a in self.ahead]

    def levels(self):
        self.ahead_in = [{h: ahead_product(k, h) for h in HALVES} for k in self.keep]
        self.behind_in = [{h: behind_product(k, h) for h in HALVES} for k in self.keep]
        inside = (column(self.keep[0].shape) & (SUB - 1)) != 0
        self.short = [jnp.where(inside, k, 0.0) for k in self.keep]

    def from_start(self, c):
        out = self.ahead[c]
        for earlier in range(c):
            out = out * self.total[earlier]
        return out

    def to_end(self, c):
        out = self.behind[c]
        for later in range(c + 1, self.count):
            out = out * self.total[later]
        return out

    def to_chunk(self, c):
        parts = []
        for earlier in range(c):
            out = self.behind[earlier]
            for between in range(earlier + 1, c):
                out = out * self.total[between]
            parts.append(out)
        return parts

    def survive(self):
        out = self.total[0]
        for t in self.total[1:]:
            out = out * t
        return out


def level_mask(half):
    shape = (CHUNK, CHUNK)
    source, target = row(shape) // half, column(shape) // half
    return ((source & 1) == 0) & (target == source + 1)


def diagonals(square):
    shape = (SUB, CHUNK)
    group = column(shape) // SUB
    out = jnp.zeros(shape, F32)
    for b in range(CHUNK // SUB):
        out = out + jnp.where(group == b, square[b * SUB : (b + 1) * SUB], 0.0)
    return out


def at_lag(compact, lag):
    shape = (SUB, CHUNK)
    hit = row(shape) == (column(shape) & (SUB - 1)) - lag
    return jnp.sum(jnp.where(hit, compact, 0.0), axis=0, keepdims=True)


def undiagonal(lagged):
    shape = (SUB, CHUNK)
    place = (column(shape) & (SUB - 1)) - row(shape)
    compact = jnp.zeros(shape, F32)
    for lag, values in enumerate(lagged):
        compact = jnp.where(place == lag, values, compact)
    group = column(shape) // SUB
    return jnp.concatenate(
        [jnp.where(group == b, compact, 0.0) for b in range(CHUNK // SUB)], axis=0
    )


def read_slots(decays, written, c, affinity, entering, dot):
    near = affinity[c * CHUNK :]
    out = decays.from_start(c) * entering
    if c > 0:
        far = jnp.concatenate(
            [b * w for b, w in zip(decays.to_chunk(c), written[:c])], axis=1
        )
        out = out + decays.ahead[c] * dot(far, affinity[: c * CHUNK], NN)
    for h in HALVES:
        part = dot(decays.behind_in[c][h] * written[c], jnp.where(level_mask(h), near, 0.0), NN)
        out = out + decays.ahead_in[c][h] * part
    compact = diagonals(near)
    weight = written[c]
    for lag in range(SUB):
        out = out + weight * at_lag(compact, lag)
        if lag + 1 < SUB:
            weight = decays.short[c] * turn(weight, 1)
    return out


def mix_sources(decays, written, c, shares):
    lagged = [[] for _ in shares]
    weight = written[c]
    for lag in range(SUB):
        for place, share in enumerate(shares):
            lagged[place].append(jnp.sum(weight * share, axis=0, keepdims=True))
        if lag + 1 < SUB:
            weight = decays.short[c] * turn(weight, 1)
    outs = []
    for place, share in enumerate(shares):
        near = undiagonal(lagged[place])
        for h in HALVES:
            part = mm(decays.behind_in[c][h] * written[c], decays.ahead_in[c][h] * share, TN)
            near = near + jnp.where(level_mask(h), part, 0.0)
        if c > 0:
            far = jnp.concatenate(
                [b * w for b, w in zip(decays.to_chunk(c), written[:c])], axis=1
            )
            near = jnp.concatenate([mm(far, decays.ahead[c] * share, TN), near], axis=0)
        outs.append(near)
    return outs


def gather_back(decays, c, shares, affinities):
    outs = []
    if c > 0:
        pulled = sum(
            mm_fine(decays.ahead[c] * s, a[: c * CHUNK], NT) for s, a in zip(shares, affinities)
        )
        outs = [b * p for b, p in zip(decays.to_chunk(c), chunks_of(pulled))]
    nears = [a[c * CHUNK :] for a in affinities]
    own = 0.0
    for h in HALVES:
        mask = level_mask(h)
        pulled = sum(
            mm_fine(decays.ahead_in[c][h] * s, jnp.where(mask, a, 0.0), NT)
            for s, a in zip(shares, nears)
        )
        own = own + decays.behind_in[c][h] * pulled
    compacts = [diagonals(a) for a in nears]
    held = 0.0
    for lag in range(SUB - 1, -1, -1):
        if lag < SUB - 1:
            held = turn(decays.short[c] * held, -1)
        for s, a in zip(shares, compacts):
            held = held + s * at_lag(a, lag)
    outs.append(own + held)
    return outs


def silu(x):
    return x * jax.nn.sigmoid(x)


def silu_slope(x):
    sig = jax.nn.sigmoid(x)
    return sig * (1.0 + x * (1.0 - sig))


def gates(logits):
    small = jnp.exp(-jnp.abs(logits))
    ratio = small / (2.0 + small)
    square = ratio * ratio
    series = jnp.full_like(square, 1.0 / 17.0)
    for odd in (15, 13, 11, 9, 7, 5, 3, 1):
        series = series * square + 1.0 / odd
    log_keep = (jnp.minimum(logits, 0.0) - 2.0 * ratio * series) / GATE_SCALE
    keep = jnp.exp(log_keep)
    near = jnp.ones_like(log_keep)
    for order in (9, 8, 7, 6, 5, 4, 3, 2):
        near = 1.0 + log_keep / order * near
    return keep, jnp.where(log_keep > -0.5, -log_keep * near, 1.0 - keep)


def piece_state(key_raw, value_raw, keep, written):
    decays = Decays(keep)
    left = jnp.concatenate(
        [decays.to_end(c) * w for c, w in enumerate(chunks_of(written))], axis=1
    )
    keys, values = mm_fine(left, silu(key_raw), NN), mm_fine(left, silu(value_raw), NN)
    state = jnp.concatenate([keys, values], axis=1)
    return state, decays.survive()


def piece_read(query_raw, key_raw, value_raw, keep, written, slots_in):
    width = query_raw.shape[1]
    query, keys, values = silu(query_raw) * width**-0.5, silu(key_raw), silu(value_raw)
    slot_keys, slot_values = slots_in[:, :width], slots_in[:, width:]
    decays = Decays(keep)
    decays.levels()
    writes = chunks_of(written)
    entering = mm_fine(slot_keys, query, NT)
    readings, scores_all, shares = [], [], []
    for c in range(decays.count):
        last = (c + 1) * CHUNK
        affinity = mm_fine(keys[:last], query[c * CHUNK : last], NT)
        scores = read_slots(
            decays, writes, c, affinity, chunks_of(entering)[c], mm_fine
        )
        spread = jnp.exp(scores - jnp.max(scores, axis=0, keepdims=True))
        share = spread / jnp.sum(spread, axis=0, keepdims=True)
        (mixing,) = mix_sources(decays, writes, c, [share])
        reading = mm(mixing, values[:last], TN)
        reading = reading + mm(decays.from_start(c) * share, slot_values, TN)
        readings.append(reading)
        scores_all.append(scores)
        shares.append(share)
    return (
        jnp.concatenate(readings, axis=0),
        jnp.concatenate(scores_all, axis=1),
        jnp.concatenate(shares, axis=1),
    )


def add_chunks(total, extra):
    return [t + e for t, e in zip(total, extra)] + total[len(extra) :]


def piece_back(query_raw, key_raw, value_raw, keep, written, slots_in, scores, share, grad_read):
    width = query_raw.shape[1]
    query, keys, values = silu(query_raw) * width**-0.5, silu(key_raw), silu(value_raw)
    slot_keys, slot_values = slots_in[:, :width], slots_in[:, width:]
    decays = Decays(keep)
    decays.levels()
    writes = chunks_of(written)
    count = decays.count
    entering = chunks_of(mm_fine(slot_values, grad_read, NT))
    grad_q = []
    grad_k = [jnp.zeros((CHUNK, width), F32)] * count
    grad_v = [jnp.zeros((CHUNK, width), F32)] * count
    back = [jnp.zeros(writes[0].shape, F32)] * count
    direct_k, direct_v, own = 0.0, 0.0, []
    for c in range(count):
        last = (c + 1) * CHUNK
        here = slice(c * CHUNK, last)
        p = chunks_of(share)[c]
        affinity = mm_fine(keys[:last], query[here], NT)
        pull = mm_fine(values[:last], grad_read[here], NT)
        grad_p = read_slots(decays, writes, c, pull, entering[c], mm_fine)
        weighed = p * grad_p
        grad_s = weighed - p * jnp.sum(weighed, axis=0, keepdims=True)
        own.append(weighed + grad_s * chunks_of(scores)[c])
        mix_k, mix_v = mix_sources(decays, writes, c, [grad_s, p])
        from_start = decays.from_start(c)
        far_s, far_p = from_start * grad_s, from_start * p
        grad_q.append(mm(mix_k, keys[:last], TN) + mm(far_s, slot_keys, TN))
        grad_k = add_chunks(grad_k, rows_of(mm(mix_k, query[here], NN)))
        grad_v = add_chunks(grad_v, rows_of(mm(mix_v, grad_read[here], NN)))
        direct_k = direct_k + mm(far_s, query[here], NN)
        direct_v = direct_v + mm(far_p, grad_read[here], NN)
        back = add_chunks(back, gather_back(decays, c, [grad_s, p], [affinity, pull]))
    grad_query = jnp.concatenate(grad_q, axis=0) * width**-0.5 * silu_slope(query_raw)
    return (
        grad_query,
        jnp.concatenate(grad_k, axis=0),
        jnp.concatenate(grad_v, axis=0),
        jnp.concatenate([direct_k, direct_v], axis=1),
        jnp.concatenate(back, axis=1),
        jnp.concatenate(own, axis=1),
    )


def piece_after(
    key_raw, value_raw, keep, written, grad_k, grad_v, back, own, after, slots_end
):
    width = key_raw.shape[1]
    keys, values = silu(key_raw), silu(value_raw)
    decays = Decays(keep)
    writes = chunks_of(written)
    to_end = jnp.concatenate([decays.to_end(c) for c in range(decays.count)], axis=1)
    left = to_end * written
    grad_k = grad_k + mm(left, after[:, :width], TN)
    grad_v = grad_v + mm(left, after[:, width:], TN)
    pulled = mm_fine(after[:, :width], keys, NT)
    pulled = pulled + mm_fine(after[:, width:], values, NT)
    back = back + to_end * pulled
    flow = own - written * back
    held = jnp.sum(after * slots_end, axis=1, keepdims=True)
    parts = chunks_of(flow)
    outs = []
    for part in reversed(parts):
        place, total, step = column(part.shape), part, 1
        while step < CHUNK:
            total = total + jnp.where(place < CHUNK - step, turn(total, -step), 0.0)
            step *= 2
        outs.append(total + held)
        held = held + total[:, :1]
    grad_log = jnp.concatenate(outs[::-1], axis=1) - (1.0 - written) * back
    return grad_k * silu_slope(key_raw), grad_v * silu_slope(value_raw), grad_log


def tie(value, *after):
    if not after:
        return value

    def body(*refs):
        pass

    anywhere = pl.BlockSpec(memory_space=pl.ANY)
    return pl.pallas_call(
        body,
        in_specs=[anywhere] * (1 + len(after)),
        out_specs=anywhere,
        out_shape=jax.ShapeDtypeStruct(value.shape, value.dtype),
        input_output_aliases={0: 0},
        cost_estimate=pl.CostEstimate(flops=0, bytes_accessed=0, transcendentals=0),
    )(value, *after)


def per_stream(work, arrays, outs, flops):
    def body(*refs):
        results = work(*[ref[...] for ref in refs[: len(arrays)]])
        for ref, result in zip(refs[len(arrays) :], results):
            ref[...] = result.astype(ref.dtype)

    def whole(shape):
        return pl.BlockSpec((None,) + tuple(shape[1:]), lambda s: (s, 0, 0))

    streams = arrays[0].shape[0]
    outs = [jax.ShapeDtypeStruct((streams,) + shape, kind) for shape, kind in outs]
    return pl.pallas_call(
        body,
        grid=(streams,),
        in_specs=[whole(a.shape) for a in arrays],
        out_specs=[whole(o.shape) for o in outs],
        out_shape=outs,
        compiler_params=pltpu.CompilerParams(vmem_limit_bytes=40 * 1024 * 1024),
        cost_estimate=pl.CostEstimate(flops=flops, bytes_accessed=1 << 16, transcendentals=0),
    )(*arrays)


def inverse_rms(values):
    return lax.rsqrt(jnp.mean(values * values, axis=-1, keepdims=True) + EPSILON)


def norm_back(values, scale, gain, grad):
    pulled = gain * grad
    along = jnp.mean(values * pulled, axis=-1, keepdims=True)
    return scale * pulled - values * (scale * scale * scale) * along


def product(left, right, dims):
    return lax.dot_general(left, right, (dims, ((), ())), preferred_element_type=F32)


def chain(earlier, later):
    return (earlier[0] * later[0], later[0][..., None] * earlier[1] + later[1])


CORE, X, Y, NEAR, FAR = 1, 2, 4, 8, 16


class Place:
    def __init__(self):
        self.seq, self.tp = lax.axis_index(SEQ), lax.axis_index(TP)
        self.core, self.x = self.tp % 2, self.tp // 2
        self.y, self.z = self.seq % 2, self.seq // 2
        self.near, self.far = self.z % 2, self.z // 2
        self.flat = self.seq * 4 + self.tp

    def partner(self, mask):
        seq, tp = self.seq, self.tp
        if mask & CORE:
            tp = tp + 1 - 2 * self.core
        if mask & X:
            tp = tp + 2 - 4 * self.x
        if mask & Y:
            seq = seq + 1 - 2 * self.y
        if mask & NEAR:
            seq = seq + 2 - 4 * self.near
        if mask & FAR:
            seq = seq + 4 - 8 * self.far
        return seq, tp

    def z_turn(self, index):
        low, high = index % 2, index // 2
        low = low + self.near - 2 * low * self.near
        high = high + self.far - 2 * high * self.far
        return 2 * high + low


class Wire:
    def __init__(self, place, sends, receives, locals_, pace):
        latency, link, beside, self.AHEAD = pace
        self.LATENCY, self.LINK, self.BESIDE = latency, 2e-3 / link, 1e-3 / beside
        self.place, self.sends, self.receives, self.locals = place, sends, receives, locals_
        self.remote, self.near_by, self.seen = [], [], set()
        self.now, self.due, self.free, self.rank = 0.0, {}, {}, 0
        self.queues = {Key.x: [], Key.y: [], Key.side: [], Key.middle: []}

    def greet(self, masks):
        barrier = pltpu.get_barrier_semaphore()
        for mask in masks:
            pl.semaphore_signal(
                barrier,
                inc=1,
                device_id=self.place.partner(mask),
                device_id_type=pl.DeviceIdType.MESH,
            )
        pl.semaphore_wait(barrier, len(masks))

    def spend(self, time):
        self.now += time

    def issue(self, at):
        source, target, mask = self.remote[at]
        copy = pltpu.make_async_remote_copy(
            src_ref=source,
            dst_ref=target,
            send_sem=self.sends.at[at],
            recv_sem=self.receives.at[at],
            device_id=self.place.partner(mask),
            device_id_type=pl.DeviceIdType.MESH,
        )
        copy.start()
        self.remote[at] = copy
        size = math.prod(source.shape) * jnp.dtype(source.dtype).itemsize
        if mask == CORE:
            uses = ((Key.core, size * self.BESIDE),)
        elif mask & X:
            uses = ((Key.x, size * self.LINK),)
        elif mask == Y:
            uses = ((Key.y, size * self.LINK),)
        elif mask == NEAR:
            uses = ((Key.side, size * self.LINK),)
        else:
            uses = ((Key.side, size * self.LINK), (Key.middle, 2 * size * self.LINK))
        end = 0.0
        for link, time in uses:
            self.free[link] = max(self.now, self.free.get(link, 0.0)) + time
            end = max(end, self.free[link])
        self.due[Key.remote, at] = end + self.LATENCY

    def send(self, source, target, mask):
        at = len(self.remote)
        self.remote.append((source, target, mask))
        if mask == CORE:
            self.issue(at)
        else:
            link = {Y: Key.y, NEAR: Key.side, FAR: Key.middle}.get(mask, Key.x)
            self.queues[link].append((self.rank, at))
        return (Key.remote, at)

    def feed(self, until):
        fed = False
        for link, queue in self.queues.items():
            while queue and self.free.get(link, 0.0) < until + self.AHEAD:
                first = min(queue)
                queue.remove(first)
                self.issue(first[1])
                fed = True
        return fed

    def keep(self, source, target):
        at = len(self.near_by)
        copy = pltpu.make_async_copy(source, target, self.locals.at[at])
        copy.start()
        self.near_by.append(copy)
        self.due[Key.local, at] = self.now + 2.0
        return (Key.local, at)

    def arrived(self, *handles):
        for handle in handles:
            if handle in self.seen:
                continue
            self.seen.add(handle)
            self.now = max(self.now, self.due[handle])
            if handle[0] == Key.remote:
                self.remote[handle[1]].wait_recv()
            else:
                self.near_by[handle[1]].wait()

    def run(self, *tasks):
        live = []
        for rank, task in enumerate(tasks):
            self.rank = rank
            live.append([rank, task, next(task)])

        def waits(entry):
            return entry[2]() if callable(entry[2]) else entry[2]

        def when(entry):
            handles = waits(entry)
            if handles is None:
                return 1e9, entry[0]
            dues = [self.due.get(h, 1e9) for h in handles if h not in self.seen]
            return max([self.now] + dues), entry[0]

        while live:
            entry = min(live, key=when)
            if self.feed(min(when(entry)[0], self.now + 1e6)):
                continue
            self.arrived(*waits(entry))
            self.rank = entry[0]
            try:
                entry[2] = next(entry[1])
            except StopIteration:
                live.remove(entry)
        self.feed(1e9)

    def finish(self):
        for at, copy in enumerate(self.remote):
            self.arrived((Key.remote, at))
            copy.wait_send()
        for at in range(len(self.near_by)):
            self.arrived((Key.local, at))


class Flags:
    def __init__(self):
        self.set = {}

    def raised(self, key, handles=()):
        self.set[key] = list(handles)

    def wait(self, *keys, more=()):
        def ask():
            if any(key not in self.set for key in keys):
                return None
            return [h for key in keys for h in self.set[key]] + list(more)

        return ask


FAST, STEADY = (2.5, 91, 400, 5.0), (3.5, 86, 300, 6.0)
KEEN, EARLY = (2.5, 91, 400, 2.0), (2.5, 91, 400, 25.0)


def comm_call(work, number, masks, arrays, in_vmem, outs, out_vmem, scratch, copies, stay, mb=48, pace=FAST):
    def space(fast):
        return pl.BlockSpec(memory_space=pltpu.VMEM if fast else pl.ANY)

    def body(*refs):
        n, m = len(arrays), len(outs)
        place = Place()
        wire = Wire(place, *refs[-3:], pace)
        wire.greet(masks)
        work(place, wire, refs[:n], refs[n : n + m], refs[n + m : -3])
        wire.finish()

    return pl.pallas_call(
        body,
        in_specs=[space(v) for v in in_vmem],
        out_specs=[space(v) for v in out_vmem],
        out_shape=[jax.ShapeDtypeStruct(shape, kind) for shape, kind in outs],
        scratch_shapes=list(scratch)
        + [
            pltpu.SemaphoreType.DMA((copies,)),
            pltpu.SemaphoreType.DMA((copies,)),
            pltpu.SemaphoreType.DMA((max(stay, 1),)),
        ],
        compiler_params=pltpu.CompilerParams(
            collective_id=number, has_side_effects=True, vmem_limit_bytes=int(mb * 1024 * 1024)
        ),
        cost_estimate=pl.CostEstimate(flops=0, bytes_accessed=1 << 16, transcendentals=0),
    )(*arrays)


def head_gather(place, wire, weight, out, flags=None, key=None, alike=False):
    rows, width = weight.shape[0], out.shape[1]
    block = 4 * rows
    base = place.y * 4 * block

    def columns(tp):
        return weight if alike else weight.at[:, pl.ds(pl.multiple_of(tp * width, 128), width)]

    def part(m):
        return out.at[pl.ds(pl.multiple_of(base + m * block, 16), block)]

    own = out.at[pl.ds(pl.multiple_of(base + place.tp * rows, 16), rows)]
    handles = [wire.keep(columns(place.tp), own)]
    for mask in (X, X | CORE, CORE):
        handles.append(wire.send(columns(place.partner(mask)[1]), own, mask))
    yield handles
    far = wire.send(part(0), part(2), FAR)
    near = wire.send(part(0), part(1), NEAR)
    over = [wire.send(part(0), part(0), Y)]
    yield [far]
    last = wire.send(part(2), part(3), NEAR)
    over.append(wire.send(part(2), part(2), Y))
    yield [near]
    over.append(wire.send(part(1), part(1), Y))
    yield [last]
    over.append(wire.send(part(3), part(3), Y))
    yield over
    if flags is not None:
        flags.raised(key)


def output_gather(place, wire, block, out, flags, key):
    def part(m):
        return out.at[m, place.y]

    yield [wire.keep(block, part(0))]
    far = wire.send(part(0), part(2), FAR)
    near = wire.send(part(0), part(1), NEAR)
    over = [wire.send(part(0), part(0), Y)]
    yield [far]
    last = wire.send(part(2), part(3), NEAR)
    over.append(wire.send(part(2), part(2), Y))
    yield [near]
    over.append(wire.send(part(1), part(1), Y))
    yield [last]
    over.append(wire.send(part(3), part(3), Y))
    yield over
    flags.raised(key)


def ffn_trade(place, wire, weight, halves, out):
    cols = halves.shape[2]

    def to_cut(rows):
        for y in range(2):
            halves[y, rows] = weight[rows, y * cols : (y + 1) * cols]

    row_loop(weight.shape[0], 32, to_cut)
    own = out.at[0, place.y]
    yield [
        wire.send(halves.at[1 - place.y], own, Y),
        wire.keep(halves.at[place.y], own),
    ]


def ffn_traded(place, wire, weight, halves, out, flags, key):
    yield from ffn_trade(place, wire, weight, halves, out)
    flags.raised(key)


def far_spread(wire, out, flags, first):
    yield flags.wait(first)
    far = [wire.send(out.at[0, y], out.at[2, y], FAR) for y in range(2)]
    yield far + [wire.send(out.at[0, y], out.at[1, y], NEAR) for y in range(2)]


def last_spread(place, wire, blocks, out):
    waits = [wire.keep(blocks.at[z], out.at[z]) for z in range(3)]
    yield waits + [wire.send(blocks.at[2, y], out.at[3, y], NEAR) for y in range(2)]


def ffn_spread(place, wire, out, flags, first, then):
    yield flags.wait(first)
    waits = [wire.send(out.at[0, y], out.at[1, y], NEAR) for y in range(2)]
    yield flags.wait(then)
    far = [wire.send(out.at[0, y], out.at[2, y], FAR) for y in range(2)]
    for y in range(2):
        yield [far[y]]
        waits.append(wire.send(out.at[2, y], out.at[3, y], NEAR))
    yield waits


def rows_gather(place, wire, own, out):
    mine = out.at[:, place.tp]
    stay = wire.keep(own, mine)
    across = wire.send(own, mine, X)
    beside = wire.send(own, mine, CORE)
    yield [across]
    theirs = out.at[:, place.partner(X)[1]]
    yield [stay, beside, wire.send(theirs, theirs, CORE)]


def small_gather(place, wire, own, out):
    handles = [
        wire.keep(own, out.at[pl.ds(place.flat, 1)]),
        wire.send(own, out.at[pl.ds(place.flat, 1)], CORE),
    ]
    size = 2
    for mask in (X, Y, NEAR, FAR):
        yield handles
        part = out.at[pl.ds(place.flat // size * size, size)]
        handles = [wire.send(part, part, mask)]
        size *= 2
    yield handles


def plane_gather(place, wire, first, second, out, flags=None):
    line_a = [out.at[0, 0, m] for m in range(4)]
    line_b = [out.at[0, 1, m] for m in range(4)]
    beside = [[], []]

    def pass_on(half, m, source=None):
        source = out.at[0, half, m] if source is None else source
        beside[half].append(wire.send(source, out.at[1, half, m], CORE))

    a_x = wire.send(first, line_a[1], X)
    b_y = wire.send(second, line_b[1], Y)
    a_y = wire.send(first, line_a[2], Y)
    b_x = wire.send(second, line_b[2], X)
    stay = [wire.keep(first, line_a[0]), wire.keep(second, line_b[0])]
    pass_on(0, 0, first)
    pass_on(1, 0, second)
    yield [a_x]
    a_xy = wire.send(line_a[1], line_a[3], Y)
    pass_on(0, 1)
    yield [b_y]
    b_xy = wire.send(line_b[1], line_b[3], X)
    pass_on(1, 1)
    yield [a_y, b_x]
    pass_on(0, 2)
    pass_on(1, 2)
    if flags is not None:
        flags.raised((0, 0), [stay[0], a_xy])
        flags.raised((0, 1), [stay[1], b_xy])
    yield [a_xy]
    pass_on(0, 3)
    if flags is not None:
        flags.raised((1, 0), beside[0])
    yield [b_xy]
    pass_on(1, 3)
    if flags is not None:
        flags.raised((1, 1), beside[1])
    yield stay + beside[0] + beside[1]


def by_tp(values, count, side):
    first, second = count
    order = [(a * second + b) * side for b in range(second) for a in range(first)]
    return jnp.concatenate([values[:, at : at + side] for at in order], axis=1)


def heads_trade(place, wire, branch, out):
    width = out.shape[1] // 4

    def columns(ref, index):
        return ref.at[:, pl.ds(pl.multiple_of(index * width, 128), width)]

    mine = columns(out, place.z_turn(place.tp))
    handles = [wire.keep(columns(branch, place.tp), mine)]
    for mask in (X, X | CORE, CORE):
        handles.append(wire.send(columns(branch, place.partner(mask)[1]), mine, mask))
    yield handles


def heads_return(place, wire, grads, out):
    width = out.shape[1] // 4

    def columns(ref, index):
        return ref.at[:, pl.ds(pl.multiple_of(index * width, 128), width)]

    mine = columns(out, place.tp)
    handles = [wire.keep(columns(grads, place.z_turn(place.tp)), mine)]
    for mask in (X, X | CORE, CORE):
        there = place.z_turn(place.partner(mask)[1])
        handles.append(wire.send(columns(grads, there), mine, mask))
    yield handles


def pieces_scan(place, wire, reverse, survive, state, out, bufs):
    send_s, send_b, got_s, got_b = bufs
    wide = state.shape[-1] // survive.shape[-1]
    total_s, total_b = survive[...], state[...]
    before_s = before_b = None

    def join(first_s, first_b, second_s, second_b):
        spread = jnp.concatenate([second_s] * wide, axis=-1)
        return first_s * second_s, spread * first_b + second_b

    for step, (mask, bit) in enumerate(((Y, place.y), (NEAR, place.near), (FAR, place.far))):
        send_s[step] = total_s
        send_b[step] = total_b.astype(BF)
        yield [
            wire.send(send_b.at[step], got_b.at[step], mask),
            wire.send(send_s.at[step], got_s.at[step], mask),
        ]
        other_s, other_b = got_s[step], got_b[step].astype(F32)
        later = bit == (0 if reverse else 1)
        if before_s is None:
            before_s = jnp.where(later, other_s, 1.0)
            before_b = jnp.where(later, other_b, 0.0)
        else:
            joined_s, joined_b = join(other_s, other_b, before_s, before_b)
            before_s = jnp.where(later, joined_s, before_s)
            before_b = jnp.where(later, joined_b, before_b)
        if mask != FAR:
            first_s, first_b = jnp.where(later, other_s, total_s), jnp.where(later, other_b, total_b)
            second_s = jnp.where(later, total_s, other_s)
            second_b = jnp.where(later, total_b, other_b)
            total_s, total_b = join(first_s, first_b, second_s, second_b)
    out[...] = before_b


def scan_buffers(state_shape, survive_shape):
    return [
        pltpu.VMEM((3,) + survive_shape, F32),
        pltpu.VMEM((3,) + state_shape, BF),
        pltpu.VMEM((3,) + survive_shape, F32),
        pltpu.VMEM((3,) + state_shape, BF),
    ]


def row_loop(count, step, work):
    def body(i, carry):
        work(pl.ds(pl.multiple_of(i * step, step), step))
        return carry

    lax.fori_loop(0, count // step, body, 0)


def rows_fold(place, wire, part, sums, got_core, got_x, finish):
    streams, count = part.shape[0], part.shape[3]
    other_x = 1 - place.x
    beside = [wire.send(part.at[s, :, 1 - place.core], got_core.at[s], CORE) for s in range(streams)]
    across = []
    for s in range(streams):
        yield [beside[s]]

        def to_send(rows, s=s):
            term = part[s, other_x, place.core, rows].astype(F32)
            sums[s, rows] = (term + got_core[s, other_x, rows].astype(F32)).astype(BF)

        row_loop(count, 16, to_send)
        across.append(wire.send(sums.at[s], got_x.at[s], X))
    for s in range(streams):
        yield [across[s]]

        def to_finish(rows, s=s):
            term = part[s, place.x, place.core, rows].astype(F32)
            term = term + got_core[s, place.x, rows].astype(F32)
            finish(s, rows, term + got_x[s, rows].astype(F32))

        row_loop(count, 16, to_finish)


def rows_buffers(part_shape):
    streams, _, _, count, width = part_shape
    return [
        pltpu.VMEM((streams, count, width), BF),
        pltpu.VMEM((streams, 2, count, width), BF),
        pltpu.VMEM((streams, count, width), BF),
    ]


def plane_fold(place, wire, near_part, far_part, bufs, finish, flags=None):
    got_core, send_two, got_two, send_one, got_one = bufs
    count = near_part.shape[2]
    if flags is None:
        flags = Flags()
        for h in range(2):
            flags.raised((Key.far, h))
            flags.raised((Key.near, h))
    beside = {}
    for h in range(2):
        yield flags.wait((Key.far, h))
        for m in (2, 3, 1, 0):
            beside[h, m] = wire.send(far_part.at[h, m], got_core.at[h, m], CORE)
    two, one = {}, {}
    for h in range(2):
        for m in (3, 2):
            yield flags.wait((Key.near, h), more=[beside[h, m]])

            def to_two(rows, h=h, m=m):
                term = near_part[h, m, rows].astype(F32) + got_core[h, m, rows].astype(F32)
                send_two[h, m - 2, rows] = term.astype(BF)

            row_loop(count, 16, to_two)
            two[h, m] = wire.send(send_two.at[h, m - 2], got_two.at[h, m - 2], (Y, X)[h])
    for h in range(2):
        yield [beside[h, 1], two[h, 3]]

        def to_one(rows, h=h):
            term = near_part[h, 1, rows].astype(F32) + got_core[h, 1, rows].astype(F32)
            send_one[h, rows] = (term + got_two[h, 1, rows].astype(F32)).astype(BF)

        row_loop(count, 16, to_one)
        one[h] = wire.send(send_one.at[h], got_one.at[h], (X, Y)[h])
    for h in range(2):
        yield [beside[h, 0], two[h, 2], one[h]]

        def to_finish(rows, h=h):
            def load(columns):
                term = near_part[h, 0, rows, columns].astype(F32)
                term = term + got_core[h, 0, rows, columns].astype(F32)
                term = term + got_two[h, 0, rows, columns].astype(F32)
                return term + got_one[h, rows, columns].astype(F32)

            finish(h, rows, load)

        row_loop(count, 16, to_finish)
        flags.raised((Key.done, h))


def plane_buffers(part_shape):
    halves, _, count, width = part_shape
    return [
        pltpu.VMEM(part_shape, BF),
        pltpu.VMEM((halves, 2, count, width), BF),
        pltpu.VMEM((halves, 2, count, width), BF),
        pltpu.VMEM((halves, count, width), BF),
        pltpu.VMEM((halves, count, width), BF),
    ]


def z_parts(place, load, width):
    size = width // 4
    parts = []
    for m in range(4):
        there = pl.multiple_of(place.z_turn(m) * size, 128)
        parts.append(load(pl.ds(there, size)))
    return jnp.concatenate(parts, axis=-1)


def add_into(target, terms, step=32):
    def work(rows):
        total = terms[0][rows].astype(F32)
        for term in terms[1:]:
            total = total + term[rows].astype(F32)
        target[rows] = total.astype(BF)

    row_loop(target.shape[0], step, work)


def ffn_fold(place, wire, part, bufs, out, flags=None, added=None, ahead=None):
    added = (part.at[0], part.at[2]) if added is None else (added.at[0], added.at[1])
    got_near, got_far, held = bufs
    first, second, far = list(ahead or []), [], []
    for z, handles in ((3, first), (1, second)):
        if z == 3 and ahead is not None:
            continue
        for y in range(2):
            if flags is not None:
                yield flags.wait((z, y))
            handles.append(wire.send(part.at[z, y], got_near.at[z // 2, y], NEAR))
    for y in range(2):
        yield [first[y]] if flags is None else flags.wait((2, y), more=[first[y]])
        add_into(held.at[0, y], [added[1].at[y], got_near.at[1, y]])
        far.append(wire.send(held.at[0, y], got_far.at[y], FAR))
    for y in range(2):
        yield [second[y], far[y]] if flags is None else flags.wait((0, y), more=[second[y], far[y]])
        add_into(held.at[1, y], [added[0].at[y], got_near.at[0, y], got_far.at[y]])
    mine = out.at[place.y]
    yield [
        wire.send(held.at[1, 1 - place.y], mine, Y),
        wire.keep(held.at[1, place.y], mine),
    ]


def weight_tiles(wire, rows_by, order, grads, put, flags=None):
    for key in order:
        yield []
        put(key, mm(rows_by(key), grads(), TN))
        wire.spend(1.2)
        if flags is not None:
            flags.raised(key)


def head_tiles(wire, rows, grads, part, flags):
    side = part.shape[2]
    for z in (3, 1, 2, 0):
        for y in range(2):
            yield []
            at = (y * 4 + z) * side
            part[y, z] = mm(rows[:, at : at + side], grads(), TN).astype(BF)
            wire.spend(0.6)
        flags.raised(z)


def ffn_buffers(part_shape):
    _, ys, rows, width = part_shape
    return [
        pltpu.VMEM((2, ys, rows, width), BF),
        pltpu.VMEM((ys, rows, width), BF),
        pltpu.VMEM((2, ys, rows, width), BF),
    ]


def line_fold(place, wire, mine, theirs, bufs, flags=None):
    got_y, got_near, got_far, held = bufs
    over = {}
    for m in (3, 1, 2, 0):
        if flags is not None:
            yield flags.wait(m)
        over[m] = wire.send(theirs(m), got_y.at[m], Y)
    yield [over[3]]
    add_into(held.at[1], [mine(3), got_y.at[3]])
    last = wire.send(held.at[1], got_near.at[1], NEAR)
    yield [over[1]]
    add_into(held.at[0], [mine(1), got_y.at[1]])
    near = wire.send(held.at[0], got_near.at[0], NEAR)
    yield [over[2], last]
    add_into(held.at[2], [mine(2), got_y.at[2], got_near.at[1]])
    far = wire.send(held.at[2], got_far, FAR)
    yield [over[0], near, far]
    add_into(held.at[3], [mine(0), got_y.at[0], got_near.at[0], got_far])


def line_buffers(rows, width):
    return [
        pltpu.VMEM((4, rows, width), BF),
        pltpu.VMEM((2, rows, width), BF),
        pltpu.VMEM((rows, width), BF),
        pltpu.VMEM((4, rows, width), BF),
    ]


def head_fold(place, wire, part, bufs, out, flags=None):
    yield from line_fold(
        place, wire, lambda m: part.at[place.y, m], lambda m: part.at[1 - place.y, m], bufs, flags
    )
    own = bufs[3].at[3]
    rows, width = out.shape[0], own.shape[1]

    def block(tp):
        return own.at[pl.ds(pl.multiple_of(tp * rows, 16), rows)]

    mine = out.at[:, pl.ds(pl.multiple_of(place.tp * width, 128), width)]
    handles = [wire.keep(block(place.tp), mine)]
    for mask in (X, X | CORE, CORE):
        handles.append(wire.send(block(place.partner(mask)[1]), mine, mask))
    yield handles


def output_fold(place, wire, part, bufs, out, flags=None):
    yield from line_fold(
        place, wire, lambda m: part.at[m, place.y], lambda m: part.at[m, 1 - place.y], bufs, flags
    )
    yield [wire.keep(bufs[3].at[3], out)]


def small_fold(place, wire, values, bufs, out):
    got, total = bufs
    source, start, size = values, 0, 16
    steps = ((FAR, place.far), (NEAR, place.near), (Y, place.y), (X, place.x), (CORE, place.core))
    for mask, bit in steps:
        here = pl.ds(start, size)
        theirs = pl.ds(source_start(start, size) + (1 - bit) * size, size)
        yield [wire.send(source.at[theirs], got.at[here], mask)]
        mine = pl.ds(source_start(start, size) + bit * size, size)
        total[here] = source[mine] + got[here]
        source, start, size = total, start + size, size // 2
    out[...] = total[pl.ds(start - 1, 1)]


def source_start(start, size):
    return 0 if start == 0 else start - 2 * size


class Bits:
    CORE, X, Y, NEAR, FAR = 1, 2, 4, 8, 16

    def __init__(self):
        seq, tp = lax.axis_index(SEQ), lax.axis_index(TP)
        self.core, self.x = tp & 1, tp >> 1
        self.y, self.z = seq & 1, seq >> 1

    def steps(self):
        return (
            (self.CORE, self.core),
            (self.X, self.x),
            (self.Y, self.y),
            (self.NEAR, self.z & 1),
            (self.FAR, self.z >> 1),
        )


def swap(values, mask):
    pairs = [(i, i ^ mask) for i in range(32)]
    return lax.ppermute(values, (SEQ, TP), pairs)


def half(values, axis, which):
    size = values.shape[axis] // 2
    return lax.dynamic_slice_in_dim(values, which * size, size, axis)


def trade(values, mask, bit, axis, kind=None):
    other = half(values, axis, 1 - bit)
    if kind is not None:
        other = other.astype(kind)
    return half(values, axis, bit), swap(other, mask)


def in_order(mine, theirs, bit):
    first = bit == 0
    return jnp.where(first, mine, theirs), jnp.where(first, theirs, mine)


def z_blocks(block):
    far = swap(block, Bits.FAR)
    return [block, swap(block, Bits.NEAR), far, swap(far, Bits.NEAR)]


def z_fold(blocks, kind=BF):
    first = blocks[0] + swap(blocks[1].astype(kind), Bits.NEAR).astype(F32)
    second = blocks[2] + swap(blocks[3].astype(kind), Bits.NEAR).astype(F32)
    return first + swap(second.astype(kind), Bits.FAR).astype(F32)


def z_relative(values, z, axis):
    size = values.shape[axis] // 4
    return jnp.concatenate(
        [lax.dynamic_slice_in_dim(values, (m ^ z) * size, size, axis) for m in range(4)], axis
    )


def spread_tp(values, at):
    streams, count, width = values.shape
    pair = jnp.stack(in_order(values, swap(values, Bits.X), at.x), axis=1)
    both = jnp.stack(in_order(pair, swap(pair, Bits.CORE), at.core), axis=2)
    return both.reshape(streams, 4 * count, width)


def fold_tp(part, at):
    streams, count, width = part.shape
    parts = part.reshape(streams, 2, 2, count // 4, width)
    mine, got = trade(parts, Bits.CORE, at.core, 2, BF)
    mine, got = trade(mine + got.astype(F32), Bits.X, at.x, 1, BF)
    return (mine + got.astype(F32)).reshape(streams, count // 4, width)


def spread_plane(rows):
    count = rows.shape[0] // 2
    first, second = rows[:count], rows[count:]
    first = jnp.concatenate([first, swap(first, Bits.X)], axis=0)
    second = jnp.concatenate([second, swap(second, Bits.Y)], axis=0)
    four = [first, swap(first, Bits.Y), second, swap(second, Bits.X)]
    four = jnp.concatenate(four, axis=0)
    return jnp.concatenate([four, swap(four, Bits.CORE)], axis=0)


def fold_half(part, mask):
    size = part.shape[0] // 2
    return part[:size] + swap(part[size:].astype(BF), mask).astype(F32)


def fold_plane(work):
    sent = swap(work(1).astype(BF), Bits.CORE)
    part = work(0) + sent.astype(F32)
    size = part.shape[0] // 2
    first = fold_half(fold_half(part[:size], Bits.Y), Bits.X)
    second = fold_half(fold_half(part[size:], Bits.X), Bits.Y)
    return jnp.concatenate([first, second], axis=0)


def gather_head(weight, at):
    rows, width = weight.shape
    mine, got = trade(weight, Bits.X, at.x, 1)
    both = jnp.stack(in_order(mine, got, at.x), axis=0)
    mine, got = trade(both, Bits.CORE, at.core, 2)
    both = jnp.stack(in_order(mine, got, at.core), axis=1).reshape(4 * rows, width // 4)
    line = jnp.concatenate(z_blocks(both), axis=0)
    return jnp.concatenate(in_order(line, swap(line, Bits.Y), at.y), axis=0)


def fold_head(grad, at):
    mine, got = trade(grad, Bits.Y, at.y, 0, BF)
    line = mine + got.astype(F32)
    rows = line.shape[0] // 4
    own = z_fold([line[m * rows : (m + 1) * rows] for m in range(4)])
    width = own.shape[1]
    own = own.reshape(2, 2, rows // 4, width)
    mine, got = trade(own, Bits.CORE, at.core, 1, BF)
    own = jnp.concatenate(in_order(mine, got.astype(F32), at.core), axis=-1)
    mine, got = trade(own, Bits.X, at.x, 0, BF)
    own = jnp.concatenate(in_order(mine, got.astype(F32), at.x), axis=-1)
    return own.reshape(rows // 4, 4 * width)


def turn_bits(values, back):
    pairs = []
    for i in range(32):
        z, y, x, core = i >> 3, (i >> 2) & 1, (i >> 1) & 1, i & 1
        there = z * 8 + core * 4 + y * 2 + x
        pairs.append((there, i) if back else (i, there))
    return lax.ppermute(values, (SEQ, TP), pairs)


def gather_output(weight, at):
    block = turn_bits(weight, False)
    line = jnp.stack(z_blocks(block), axis=0)
    both = jnp.stack(in_order(line, swap(line, Bits.Y), at.y), axis=1)
    return both.reshape(8 * weight.shape[0], weight.shape[1])


def fold_output(grad, at):
    rows, width = grad.shape
    parts = grad.reshape(4, 2, rows // 8, width)
    mine, got = trade(parts, Bits.Y, at.y, 1, BF)
    line = (mine + got.astype(F32)).reshape(4, rows // 8, width)
    own = z_fold([line[m] for m in range(4)])
    return turn_bits(own.astype(BF), True).astype(F32)


def heads_to_rows(values, at):
    mine, got = trade(values, Bits.X, at.x, 1)
    both = jnp.stack(in_order(mine, got, at.x), axis=0)
    mine, got = trade(both, Bits.CORE, at.core, 2)
    both = jnp.stack(in_order(mine, got, at.core), axis=1)
    parts = both.reshape((4,) + both.shape[2:])
    return jnp.concatenate(
        [lax.dynamic_index_in_dim(parts, m ^ at.z, 0, False) for m in range(4)], axis=1
    )


def rows_to_heads(values, at):
    width = values.shape[1] // 4
    parts = jnp.stack(
        [
            lax.dynamic_slice_in_dim(values, (m ^ at.z) * width, width, 1)
            for m in range(4)
        ],
        axis=0,
    ).reshape(2, 2, values.shape[0], width)
    mine, got = trade(parts, Bits.X, at.x, 0)
    first, second = in_order(mine[0], got[0], at.x)
    both = jnp.stack([first, second], axis=0)
    mine, got = trade(both, Bits.CORE, at.core, 1)
    first, second = in_order(mine[:, 0], got[:, 0], at.core)
    both = jnp.stack([first, second], axis=1)
    return jnp.concatenate([both[0, 0], both[0, 1], both[1, 0], both[1, 1]], axis=1)


class FfnGather:
    def __init__(self, weight, at):
        mine, got = trade(weight, Bits.Y, at.y, 1)
        self.block = jnp.concatenate(in_order(mine, got, at.y), axis=0)

    def far(self, *after):
        self.block = tie(self.block, *after)
        self.far_block = swap(self.block, Bits.FAR)
        return (self.far_block,)

    def near(self, *after):
        self.block = tie(self.block, *after)
        self.near_block = swap(self.block, Bits.NEAR)
        self.last_block = swap(self.far_block, Bits.NEAR)
        return (self.near_block, self.last_block)

    def whole(self):
        parts = [self.block, self.near_block, self.far_block, self.last_block]
        return jnp.concatenate(parts, axis=0)


class FfnFold:
    def __init__(self, grad, at):
        self.at = at
        rows = grad.shape[0] // 4
        self.parts = [grad[m * rows : (m + 1) * rows] for m in range(4)]

    def near(self, *after):
        sent = [tie(self.parts[1].astype(BF), *after), self.parts[3].astype(BF)]
        self.got = [swap(s, Bits.NEAR) for s in sent]
        return tuple(self.got)

    def far(self, *after):
        second = self.parts[2] + self.got[1].astype(F32)
        self.last = swap(tie(second.astype(BF), *after), Bits.FAR)
        return (self.last,)

    def whole(self):
        own = self.parts[0] + self.got[0].astype(F32) + self.last.astype(F32)
        mine, got = trade(own, Bits.Y, self.at.y, 0, BF)
        return jnp.concatenate(in_order(mine, got.astype(F32), self.at.y), axis=1)


class PlainWhole:
    def __init__(self, value):
        self.value = value

    def far(self, *after):
        return ()

    near = far

    def whole(self):
        return self.value


def spread_all(values, at):
    for mask, bit in at.steps():
        values = jnp.concatenate(in_order(values, swap(values, mask), bit), axis=0)
    return values


def fold_all(values, at):
    for mask, bit in reversed(at.steps()):
        mine, got = trade(values, mask, bit, 0)
        values = mine + got
    return values


def scan_pieces(part, at, reverse):
    total, before = part, None
    steps = ((Bits.Y, at.y), (Bits.NEAR, at.z & 1), (Bits.FAR, at.z >> 1))
    for mask, bit in steps:
        other = (swap(total[0], mask), swap(total[1].astype(BF), mask).astype(F32))
        later = bit == (0 if reverse else 1)
        if before is None:
            before = (
                jnp.where(later, other[0], 1.0),
                jnp.where(later, other[1], 0.0),
            )
        else:
            joined = chain(other, before)
            before = tuple(jnp.where(later, a, b) for a, b in zip(joined, before))
        if mask != Bits.FAR:
            first = tuple(jnp.where(later, o, t) for o, t in zip(other, total))
            second = tuple(jnp.where(later, t, o) for o, t in zip(other, total))
            total = chain(first, second)
    return before


@dataclasses.dataclass
class Mixer:
    reading: jax.Array
    scores: jax.Array
    share: jax.Array
    branch: jax.Array
    normed: jax.Array
    logits: jax.Array
    keep: jax.Array
    written: jax.Array
    slots_in: jax.Array
    slots_end: jax.Array
    weights: list
    raw: list
    output: jax.Array
    rows: jax.Array = None
    low: jax.Array = None
    low_rank: jax.Array = None
    rank: jax.Array = None
    survive: jax.Array = None
    out_gain: jax.Array = None
    ffn_gain: jax.Array = None
    attn_gain: jax.Array = None


def alive_rows(seq_cuts, seq, length):
    positions = seq * length + jnp.arange(length)
    starts = (positions[None, :] == 0) | (positions[None, :] == seq_cuts[:, None])
    return jnp.where(starts, 0.0, 1.0).astype(F32)[:, None, :]


class Plain:
    def __init__(self):
        self.seq, self.tp = lax.axis_index(SEQ), lax.axis_index(TP)
        self.seq_count, self.tp_count = lax.axis_size(SEQ), lax.axis_size(TP)
        self.sharing = self.tp_count // H
        self.head, self.member = self.tp // self.sharing, self.tp % self.sharing


def plain_scan(part, at, reverse):
    gathered = (
        lax.all_gather(part[0], SEQ),
        lax.all_gather(part[1].astype(BF), SEQ),
    )
    state = (jnp.ones_like(part[0]), jnp.zeros_like(part[1]))

    def step(count, state):
        source = at.seq_count - 1 - count if reverse else count
        piece = tuple(lax.dynamic_index_in_dim(a, source, 0, False) for a in gathered)
        return chain(state, (piece[0], piece[1].astype(F32)))

    steps = at.seq_count - 1 - at.seq if reverse else at.seq
    return lax.fori_loop(0, steps, step, state)


class PlainMoves:
    def small(self, packed):
        return lax.all_gather(packed, (SEQ, TP))

    def small_sum(self, packed):
        return lax.psum_scatter(packed, (SEQ, TP), scatter_dimension=0, tiled=True)[0]

    def start(self, tokens, seq_cuts, weights, w_output, small, ffn, cotangent):
        self.ffn = ffn
        devices = self.at.seq_count * self.at.tp_count
        gathered = self.small(jnp.concatenate([a.reshape(-1) for a in small]))
        unpacked, taken = [], 0
        for a in small:
            part = gathered[:, taken : taken + a.size]
            unpacked.append(part.reshape((devices * a.shape[0],) + a.shape[1:]))
            taken += a.size
        low, full_rank, full_bias, attn, out, ffn_gain = unpacked
        slots = full_bias.shape[0] // H
        rank = lax.dynamic_slice_in_dim(full_rank, self.head * slots, slots, 0).astype(F32)
        bias = lax.dynamic_slice_in_dim(full_bias, self.head * slots, slots, 0).astype(F32)
        rows = self.piece(tokens)
        held, length, width = rows.shape
        inputs = rows.reshape(held * length, width).astype(F32)
        normed = (inputs * inverse_rms(inputs) * attn.astype(F32)).astype(BF)
        low_rank = product(normed, low, NN).reshape(held, length, -1)
        logits = jnp.einsum("mr,str->smt", rank, low_rank, precision=lax.Precision.HIGHEST)
        logits = logits + bias[None, :, None]
        true_keep, written = gates(logits)
        alive = self.own_streams(alive_rows(seq_cuts, self.at.seq, length))
        keep = true_keep * alive
        weights = [self.head_weight(w) for w in weights]
        raw = [product(normed, w, NN).reshape(held, length, -1) for w in weights]
        hd = raw[0].shape[-1]
        state, survive = per_stream(
            piece_state,
            [raw[0], raw[1], keep, written],
            [((slots, 2 * hd), F32), ((slots, 1), F32)],
            1 << 30,
        )
        slots_in = self.scan((survive[..., 0], state), False)[1]
        key_raw, value_raw, query_raw, gate_raw = raw
        reading, scores, share = per_stream(
            piece_read,
            [query_raw, key_raw, value_raw, keep, written, slots_in],
            [((length, hd), F32), ((slots, length), F32), ((slots, length), F32)],
            1 << 30,
        )
        read_normed = reading * inverse_rms(reading) * out.astype(F32)
        branch = (read_normed * silu(gate_raw)).astype(BF).reshape(held * length, hd)
        output = self.output_weight(w_output)
        self.mixed = product(branch, output, NN).reshape(held, length, width)
        return Mixer(
            reading=reading,
            scores=scores,
            share=share,
            branch=branch,
            rows=rows,
            normed=normed,
            low=low,
            low_rank=low_rank,
            rank=rank,
            logits=logits,
            keep=keep,
            written=written,
            survive=survive[..., 0],
            slots_in=slots_in,
            slots_end=survive * slots_in + state,
            weights=weights,
            raw=raw,
            output=output,
            out_gain=out.astype(F32),
            ffn_gain=ffn_gain.astype(F32),
            attn_gain=attn.astype(F32),
        )

    def feed_forward(self, tokens, gain, cotangent):
        streams, count, width = tokens.shape
        own_rows = streams * count
        hidden = (tokens.astype(F32) + self.sum_piece(self.mixed)).reshape(own_rows, width)
        scale = inverse_rms(hidden)
        ffn_in = self.ffn_rows((hidden * scale * gain).astype(BF))
        cot = self.ffn_rows(cotangent.reshape(own_rows, width))
        down, gate, up = [lax.all_gather(w, SEQ, axis=0, tiled=True) for w in self.ffn]
        grad_product = product(cot, down, NN)
        gate_pre, up_pre = product(ffn_in, gate, NN), product(ffn_in, up, NN)
        sig = jax.nn.sigmoid(gate_pre)
        act = (gate_pre * sig * up_pre).astype(BF)
        slope = sig * (1.0 + gate_pre * (1.0 - sig))
        grad_gate = (grad_product * up_pre * slope).astype(BF)
        grad_up = (grad_product * gate_pre * sig).astype(BF)
        grad = self.ffn_sum(product(grad_gate, gate, NT) + product(grad_up, up, NT))
        self.gate_grad = self.ffn_grad(product(ffn_in, grad_gate, TN).astype(BF))
        self.up_grad = self.ffn_grad(product(ffn_in, grad_up, TN).astype(BF))
        self.down_sum = self.ffn_grad(product(cot, act, TN).astype(BF))
        self.result = (hidden + self.ffn_sum(product(act, down, NT))).astype(BF)
        gain_grad = jnp.sum(grad * hidden * scale, axis=0)
        grad_hidden = cotangent.reshape(own_rows, width).astype(F32)
        grad_hidden = grad_hidden + norm_back(hidden, scale, gain, grad)
        return grad_hidden, gain_grad, self.piece(grad_hidden.astype(BF).reshape(cotangent.shape))

    def ffn_grad(self, grad):
        own = lax.psum_scatter(grad, SEQ, scatter_dimension=0, tiled=True)
        return own.astype(F32)

    def mixer_back(self, mixer, grad_mixed):
        reading, scores, share, branch_out = mixer.reading, mixer.scores, mixer.share, mixer.branch
        streams, length, hd = reading.shape
        slots = scores.shape[1]
        key_raw, value_raw, query_raw, gate_raw = mixer.raw
        grad_branch = product(grad_mixed, mixer.output, NT).reshape(reading.shape)
        self.output_sum = self.output_grad(product(branch_out, grad_mixed, TN))
        scale = inverse_rms(reading)
        normed = reading * scale * mixer.out_gain
        grad_gate = (grad_branch * normed * silu_slope(gate_raw)).astype(BF)
        grad = grad_branch * silu(gate_raw)
        gain_sum = jnp.sum(grad * reading * scale, axis=(0, 1))[None]
        grad_read = norm_back(reading, scale, mixer.out_gain, grad)
        grad_query, grad_k, grad_v, direct, back, own = per_stream(
            piece_back,
            [query_raw, key_raw, value_raw, mixer.keep, mixer.written]
            + [mixer.slots_in, scores, share, grad_read],
            [
                ((length, hd), BF),
                ((length, hd), F32),
                ((length, hd), F32),
                ((slots, 2 * hd), F32),
                ((slots, length), F32),
                ((slots, length), F32),
            ],
            1 << 30,
        )
        after = self.scan((mixer.survive, direct), True)[1]
        self.head_sums = [
            self.head_grad(product(mixer.normed, g.reshape(-1, hd), TN))
            for g in (grad_query, grad_gate)
        ]
        return after, gain_sum, grad_query, grad_gate, grad_k, grad_v, back, own

    def finish(self, mixer, back, tokens, grad_hidden, ffn_gain_grad, small):
        after, out_gain_grad, grad_query, grad_gate, grad_k, grad_v, pulled, flow = back
        held, length, hd = grad_k.shape
        width, slots = tokens.shape[-1], flow.shape[1]
        grad_key, grad_value, grad_log = per_stream(
            piece_after,
            [mixer.raw[0], mixer.raw[1], mixer.keep, mixer.written]
            + [grad_k, grad_v, pulled, flow, after, mixer.slots_end],
            [((length, hd), BF), ((length, hd), BF), ((slots, length), F32)],
            1 << 30,
        )
        highest = lax.Precision.HIGHEST
        grad_f = grad_log * jax.nn.sigmoid(-mixer.logits) / GATE_SCALE
        grad_bias = jnp.sum(grad_f, axis=(0, 2))
        grad_rank = jnp.einsum("smt,str->mr", grad_f, mixer.low_rank, precision=highest)
        low_grad = jnp.einsum("smt,mr->str", grad_f, mixer.rank, precision=highest)
        low_grad = low_grad.reshape(held * length, -1)
        grads = [g.reshape(-1, hd) for g in (grad_key, grad_value, grad_query, grad_gate)]
        grad_normed = sum(product(g, w, NT) for g, w in zip(grads, mixer.weights))
        grad_normed = grad_normed + product(low_grad, mixer.low.astype(F32), NT)
        inputs = mixer.rows.reshape(-1, width).astype(F32)
        attn_grad = jnp.sum(grad_normed * inputs * inverse_rms(inputs), axis=0)
        grad_low = product(mixer.normed.astype(F32), low_grad, TN)

        def placed(part):
            entire = jnp.zeros((part.shape[0] * H,) + part.shape[1:], F32)
            return lax.dynamic_update_slice_in_dim(entire, part, self.head * part.shape[0], 0)

        sums = (grad_low, placed(grad_rank), placed(grad_bias), attn_grad)
        sums = sums + (out_gain_grad[0], ffn_gain_grad)
        devices = self.at.seq_count * self.at.tp_count
        packed = jnp.concatenate([a.reshape(devices, -1) for a in sums], axis=1)
        own = self.small_sum(packed)
        small_grads, taken = [], 0
        for a in small:
            small_grads.append(own[taken : taken + a.size].reshape(a.shape))
            taken += a.size
        heads = [self.head_grad(product(mixer.normed, g, TN)) for g in grads[:2]]
        heads = heads + self.head_sums + [self.output_sum]
        x = tokens.astype(F32)
        total = self.sum_piece(grad_normed.reshape(held, length, width))
        grad_tokens = norm_back(x, inverse_rms(x), mixer.attn_gain, total)
        grad_tokens = grad_tokens + grad_hidden.reshape(x.shape)
        ffn_grads = [self.gate_grad, self.up_grad, self.down_sum]
        return heads, ffn_grads, grad_tokens, self.result, small_grads

    def __init__(self):
        self.at = Plain()
        self.head, self.member = self.at.head, self.at.member

    def own_streams(self, values):
        count = values.shape[0] // self.at.sharing
        return lax.dynamic_slice_in_dim(values, self.member * count, count, 0)

    def piece(self, own):
        return self.own_streams(lax.all_gather(own, TP, axis=1, tiled=True))

    def sum_piece(self, part):
        streams = part.shape[0] * self.at.sharing
        entire = jnp.zeros((streams,) + part.shape[1:], BF)
        entire = lax.dynamic_update_slice_in_dim(
            entire, part.astype(BF), self.member * part.shape[0], 0
        )
        own = lax.psum_scatter(entire, TP, scatter_dimension=1, tiled=True)
        return own.astype(F32)

    def mixer_order(self, values):
        return values

    mixer_unorder = ffn_order = ffn_unorder = mixer_order

    def head_weight(self, weight):
        entire = lax.all_gather(weight, (SEQ, TP), axis=0, tiled=True)
        width = entire.shape[1] // H
        return lax.dynamic_slice_in_dim(entire, self.head * width, width, 1)

    def head_grad(self, grad):
        entire = jnp.zeros((grad.shape[0], grad.shape[1] * H), BF)
        entire = lax.dynamic_update_slice_in_dim(
            entire, grad.astype(BF), self.head * grad.shape[1], 1
        )
        own = lax.psum_scatter(entire, (SEQ, TP), scatter_dimension=0, tiled=True)
        return own.astype(F32)

    def output_weight(self, weight):
        entire = lax.all_gather(weight, (SEQ, TP), axis=0, tiled=True)
        rows = entire.shape[0] // H
        return lax.dynamic_slice_in_dim(entire, self.head * rows, rows, 0)

    def output_grad(self, grad):
        entire = jnp.zeros((grad.shape[0] * H, grad.shape[1]), BF)
        entire = lax.dynamic_update_slice_in_dim(
            entire, grad.astype(BF), self.head * grad.shape[0], 0
        )
        own = lax.psum_scatter(entire, (SEQ, TP), scatter_dimension=0, tiled=True)
        return own.astype(F32)

    def scan(self, part, reverse):
        return plain_scan(part, self.at, reverse)

    def ffn_rows(self, own):
        entire = lax.all_gather(own, TP, axis=0)
        return entire.reshape((-1,) + own.shape[1:])

    def ffn_sum(self, part):
        parts = part.astype(BF).reshape((self.at.tp_count, -1) + part.shape[1:])
        own = lax.psum_scatter(parts, TP, scatter_dimension=0, tiled=True)
        return own.reshape((-1,) + part.shape[1:]).astype(F32)


class BitMoves:
    def __init__(self):
        self.at = Bits()
        self.head, self.member = lax.axis_index(TP), 0

    def start(self, tokens, seq_cuts, weights, w_output, small, ffn, cotangent):
        w_low, w_rank, bias, attn_gain, out_gain, ffn_gain = small
        rank = w_low.shape[1]
        gains = jnp.stack([attn_gain, ffn_gain], axis=1)
        pack = jnp.concatenate([w_low, gains], axis=1)
        pack = jnp.pad(pack, ((0, 0), (0, 128 - pack.shape[1])))
        tall = w_rank.shape[0]
        lines = jnp.concatenate([w_rank, bias[:, None]], axis=1)
        lines = jnp.pad(lines, ((0, 0), (0, 128 - lines.shape[1])))
        gain_line = jnp.pad(out_gain, (0, 128 - out_gain.shape[0]))[None]
        lines = jnp.concatenate([lines, gain_line], axis=0)
        lines = jnp.pad(lines, ((0, 16 - lines.shape[0]), (0, 0)))[None]
        streams, count, width = tokens.shape
        length = 4 * count
        hd = width // 4
        per = out_gain.shape[0]
        slots = 8 * tall
        head = (width, hd)
        cut = (2, ffn[0].shape[0], ffn[0].shape[1] // 2)
        ffn_shape = (4,) + cut
        block = w_output
        alive = alive_rows(seq_cuts, lax.axis_index(SEQ), length)
        state_shape, slim = (streams, slots, 2 * hd), (streams, slots, 128)
        gate_shape = (streams, slots, length)

        def work(place, wire, given, outs, scratch):
            pack, lines, tokens, alive, own_tokens = given[:5]
            given = given[1:]
            heads_in, block, ffn_in, cot = given[4:8], given[8], given[9:12], given[12]
            pack_out, lines_out, low_out, logits, keep, written = outs[:6]
            survive, slots_in, slots_end, scores, share = outs[6:11]
            factor_out, normed_out, reading_out, branch_out, hidden_out = outs[11:16]
            gain_rows = outs[30]
            heads_out, raws_out, output_out = outs[16:20], outs[20:24], outs[24]
            ffn_out, cot_out, ffn_rows = outs[25:28], outs[28], outs[29]
            rows, normed, state = scratch[:3]
            heads, raws, cuts, scan = scratch[3:7], scratch[7:11], scratch[11:14], scratch[14:18]
            output_w, reading, branch, traded, mixed = scratch[18:23]
            hidden, ready = scratch[23:25]
            fold_bufs, cot_own = scratch[25:28], scratch[28]
            here = Flags()

            def fetch_rows():
                yield from rows_gather(place, wire, tokens, rows)
                here.raised(Key.rows)

            def fetch_lines():
                yield from small_gather(place, wire, lines, lines_out)
                here.raised(Key.lines)

            def across(row_at):
                side = width // 8
                for y in range(2):
                    for m in range(4):
                        to = pl.multiple_of((place.z_turn(m) * 2 + y) * side, 128)
                        yield pl.ds(to, side), slice((y * 4 + m) * side, (y * 4 + m + 1) * side)

            def norm():
                tall_rows = jnp.transpose(pack_out[...].astype(F32))
                gain_rows[2:3] = tall_rows[rank : rank + 1]
                for there, at in across(0):
                    gain_rows[3:4, there] = tall_rows[rank : rank + 1, at]
                    gain_rows[1:2, there] = tall_rows[rank + 1 : rank + 2, at]
                steps = count // 16

                def body(i, carry):
                    stream, tp, part = i // (4 * steps), i // steps % 4, i % steps
                    at = pl.multiple_of(part * 16, 16)
                    x = rows[stream, tp, pl.ds(at, 16)].astype(F32)
                    to = pl.ds(pl.multiple_of(i * 16, 16), 16)
                    scale = inverse_rms(x)
                    for there, here_at in across(0):
                        part = rows[stream, tp, pl.ds(at, 16), there].astype(F32)
                        part = part * scale * gain_rows[2:3, here_at]
                        normed[to, here_at] = part.astype(BF)
                    return carry

                lax.fori_loop(0, streams * 4 * steps, body, 0)

            def project(index):
                for s in range(streams):
                    raws[index][s] = mm(normed[s * length : (s + 1) * length], heads[index][...], NN)
                wire.spend(3.0)
                here.raised((Key.raw, index))
                wire.keep(heads[index], heads_out[index])
                wire.keep(raws[index], raws_out[index])

            def gains():
                own = lines_out[...].astype(F32)[:, tall]
                spot, turn_of = row((128, hd)), column((128, hd))
                spread = jnp.where(spot == turn_of % per, 1.0, 0.0)
                wide = mm(own, spread, NN)
                here_is = row(wide.shape) == column(wide.shape) // per
                out_row = jnp.sum(jnp.where(here_is, wide, 0.0), axis=0, keepdims=True)
                gain_rows[0:1, :hd] = out_row

            def read(s, carry):
                values = piece_read(
                    raws[2][s], raws[0][s], raws[1][s], keep[s], written[s], slots_in[s]
                )
                reading[s], scores[s], share[s] = values
                return carry

            def gated(s):
                def chunk(part):
                    at = pl.ds(pl.multiple_of(s * length + part.start, 16), part.size)
                    values = reading[s, part]
                    normed_read = values * inverse_rms(values) * gain_rows[0:1, :hd]
                    opened = normed_read * silu(raws[3][s, part])
                    branch[at] = by_tp(opened, (2, 4), hd // 8).astype(BF)

                row_loop(length, 32, chunk)

            def finish(stream, rows, part):
                values = own_tokens[stream, rows].astype(F32) + part
                hidden[stream, rows] = values
                normed = (values * inverse_rms(values) * gain_rows[1:2]).astype(BF)
                size = width // 4
                for m in range(4):
                    there = pl.ds(pl.multiple_of(place.z_turn(m) * size, 128), size)
                    ready[stream, rows, there] = normed[:, m * size : (m + 1) * size]

            def to_rows():
                yield here.wait(Key.branch)
                yield from heads_trade(place, wire, branch, traded)
                here.raised(Key.traded)
                wire.keep(traded, branch_out)
                yield here.wait(Key.mixed)
                yield from rows_fold(place, wire, mixed, *fold_bufs, finish)
                wire.keep(hidden, hidden_out)
                yield from plane_gather(place, wire, ready.at[0], ready.at[1], ffn_rows)

            def trade(i):
                return ffn_traded(place, wire, ffn_in[i], cuts[i], ffn_out[i], here, (Key.trade, i))

            def fetch_cot():
                side = width // 4

                def turn_row(at, stream):
                    for m in range(4):
                        there = pl.ds(pl.multiple_of(place.z_turn(m) * side, 128), side)
                        cot_own[stream, at, m * side : (m + 1) * side] = cot[stream, at, there]

                for stream in range(streams):
                    row_loop(count, 16, lambda at, stream=stream: turn_row(at, stream))
                yield from plane_gather(place, wire, cot_own.at[0], cot_own.at[1], cot_out)

            def compute():
                yield here.wait(Key.rows, Key.pack)
                norm()
                wire.spend(3.0)
                wire.keep(normed, normed_out)
                yield here.wait(Key.lines)
                own = lines_out[pl.ds(place.tp * 8, 8)].astype(F32)[:, :tall].reshape(slots, 128)
                factor = jnp.where(column(own.shape) < rank, own, 0.0)
                factor_out[...] = factor
                for s in range(streams):
                    low = mm(normed[s * length : (s + 1) * length], pack_out[...], NN)
                    low_out[s] = low
                    f = mm_fine(factor, low, NT) + own[:, rank : rank + 1]
                    logits[s] = f
                    kept, wrote = gates(f)
                    written[s] = wrote
                    keep[s] = kept * alive[s]
                wire.spend(2.0)
                for index in range(2):
                    yield here.wait(index)
                    project(index)
                for s in range(streams):
                    part, left = piece_state(raws[0][s], raws[1][s], keep[s], written[s])
                    state[s] = part
                    survive[s] = jnp.broadcast_to(left, slim[1:])
                wire.spend(3.0)
                here.raised(Key.state)
                for index in (2, 3):
                    yield here.wait(index)
                    project(index)
                gains()
                yield here.wait(Key.slots)
                lax.fori_loop(0, streams, read, 0)
                wire.spend(10.0)
                for s in range(streams):
                    gated(s)
                wire.spend(2.0)
                here.raised(Key.branch)
                wire.keep(reading, reading_out)
                yield here.wait(Key.traded, 4)
                wire.keep(output_w, output_out)
                for s in range(streams):
                    rows_in = traded[s * length : (s + 1) * length]
                    total = mm(rows_in, output_w[...].reshape(hd, width), NN)
                    mixed[s] = total.astype(BF).reshape(mixed.shape[1:])
                wire.spend(2.5)
                here.raised(Key.mixed)

            def exchange():
                yield here.wait(Key.state)
                yield from pieces_scan(place, wire, False, survive, state, slots_in, scan)
                for s in range(streams):
                    slots_end[s] = survive[s][:, :1] * slots_in[s] + state[s]
                here.raised(Key.slots)

            wire.run(
                fetch_lines(),
                head_gather(place, wire, pack, pack_out, here, Key.pack, True),
                exchange(),
                to_rows(),
                *[
                    head_gather(place, wire, w, o, here, i)
                    for i, (w, o) in enumerate(zip(heads_in, heads))
                ],
                fetch_rows(),
                trade(0),
                trade(1),
                output_gather(place, wire, block, output_w, here, 4),
                trade(2),
                far_spread(wire, ffn_out[0], here, (Key.trade, 0)),
                ffn_spread(place, wire, ffn_out[1], here, (Key.trade, 1), Key.slots),
                ffn_spread(place, wire, ffn_out[2], here, (Key.trade, 2), Key.slots),
                fetch_cot(),
                compute(),
            )

        vmem = pltpu.VMEM
        plane = (2, 2, 4, count, width)
        flat = (streams * length, width)
        raw = (streams, length, hd)
        mixed_shape = (streams, 2, 2, count, width)
        outs = comm_call(
            work,
            1,
            (CORE, X, X | CORE, Y, NEAR, FAR),
            [pack, lines, tokens, alive, tokens]
            + list(weights)
            + [block]
            + list(ffn)
            + [cotangent],
            [False, False, False, True, True] + [False] * 5 + [True] * 4,
            [
                ((width, 128), BF),
                ((32, 16, 128), BF),
                ((streams, length, 128), F32),
                (gate_shape, F32),
                (gate_shape, F32),
                (gate_shape, F32),
                (slim, F32),
                (state_shape, F32),
                (state_shape, F32),
                (gate_shape, F32),
                (gate_shape, F32),
                ((slots, 128), F32),
                (flat, BF),
                (raw, F32),
                ((flat[0], hd), BF),
                (tokens.shape, F32),
            ]
            + [(head, BF)] * 4
            + [(raw, F32)] * 4
            + [((4, 2) + block.shape, BF)]
            + [(ffn_shape, BF)] * 3
            + [(plane, BF)] * 2
            + [((8, width), F32)],
            [True] * 12 + [False] * 18 + [True],
            [vmem((streams, 4, count, width), BF), vmem(flat, BF), vmem(state_shape, F32)]
            + [vmem(head, BF)] * 4
            + [vmem(raw, F32)] * 4
            + [vmem(cut, BF)] * 3
            + scan_buffers(state_shape, slim)
            + [
                vmem((4, 2) + block.shape, BF),
                vmem(raw, F32),
                vmem((flat[0], hd), BF),
                vmem((flat[0], hd), BF),
                vmem(mixed_shape, BF),
                vmem(tokens.shape, F32),
                vmem(tokens.shape, BF),
            ]
            + rows_buffers(mixed_shape)
            + [vmem(tokens.shape, BF)],
            150,
            50,
            mb=63,
            pace=STEADY,
        )
        pack, lines, low_rank, logits, keep, written = outs[:6]
        survive, slots_in, slots_end, scores, share = outs[6:11]
        self.ranks, normed, reading, branch, self.hidden_rows = outs[11:16]
        self.down, self.gate, self.up = outs[25:28]
        self.cot, self.ffn_in, self.gains = outs[28:31]
        self.low_rank, self.pack, self.survive = low_rank, pack, survive
        return Mixer(
            reading=reading,
            scores=scores,
            share=share,
            branch=branch,
            normed=normed,
            logits=logits,
            keep=keep,
            written=written,
            slots_in=slots_in,
            slots_end=slots_end,
            weights=list(outs[16:20]),
            raw=list(outs[20:24]),
            output=outs[24].reshape(8 * block.shape[0], width),
        )

    def feed_forward(self, tokens, gain, cotangent):
        streams, count, width = tokens.shape
        plane = (2, 2, 4, count, width)
        half = plane[1:]
        ffn = self.down.shape
        cols = ffn[-1]
        many = 4 * count
        group = (2, 2, many, cols)
        z_line = [(z, y) for z in (3, 1, 2, 0) for y in range(2)]
        side = ffn[2]

        def work(place, wire, given, outs, scratch):
            hidden, gains, cot, rows_in, gate_in, up_in, cot_in, down_in = given
            grad_hidden, gain_sum, rows_out, gate_out, up_out, down_out, result_out, up_ahead = outs
            ffn_in, turned, part, up_grad, gate, up, grad_gate, grad_up, gate_grad = scratch[:9]
            act, cot_rows, down, tile, block = scratch[9:14]
            plane_bufs, gate_bufs = scratch[14:19], scratch[19:]
            loaded = Flags()
            for c in range(2):
                for h in range(2):
                    loaded.raised((c, h), [wire.keep(rows_in.at[c, h], ffn_in.at[c, h])])
                    if (c, h) == (0, 0):
                        loaded.raised(Key.gate, [wire.keep(gate_in, gate)])
                        loaded.raised(Key.up, [wire.keep(up_in, up)])
            loaded.raised(Key.cot, [wire.keep(cot_in, cot_rows)])
            gain_sum[...] = jnp.zeros_like(gain_sum)

            made, gate_made, up_made = Flags(), Flags(), Flags()

            def down_rows():
                yield from last_spread(place, wire, down_in, down)
                loaded.raised(Key.down)

            def up_rows():
                handles = []
                for y in range(2):
                    yield up_made.wait((3, y))
                    handles.append(wire.send(up_grad.at[3, y], up_ahead.at[y], NEAR))
                yield handles

            def rows_of(ref, c, h):
                return ref[c, h].reshape(many, width)

            def weight(ref):
                return ref[...].reshape(width, cols)

            def compute():
                groups = [(c, h) for c in range(2) for h in range(2)]

                def columns(key):
                    at = (key[0] * 2 + key[1]) * side
                    return ffn_in[:, :, :, :, at : at + side].reshape(4 * many, side)

                def put(key, value):
                    gate_grad[key[0], key[1]] = value.astype(BF)

                def gate_rows():
                    return grad_gate[...].reshape(4 * many, cols)

                for c, h in groups:
                    yield loaded.wait((c, h), Key.gate, Key.up)
                    x = rows_of(ffn_in, c, h)
                    grad_gate[c, h] = mm(x, weight(gate), NN).astype(BF)
                    act[c, h] = mm(x, weight(up), NN).astype(BF)
                    wire.spend(3.2)
                yield loaded.wait(Key.cot, Key.down)
                for c, h in groups:
                    yield []
                    grad = mm(rows_of(cot_rows, c, h), weight(down), NN)
                    gate_pre = grad_gate[c, h].astype(F32)
                    up_pre = act[c, h].astype(F32)
                    sig = jax.nn.sigmoid(gate_pre)
                    act[c, h] = (gate_pre * sig * up_pre).astype(BF)
                    slope = sig * (1.0 + gate_pre * (1.0 - sig))
                    grad_gate[c, h] = (grad * up_pre * slope).astype(BF)
                    grad_up[c, h] = (grad * gate_pre * sig).astype(BF)
                    wire.spend(2.3)
                yield from weight_tiles(wire, columns, z_line[:2], gate_rows, put, gate_made)
                for c in (1, 0):
                    for h in range(2):
                        yield []
                        total = mm(grad_gate[c, h], weight(gate), NT)
                        total = total + mm(grad_up[c, h], weight(up), NT)
                        part[c, h] = total.astype(BF).reshape(half[1:])
                        wire.spend(3.0)
                        made.raised(((Key.near, Key.far)[c], h))

                yield from weight_tiles(wire, columns, z_line[2:], gate_rows, put, gate_made)

                def put_up(key, value):
                    up_grad[key[0], key[1]] = value.astype(BF)
                    wire.keep(up_grad.at[key[0], key[1]], up_out.at[key[0], key[1]])
                    up_made.raised(key)

                def up_rows_all():
                    return grad_up[...].reshape(4 * many, cols)

                yield from weight_tiles(wire, columns, z_line, up_rows_all, put_up)
                busy = {}

                def cot_columns(key):
                    at = (key[0] * 2 + key[1]) * side
                    return cot_rows[:, :, :, :, at : at + side].reshape(4 * many, side)

                def put_down(key, value):
                    slot = key[1]
                    wire.arrived(*busy.get(slot, ()))
                    tile[slot] = value.astype(BF)
                    busy[slot] = [wire.keep(tile.at[slot], down_out.at[key[0], key[1]])]

                def act_rows():
                    return act[...].reshape(4 * many, cols)

                yield from weight_tiles(wire, cot_columns, z_line, act_rows, put_down)
                for c in (1, 0):
                    for h in range(2):
                        yield []
                        wire.arrived(*busy.get(Key.block, ()))
                        total = mm(act[c, h], weight(down), NT)
                        block[...] = total.astype(BF).reshape(half[1:])
                        busy[Key.block] = [wire.keep(block, result_out.at[c, h])]
                        wire.spend(2.0)

            def finish_grad(stream, rows, load):
                part = z_parts(place, load, width)
                held = hidden[stream, rows]
                scale = inverse_rms(held)
                gain_sum[...] += jnp.sum(part * held * scale, axis=0, keepdims=True)
                total = cot[stream, rows].astype(F32) + norm_back(held, scale, gains[1:2], part)
                grad_hidden[stream, rows] = total
                turned[stream, rows] = total.astype(BF)

            def back_rows():
                yield from plane_fold(
                    place, wire, part.at[0], part.at[1], plane_bufs, finish_grad, made
                )

            def back_stream(h):
                here = pl.ds(h, 1)
                yield made.wait((Key.done, h))
                yield from rows_gather(place, wire, turned.at[here], rows_out.at[here])

            wire.run(
                down_rows(),
                back_stream(0),
                back_stream(1),
                back_rows(),
                ffn_fold(place, wire, gate_grad, gate_bufs, gate_out, gate_made),
                up_rows(),
                compute(),
            )

        vmem = pltpu.VMEM
        outs = comm_call(
            work,
            3,
            (CORE, X, Y, NEAR, FAR),
            [self.hidden_rows, self.gains, cotangent, self.ffn_in]
            + [self.gate, self.up, self.cot, self.down],
            [True] * 3 + [False] * 5,
            [
                ((streams, count, width), F32),
                ((1, width), F32),
                ((streams, 4, count, width), BF),
                (ffn[1:], BF),
                (ffn, BF),
                (ffn, BF),
                (plane, BF),
                (ffn[1:], BF),
            ],
            [True] * 2 + [False] * 6,
            [
                vmem(plane, BF),
                vmem((streams, count, width), BF),
                vmem(plane, BF),
                vmem(ffn, BF),
                vmem(ffn, BF),
                vmem(ffn, BF),
                vmem(group, BF),
                vmem(group, BF),
                vmem(ffn, BF),
                vmem(group, BF),
                vmem(plane, BF),
                vmem(ffn, BF),
                vmem((2,) + ffn[2:], BF),
                vmem(half[1:], BF),
            ]
            + plane_buffers(half)
            + ffn_buffers(ffn),
            60,
            40,
            mb=63,
            pace=KEEN,
        )
        grad_hidden, gain_grad, rows, self.gate_grad = outs[:4]
        self.up_part, self.down_part, self.result_part, self.up_ahead = outs[4:]
        rows = rows.reshape(streams, 4 * count, width)
        return grad_hidden.reshape(streams * count, width), gain_grad[0], rows

    def own_streams(self, values):
        return values

    def mixer_order(self, values):
        lead, width = values.shape[:-1], values.shape[-1]
        parts = jnp.swapaxes(values.reshape(lead + (4, 2, width // 8)), -3, -2)
        return z_relative(parts, self.at.z, len(lead) + 1).reshape(lead + (width,))

    def mixer_unorder(self, values):
        lead, width = values.shape[:-1], values.shape[-1]
        parts = z_relative(values.reshape(lead + (2, 4, width // 8)), self.at.z, len(lead) + 1)
        return jnp.swapaxes(parts, -3, -2).reshape(lead + (width,))

    def ffn_order(self, values):
        return z_relative(values, self.at.z, values.ndim - 1)

    def mixer_back(self, mixer, grad_mixed):
        reading, scores, share, branch_out = mixer.reading, mixer.scores, mixer.share, mixer.branch
        streams, length, hd = reading.shape
        rows, width = grad_mixed.shape
        slots = scores.shape[1]
        state_shape, slim = (streams, slots, 2 * hd), (streams, slots, 128)
        ffn = self.up_part.shape
        line = (4, 2, hd // 8, width)
        head = (2, 4, width // 8, hd)
        own = (head[2] // 4, width)
        raw, gate_shape = (streams, length, hd), (streams, slots, length)
        key_raw, value_raw, query_raw, gate_raw = mixer.raw

        def work(place, wire, given, outs, scratch):
            grad_mixed, output_w, survive, gains = given[:4]
            up_ahead = given[-1]
            out_gain = gains.at[0:1, :hd]
            after, gain_sum, grad_query, grad_gate, grad_k, grad_v, back, own_flow = outs[:8]
            up_out, output_out, query_out, gate_out, part_out = outs[8:]
            loads = {
                key: (source, target)
                for key, source, target in zip(
                    (Key.reading, Key.gate, Key.query, Key.key, Key.value, Key.keep, Key.written)
                    + (Key.scores, Key.share, Key.slots, Key.branch, Key.normed, Key.up)
                    + (Key.query_w, Key.gate_w),
                    given[4:],
                    scratch,
                )
            }
            here, up_made, lines_made = Flags(), Flags(), Flags()
            heads_made = [Flags(), Flags()]

            def load(*keys):
                for key in keys:
                    here.raised(key, [wire.keep(*loads[key])])

            kept = {key: pair[1] for key, pair in loads.items()}
            sent, got, grad_read, direct, output_part, query_part, gate_part = scratch[15:22]
            scan, up_bufs = scratch[22:26], scratch[26:29]
            lines, query_bufs, gate_bufs = scratch[29:33], scratch[33:37], scratch[37:41]
            normed_part = scratch[41]
            load(Key.up, Key.branch, Key.reading, Key.gate, Key.normed, Key.query, Key.key, Key.value)
            load(Key.keep, Key.written, Key.scores, Key.share, Key.slots, Key.query_w, Key.gate_w)
            gain_sum[...] = jnp.zeros_like(gain_sum)

            def returned():
                yield here.wait(Key.sent)
                yield from heads_return(place, wire, sent, got)
                here.raised(Key.got)

            def scanned():
                yield here.wait(Key.direct)
                yield from pieces_scan(place, wire, True, survive, direct, after, scan)

            def up_rows():
                yield here.wait(Key.up)
                got = up_bufs[0].at[1]
                ahead = [wire.keep(up_ahead.at[y], got.at[y]) for y in range(2)]
                yield from ffn_fold(
                    place, wire, kept[Key.up], up_bufs, up_out, None, None, ahead
                )

            def gated(s):
                def chunk(part):
                    at = pl.ds(pl.multiple_of(s * length + part.start, 16), part.size)
                    values, opened = kept[Key.reading][s, part], kept[Key.gate][s, part]
                    grad = by_tp(got[at].astype(F32), (4, 2), hd // 8)
                    scale = inverse_rms(values)
                    normed = values * scale * out_gain[...]
                    grad_gate[s, part] = (grad * normed * silu_slope(opened)).astype(BF)
                    grad = grad * silu(opened)
                    gain_sum[...] += jnp.sum(grad * values * scale, axis=0, keepdims=True)
                    grad_read[s, part] = norm_back(values, scale, out_gain[...], grad)

                row_loop(length, 32, chunk)

            def streams_back(s, carry):
                results = piece_back(
                    *[kept[key][s] for key in (Key.query, Key.key, Key.value, Key.keep, Key.written)],
                    *[kept[key][s] for key in (Key.slots, Key.scores, Key.share)],
                    grad_read[s],
                )
                targets = (grad_query, grad_k, grad_v, direct, back, own_flow)
                for target, result in zip(targets, results):
                    target[s] = result.astype(target.dtype)
                return carry

            def compute():
                half = rows // 2
                for at in (0, half):
                    part = mm(grad_mixed[at : at + half], output_w[...], NT)
                    sent[at : at + half] = part.astype(BF)
                wire.spend(3.0)
                here.raised(Key.sent)
                yield here.wait(Key.branch)
                block = hd // 4
                for m in (3, 1, 2, 0):
                    yield []
                    cols = kept[Key.branch][:, m * block : (m + 1) * block]
                    total = mm(cols, grad_mixed[...], TN)
                    output_part[m] = total.astype(BF).reshape(line[1:])
                    wire.spend(1.2)
                    lines_made.raised(m)
                yield here.wait(Key.got, Key.reading, Key.gate)
                for s in range(streams):
                    gated(s)
                wire.spend(2.0)
                yield here.wait(Key.normed)
                yield from head_tiles(
                    wire,
                    kept[Key.normed],
                    lambda: grad_gate[...].reshape(rows, hd),
                    gate_part,
                    heads_made[1],
                )
                yield here.wait(Key.query, Key.key, Key.value, Key.keep, Key.written, Key.scores, Key.share, Key.slots)
                lax.fori_loop(0, streams, streams_back, 0)
                wire.spend(13.0)
                here.raised(Key.direct)
                yield from head_tiles(
                    wire,
                    kept[Key.normed],
                    lambda: grad_query[...].reshape(rows, hd),
                    query_part,
                    heads_made[0],
                )
                yield here.wait(Key.query_w, Key.gate_w)
                for s in range(streams):
                    yield []
                    total = mm(grad_query[s], kept[Key.query_w][...], NT)
                    total = total + mm(grad_gate[s], kept[Key.gate_w][...], NT)
                    normed_part[s] = total.astype(BF)
                    wire.keep(normed_part.at[s], part_out.at[s])
                    wire.spend(2.5)

            wire.run(
                returned(),
                scanned(),
                up_rows(),
                output_fold(place, wire, output_part, lines, output_out, lines_made),
                head_fold(place, wire, gate_part, gate_bufs, gate_out, heads_made[1]),
                head_fold(place, wire, query_part, query_bufs, query_out, heads_made[0]),
                compute(),
            )

        vmem = pltpu.VMEM
        later = [
            reading,
            gate_raw,
            query_raw,
            key_raw,
            value_raw,
            mixer.keep,
            mixer.written,
            scores,
            share,
            mixer.slots_in,
            branch_out,
            mixer.normed,
            self.up_part,
            mixer.weights[2],
            mixer.weights[3],
        ]
        outs = comm_call(
            work,
            7,
            (CORE, X, X | CORE, Y, NEAR, FAR),
            [grad_mixed, mixer.output, self.survive, self.gains] + later + [self.up_ahead],
            [True] * 4 + [False] * (1 + len(later)),
            [
                (state_shape, F32),
                ((1, hd), F32),
                (raw, BF),
                (raw, BF),
                (raw, BF),
                (raw, BF),
                (gate_shape, F32),
                (gate_shape, F32),
                (ffn[1:], BF),
                (line[2:], BF),
                (own, BF),
                (own, BF),
                ((streams, length, width), BF),
            ],
            [True] * 8 + [False] * 5,
            [vmem(a.shape, a.dtype) for a in later]
            + [
                vmem((rows, hd), BF),
                vmem((rows, hd), BF),
                vmem(raw, F32),
                vmem(state_shape, F32),
                vmem(line, BF),
                vmem(head, BF),
                vmem(head, BF),
            ]
            + scan_buffers(state_shape, slim)
            + ffn_buffers(ffn)
            + line_buffers(line[2], line[3])
            + line_buffers(head[2], head[3])
            + line_buffers(head[2], head[3])
            + [vmem((streams, length, width), BF)],
            60,
            30,
            mb=63,
            pace=EARLY,
        )
        self.up_grad, output_sum, query_sum, gate_sum, self.normed_part = outs[8:]
        self.output_sum = output_sum
        self.head_sums = [query_sum, gate_sum]
        return outs[:8]

    def finish(self, mixer, back, tokens, grad_hidden, ffn_gain_grad, small):
        after, out_gain_grad, unused, unused, grad_k, grad_v, pulled, flow = back
        streams, count, width = tokens.shape
        slots, length = flow.shape[1:]
        rank, hd = small[0].shape[1], grad_k.shape[-1]
        rows = streams * length
        part_shape = (streams, 2, 2, count, width)
        head = (2, 4, width // 8, hd)
        own = (head[2] // 4, width)
        plane, ffn = self.cot.shape, self.down.shape
        half = plane[1:]
        raw = (streams, length, hd)
        sheet = (24, width + H * slots)
        halves = [width // 2, width // 4, width // 8, width // 16, width // 16]
        key_raw, value_raw = mixer.raw[:2]

        def work(place, wire, given, outs, scratch):
            after, slots_end, keep, written, pulled, flow, logits = given[:7]
            low, ranks, gains, tokens, hidden, ffn_sum, out_sum = given[7:14]
            result_in, down_in, hidden_grad = given[14:17]
            far_in = result_in.at[1]
            grad_tokens, result, total_out, key_out, value_out, down_out = outs
            names = (Key.key, Key.value, Key.grad_k, Key.grad_v, Key.normed, Key.part, Key.key_w, Key.value_w)
            names = names + (Key.pack,)
            loads = dict(zip(names, zip(given[17:], scratch)))
            loads[Key.near] = (result_in.at[0], scratch[9])
            loads[Key.down] = (down_in.at[0], scratch[10].at[0])
            kept = {key: pair[1] for key, pair in loads.items()}
            kept[Key.down] = scratch[10]
            grads, parts, grad_f = scratch[11:13], scratch[13:15], scratch[15]
            normed_part, sums, tidy = scratch[16], scratch[17:20], scratch[20]
            lines = [scratch[21:25], scratch[25:29]]
            plane_bufs, fold_bufs = scratch[29:34], scratch[34:37]
            sheets, got_sheets, far_row = scratch[37], scratch[38:43], scratch[43]
            here, made = Flags(), Flags()
            heads_made = [Flags(), Flags()]
            for key in (Key.key, Key.value, Key.grad_k, Key.grad_v, Key.normed, Key.part):
                here.raised(key, [wire.keep(*loads[key])])
            for key in (Key.pack, Key.key_w, Key.value_w, Key.near, Key.down):
                here.raised(key, [wire.keep(*loads[key])])
            here.raised(Key.hidden_grad, [wire.keep(hidden_grad, grad_tokens)])
            here.raised(Key.down_2, [wire.keep(down_in.at[2], scratch[10].at[1])])
            made.raised((Key.far, 0))
            made.raised((Key.far, 1))

            def down_rows():
                yield here.wait(Key.down, Key.down_2)
                yield from ffn_fold(
                    place, wire, down_in, fold_bufs, down_out, None, kept[Key.down]
                )

            def result_rows():
                yield here.wait(Key.near)
                made.raised((Key.near, 0))
                made.raised((Key.near, 1))
                yield from plane_fold(
                    place, wire, kept[Key.near], far_in, plane_bufs, finish_result, made
                )

            def finish_result(stream, rows, load):
                total = hidden[stream, rows] + z_parts(place, load, width)
                result[stream, rows] = total.astype(BF)

            def finish_tokens(stream, rows, total):
                side = width // 8
                for y in range(2):
                    for m in range(4):
                        to = pl.multiple_of((place.z_turn(m) * 2 + y) * side, 128)
                        at = (y * 4 + m) * side
                        tidy[:, pl.ds(to, side)] = total[:, at : at + side]
                x = tokens[stream, rows].astype(F32)
                grad = norm_back(x, inverse_rms(x), gains[3:4], tidy[...])
                grad_tokens[stream, rows] += grad

            def token_rows():
                yield here.wait(Key.normed_part, Key.hidden_grad)
                yield from rows_fold(place, wire, normed_part, *sums, finish_tokens)

            def all_sums():
                yield here.wait(Key.sheet)
                total, rest, half = sheets.at[0, :, :width], sheets.at[0, :, width:], width // 2
                steps = ((FAR, place.far), (NEAR, place.near), (Y, place.y), (X, place.x))
                for step, (mask, bit) in enumerate(steps):
                    theirs = pl.ds(pl.multiple_of((1 - bit) * half, 128), half)
                    mine = pl.ds(pl.multiple_of(bit * half, 128), half)
                    got = got_sheets[step]
                    yield [
                        wire.send(total.at[:, theirs], got.at[:, :half], mask),
                        wire.send(rest, got.at[:, half:], mask),
                    ]
                    got[:, :half] += total[:, mine]
                    got[:, half:] += rest[...]
                    total, rest, half = got.at[:, :half], got.at[:, half:], half // 2
                got = got_sheets[4]
                yield [wire.send(got_sheets[3], got, CORE)]
                total_out[...] = got[...] + got_sheets[3][...]

            def ending(s, carry):
                results = piece_after(
                    *[kept[key][s] for key in (Key.key, Key.value)],
                    *[ref[s] for ref in (keep, written)],
                    *[kept[key][s] for key in (Key.grad_k, Key.grad_v)],
                    *[ref[s] for ref in (pulled, flow, after, slots_end)],
                )
                for target, value in zip((grads[0], grads[1], grad_f), results):
                    target[s] = value.astype(target.dtype)
                grad_f[s] = grad_f[s] * jax.nn.sigmoid(-logits[s]) / GATE_SCALE
                return carry

            def unorder(target_row, count, values):
                side = width // 8
                for y in range(2):
                    for m in range(4):
                        to = pl.multiple_of((place.z_turn(m) * 2 + y) * side, 128)
                        at = (y * 4 + m) * side
                        there = (0, slice(target_row, target_row + count), pl.ds(to, side))
                        sheets[there] = values[:, at : at + side]

            def weight_grad(index):
                return head_tiles(
                    wire,
                    kept[Key.normed],
                    lambda: grads[index][...].reshape(rows, hd),
                    parts[index],
                    heads_made[index],
                )

            def compute():
                yield here.wait(Key.key, Key.value, Key.grad_k, Key.grad_v)
                lax.fori_loop(0, streams, ending, 0)
                wire.spend(6.0)
                yield here.wait(Key.normed)
                yield from weight_grad(0)
                yield here.wait(Key.part, Key.pack, Key.key_w, Key.value_w)
                sheets[0] = jnp.zeros(sheet, F32)
                far_row[...] = jnp.zeros_like(far_row)
                low_sum, rank_sum, bias_sum = 0.0, 0.0, 0.0
                for s in range(streams):
                    normed = kept[Key.normed][s * length : (s + 1) * length]
                    f = grad_f[s]
                    low_grad = mm_fine(f, ranks[...], TN)
                    total = kept[Key.part][s].astype(F32)
                    total = total + mm(grads[0][s], kept[Key.key_w][...], NT)
                    total = total + mm(grads[1][s], kept[Key.value_w][...], NT)
                    total = total + mm(low_grad, kept[Key.pack][...], NT)
                    normed_part[s] = total.astype(BF).reshape(part_shape[1:])
                    far_row[...] += jnp.sum(total * normed.astype(F32), axis=0, keepdims=True)
                    wire.spend(4.0)
                    yield []
                    low_sum = low_sum + mm_fine(low_grad, normed, TN)
                    rank_sum = rank_sum + mm_fine(f, low[s], NN)
                    bias_sum = bias_sum + jnp.sum(f, axis=1, keepdims=True)
                    wire.spend(2.0)
                here.raised(Key.normed_part)
                wide = (slots, H * slots)
                spot = column(wide) - place.tp * slots
                spread = jnp.where(row(wide) == spot, 1.0, 0.0)
                unorder(0, rank, low_sum[:rank])
                unorder(16, 1, far_row[...] / gains[2:3])
                sheets[0, 0:rank, width:] = mm_fine(rank_sum, spread, TN)[:rank]
                bias_sum = jnp.broadcast_to(bias_sum, (slots, 128))
                sheets[0, 16:17, width:] = mm_fine(bias_sum, spread, TN)[:1]
                sheets[0, 17:18, :width] = ffn_sum[...]
                per = H * slots
                for at in range(hd // per):
                    sheets[0, 17 + at : 18 + at, width:] = out_sum[:, at * per : (at + 1) * per]
                here.raised(Key.sheet)
                yield from weight_grad(1)

            wire.run(
                token_rows(),
                all_sums(),
                head_fold(place, wire, parts[0], lines[0], key_out, heads_made[0]),
                head_fold(place, wire, parts[1], lines[1], value_out, heads_made[1]),
                down_rows(),
                result_rows(),
                compute(),
            )

        vmem = pltpu.VMEM
        soon = [after, mixer.slots_end, mixer.keep, mixer.written, pulled, flow]
        soon = soon + [mixer.logits, self.low_rank, self.ranks, self.gains, tokens]
        soon = soon + [self.hidden_rows]
        soon = soon + [ffn_gain_grad[None], out_gain_grad]
        later = [key_raw, value_raw, grad_k, grad_v, mixer.normed, self.normed_part]
        later = later + [mixer.weights[0], mixer.weights[1], self.pack]
        aside = [self.result_part, self.down_part, grad_hidden.reshape(tokens.shape)]
        grad_tokens, result, total, key_sum, value_sum, down_grad = comm_call(
            work,
            8,
            (CORE, X, X | CORE, Y, NEAR, FAR),
            soon + aside + later,
            [True] * len(soon) + [False] * (len(aside) + len(later)),
            [
                (tokens.shape, F32),
                (tokens.shape, BF),
                ((24, width // 16 + H * slots), F32),
                (own, BF),
                (own, BF),
                (ffn[1:], BF),
            ],
            [True] * 3 + [False] * 3,
            [vmem(a.shape, a.dtype) for a in later]
            + [vmem(half, BF), vmem((2,) + ffn[1:], BF)]
            + [vmem(raw, BF)] * 2
            + [vmem(head, BF)] * 2
            + [vmem((streams, slots, length), F32), vmem(part_shape, BF)]
            + rows_buffers(part_shape)
            + [vmem((16, width), F32)]
            + line_buffers(head[2], head[3])
            + line_buffers(head[2], head[3])
            + plane_buffers(half)
            + ffn_buffers(ffn)
            + [vmem((1,) + sheet, F32)]
            + [vmem((24, size + H * slots), F32) for size in halves]
            + [vmem((1, width), F32)],
            80,
            20,
            mb=63.5,
        )
        heads = [h.astype(F32) for h in [key_sum, value_sum] + self.head_sums + [self.output_sum]]

        def both(parts):
            return jnp.concatenate([parts[0], parts[1]], axis=1).astype(F32)

        ffn_grads = [both(g) for g in (self.gate_grad, self.up_grad, down_grad)]
        tp = lax.axis_index(TP)
        flat = lax.axis_index(SEQ) * 4 + tp
        w_low, w_rank, bias, attn_gain, out_gain, ffn_gain = small
        tall, wide = w_low.shape[0], width // 16
        in_low = lax.dynamic_slice_in_dim(total[:, :wide], tp % 2 * tall, tall, 1)
        in_rank = lax.dynamic_slice_in_dim(
            total[:, wide:], flat * w_rank.shape[0], w_rank.shape[0], 1
        )
        out_sums = total[17 : 17 + hd // (H * slots), wide:].reshape(-1)
        small_grads = (
            jnp.swapaxes(in_low[:rank], 0, 1),
            jnp.swapaxes(in_rank[:rank], 0, 1),
            in_rank[16],
            in_low[16],
            lax.dynamic_slice_in_dim(out_sums, flat * out_gain.shape[0], out_gain.shape[0], 0),
            in_low[17],
        )
        return heads, ffn_grads, grad_tokens, result, small_grads


def on_device(
    tokens,
    seq_cuts,
    w_query,
    w_key,
    w_value,
    w_gate_out,
    w_output,
    w_low,
    w_rank,
    gate_bias,
    attn_gain,
    out_gain,
    ffn_gain,
    w_gate,
    w_up,
    w_down,
    cotangent,
):
    sizes = lax.axis_size(SEQ), lax.axis_size(TP)
    move = BitMoves() if sizes == (8, 4) else PlainMoves()
    small = (w_low, w_rank, gate_bias, attn_gain, out_gain, ffn_gain)
    mixer = move.start(
        tokens,
        seq_cuts,
        (w_key, w_value, w_query, w_gate_out),
        w_output,
        small,
        (w_down, w_gate, w_up),
        cotangent,
    )
    grad_hidden, grad_ffn_gain, grad_mixed = move.feed_forward(
        tokens, mixer.ffn_gain, cotangent
    )
    back = move.mixer_back(mixer, grad_mixed.reshape(-1, tokens.shape[-1]))
    heads, ffn_grads, grad_tokens, result, small_grads = move.finish(
        mixer, back, tokens, grad_hidden, grad_ffn_gain, small
    )
    grad_w_key, grad_w_value, grad_w_query, grad_w_gate_out, grad_w_output = heads
    return (
        (result.reshape(tokens.shape), grad_tokens)
        + (grad_w_query, grad_w_key, grad_w_value, grad_w_gate_out, grad_w_output)
        + tuple(small_grads)
        + tuple(ffn_grads)
    )


def solution(mesh):
    both, row_split, line = (SEQ, TP), P((SEQ, TP), None), P((SEQ, TP))
    tokens_at, ffn_at = P(None, both, None), P(SEQ, TP)
    params = (row_split,) * 7 + (line,) * 4 + (ffn_at,) * 3
    return jax.shard_map(
        on_device,
        mesh=mesh,
        in_specs=(tokens_at, P()) + params + (tokens_at,),
        out_specs=(tokens_at, tokens_at) + params,
        check_vma=False,
    )
```
